32 devices in a mesh: boxes: 2 (over y), gx: 4 (over z), gy: 2 (over x), gz: 2 (over core).
Axes of the slice: x: 2, y: 2, z: 4, core: 2. Of those that a mesh axis runs over, the one named last changes fastest.
Arguments:
- density: float32 [64, 8, 256], P(('boxes', 'gx'), 'gy', 'gz'), parts along dimension 0, may hold values from 0.2 to 7, as said below
- external: float32 [64, 8, 256], P(('boxes', 'gx'), 'gy', 'gz'), parts along dimension 0, may hold values from -4 to 4
- w_first: bfloat16 [27, 32], replicated, may hold values from -1.25 to 1.25
- w_second: bfloat16 [27, 32, 32], replicated, may hold values from -0.21875 to 0.21875
- w_third: bfloat16 [27, 32, 32], replicated, may hold values from -0.21875 to 0.21875
- w_last: bfloat16 [27, 32], replicated, may hold values from -0.21875 to 0.21875
Outputs:
- new_density: float32 [64, 8, 256], P(('boxes', 'gx'), 'gy', 'gz'), parts along dimension 0
- potential: float32 [64, 8, 256], P(('boxes', 'gx'), 'gy', 'gz'), parts along dimension 0
- chem_potential: float32 [4], P('boxes'), parts along dimension 0
- stress: float32 [4, 3, 3], P('boxes'), parts along dimension 0
The draws below stay inside these ranges and needn't reach their ends.
There are 2 independent parts, one for each index of `boxes`. The reference program is written for one: setup_inputs(seed, part) draws one part's arguments, and reference() takes and returns one part's arrays. A program takes and returns all parts, laid end to end along the dimension named above; an argument that names none is the same for every part. Nothing has to cross between parts.
Inputs may be any that keep to these rules, and one draw needn't show every extreme that they name: Electron density of each cell, positive.
All inputs are finite; a program needn't handle non-finite values.
Results may differ from the reference program's by a relative error of at most 0.0024.
Values may be sent and summed in bfloat16 or wider, within the bound.
No kernel may reach another device: no remote copies, remote signals or barrier semaphores. Data moves between devices by JAX's collectives and lax.ppermute only.
A program may use at most 64 MiB of HBM per device.

```python
import jax
import jax.numpy as jnp
from jax import lax

CH = 32
STEPS = 2
NX = 32
NY = 8
NZ = 256
NCELL = 65536


def draw_density(key, part):
    key = jax.random.fold_in(key, 3)
    first = jax.random.fold_in(key, 0)
    place_x = (jnp.arange(NX, dtype=jnp.float32)[:, None, None] + 0.5) / NX
    rough = jax.random.uniform(first, (NX, NY, NZ), jnp.float32, 0.6, 1.8)
    base = (2.0 + jnp.cos(6.2831853 * place_x)) * jnp.ones((1, NY, 1), jnp.float32)
    return base * rough


def draw_external(key, part):
    key = jax.random.fold_in(key, 11)
    first, second, third = jax.random.split(key, 3)
    half_y = jnp.where(jnp.arange(NY)[None, :, None] < NY // 2, 1.0, -1.0).astype(jnp.float32)
    half_z = jnp.where(jnp.arange(NZ)[None, None, :] < NZ // 2, 1.0, -1.0).astype(jnp.float32)
    sign = jnp.where(jax.random.uniform(second, ()) < 0.5, 1.0, -1.0).astype(jnp.float32)
    level = jax.random.uniform(third, (), jnp.float32, 1.6, 2.2)
    offset = sign * level * half_y * half_z
    rough = jnp.clip(0.8 * jax.random.normal(first, (NX, NY, NZ), jnp.float32), -1.8, 1.8)
    return rough + offset


def centred(key, extent, deviation, limit, held_as=jnp.bfloat16):
    values = jax.random.normal(key, extent, jnp.float32) * deviation
    return jnp.minimum(jnp.maximum(values, -limit), limit).astype(held_as)


def setup_inputs(seed: int = 0, part: int = 0) -> dict:
    arg_keys = jax.random.split(jax.random.key(seed), 7)
    own_keys = jax.random.split(jax.random.fold_in(arg_keys[6], part), 7)
    density = draw_density(jax.random.fold_in(jax.random.fold_in(arg_keys[6], part), 71), part)
    external = draw_external(jax.random.fold_in(jax.random.fold_in(arg_keys[6], part), 71), part)
    w_first = centred(arg_keys[2], (27, CH), 27 ** -0.5, 1.25)
    w_second = centred(arg_keys[3], (27, CH, CH), (27 * CH) ** -0.5, 0.21875)
    w_third = centred(arg_keys[4], (27, CH, CH), (27 * CH) ** -0.5, 0.21875)
    w_last = centred(arg_keys[5], (27, CH), (27 * CH) ** -0.5, 0.21875)
    return dict(density=density, external=external, w_first=w_first, w_second=w_second, w_third=w_third, w_last=w_last)


C_TF = 2.871234
C_X = 0.7385588
TAU = 0.1
OFFSETS = [(along_x - 1, along_y - 1, along_z - 1) for along_x in range(3) for along_y in range(3) for along_z in range(3)]


def moved(field, offset, direction):
    return jnp.roll(field, (-direction * offset[0], -direction * offset[1], -direction * offset[2]), axis=(-3, -2, -1))


def silu_slope(argument):
    logistic = jax.nn.sigmoid(argument)
    return logistic * (1.0 + argument * (1.0 - logistic))


def dense_conv(activity, weights, direction):
    channels = activity.shape[0]
    grid_shape = activity.shape[1:]
    summed = None
    for ordinal, offset in enumerate(OFFSETS):
        shifted = moved(activity, offset, direction).reshape(channels, -1)
        matrix = weights[ordinal] if direction > 0 else weights[ordinal].T
        product = jnp.dot(matrix, shifted, preferred_element_type=jnp.float32)
        summed = product if summed is None else summed + product
    return summed.reshape((summed.shape[0],) + grid_shape)


def single_conv(field, weights, direction):
    stacked = jnp.stack([moved(field, offset, direction).reshape(-1) for offset in OFFSETS])
    result = jnp.dot(weights.astype(jnp.float32).T, stacked, precision=lax.Precision.HIGHEST, preferred_element_type=jnp.float32)
    return result.reshape((weights.shape[1],) + field.shape)


def narrow_planes(activity, weights):
    channels = activity.shape[0]
    planes = jnp.dot(weights, activity.reshape(channels, -1), preferred_element_type=jnp.float32)
    return planes.reshape((27,) + activity.shape[1:])


def fold_planes(planes, factors, direction):
    summed = jnp.zeros(planes.shape[1:], jnp.float32)
    for ordinal, offset in enumerate(OFFSETS):
        if factors[ordinal] != 0.0:
            summed = summed + factors[ordinal] * moved(planes[ordinal], offset, direction)
    return summed


def evaluate(current, external, w_first, w_second, w_third, w_last):
    cube = jnp.cbrt(current)
    pre_one = single_conv(cube, w_first, 1)
    act_one = jax.nn.silu(pre_one).astype(jnp.bfloat16)
    pre_two = dense_conv(act_one, w_second, 1)
    act_two = jax.nn.silu(pre_two).astype(jnp.bfloat16)
    pre_three = dense_conv(act_two, w_third, 1)
    act_three = jax.nn.silu(pre_three).astype(jnp.bfloat16)
    enhance = fold_planes(narrow_planes(act_three, w_last), [1.0] * 27, 1)
    source = current * cube * cube
    back_three = single_conv(source, w_last, -1)
    delta_three = (back_three * silu_slope(pre_three)).astype(jnp.bfloat16)
    back_two = dense_conv(delta_three, w_third, -1)
    delta_two = (back_two * silu_slope(pre_two)).astype(jnp.bfloat16)
    back_one = dense_conv(delta_two, w_second, -1)
    delta_one = (back_one * silu_slope(pre_one)).astype(jnp.bfloat16)
    planes_one = narrow_planes(delta_one, w_first)
    cotangent = fold_planes(planes_one, [1.0] * 27, -1)
    levers = [fold_planes(planes_one, [float(offset[axis_no]) for offset in OFFSETS], -1) for axis_no in range(3)]
    potential = (5.0 / 3.0) * cube * cube * (C_TF + enhance) + cotangent / (3.0 * cube * cube) + external - (4.0 / 3.0) * C_X * cube
    energy = jnp.sum(source * (C_TF + enhance) + external * current - C_X * current * cube)
    virial = jnp.sum(current * potential)
    units = [(1, 0, 0), (0, 1, 0), (0, 0, 1)]
    slopes = [(moved(cube, unit, 1) - moved(cube, unit, -1)) * 0.5 for unit in units]
    moments = jnp.stack([jnp.stack([jnp.sum(slopes[row_no] * levers[col_no]) for col_no in range(3)]) for row_no in range(3)])
    weighted = current * jnp.exp(-TAU * potential)
    return potential, weighted, energy, virial, moments


def reference(density, external, w_first, w_second, w_third, w_last):
    total_mass = jnp.sum(density)
    current = density
    chem_list = []
    stress_list = []
    potential = density
    for repeat_count in range(STEPS):
        potential, weighted, energy, virial, moments = evaluate(current, external, w_first, w_second, w_third, w_last)
        norm = jnp.sum(weighted)
        chem_list.append(jnp.log(total_mass / norm) / TAU)
        stress_list.append((moments + jnp.eye(3, dtype=jnp.float32) * (energy - virial)) / NCELL)
        current = weighted * (total_mass / norm)
    return current, potential, jnp.stack(chem_list), jnp.stack(stress_list)
```

```python
import functools

import jax
import jax.numpy as jnp
from jax import lax
from jax.experimental import pallas as pl
from jax.experimental.pallas import tpu as pltpu
from jax.sharding import PartitionSpec as P

STEPS = 2
C_TF = 2.871234
C_X = 0.7385588
TAU = 0.1
REACH = 6
STRIPS = 16
GROUP = 4
SUMS = 16
LIMIT = 60 << 20
BF = jnp.bfloat16
F32 = jnp.float32
VM = pl.BlockSpec(memory_space=pltpu.VMEM)
SM = pl.BlockSpec(memory_space=pltpu.SMEM)


def up(number, unit):
    return -(-number // unit) * unit


def iota(shape, dim):
    return lax.broadcasted_iota(jnp.int32, shape, dim)


def dot(a, b):
    return jnp.dot(a, b, preferred_element_type=F32)


def dot_tn(a, b):
    return lax.dot_general(a, b, (((0,), (0,)), ((), ())), preferred_element_type=F32)


def dot_nt(a, b):
    return lax.dot_general(a, b, (((1,), (1,)), ((), ())), preferred_element_type=F32)


class Plan:
    def __init__(self, xo, yw, own_y, ny, zo, ch):
        self.xo, self.yw, self.own_y, self.ny, self.zo, self.ch = xo, yw, own_y, ny, zo, ch
        self.xe = xo + 2 * REACH
        self.ze = up(zo + 2 * REACH, STRIPS)
        self.zh = (self.ze - zo) // 2
        self.lo = self.ze // STRIPS
        self.zp = up(self.ze, 128)
        self.zq = up(zo, 128)
        self.lanes = yw * ch
        self.fields = 4 * yw
        self.narrow = up(GROUP * self.fields, 128)


def tap_no(tx, ty, tz, direction):
    number = 9 * tx + 3 * ty + tz
    return number if direction > 0 else 26 - number


def weights_kernel(p, dense_in, single_in, dense_out, first_out, last_out):
    ch, yw, lanes = p.ch, p.yw, p.lanes

    for ref_in, ref_out, direction in zip(dense_in, dense_out, (1, 1, -1, -1)):
        taps = []
        for ty in range(3):
            taps.append(
                jnp.concatenate(
                    [ref_in[tap_no(t // 3, ty, t % 3, direction)] for t in range(9)], axis=0
                )
            )
        for yi in range(yw):
            spread = None
            for ty in range(3):
                yo = (yi - ty + 1) % yw
                place = (iota((ch, lanes), 1) == iota((ch, lanes), 0) + yo * ch).astype(F32)
                part = dot(taps[ty], place.astype(BF))
                spread = part if spread is None else spread + part
            ref_out[:, yi * ch : (yi + 1) * ch, :] = spread.astype(BF).reshape(9, ch, lanes)

    tile = (
        jnp.bitwise_and(iota((ch, lanes), 1), ch - 1) == iota((ch, lanes), 0)
    ).astype(F32).astype(BF)
    tiled = [dot(ref[...], tile).astype(BF) for ref in single_in]

    rows = 18 * yw
    row = iota((rows, 1), 0)
    yi = lax.rem(row, yw)
    tx = lax.rem(lax.div(row, yw), 3)
    tz = lax.rem(lax.div(row, 3 * yw), 3)
    yo = lax.div(iota((rows, lanes), 1), ch)
    for wide, ref_out, direction in zip(tiled, first_out, (1, -1)):
        total = jnp.zeros((rows, lanes), F32)
        for ty in range(3):
            number = 9 * tx + 3 * ty + tz
            number = number if direction > 0 else 26 - number
            pick = (iota((rows, 27), 1) == number).astype(F32).astype(BF)
            here = lax.rem(yo + (ty - 1 + yw), yw) == yi
            total = total + jnp.where(here, dot(pick, wide), 0.0)
        ref_out[...] = total.astype(BF)

    rows = p.narrow
    row = iota((rows, 1), 0)
    yo = lax.rem(row, yw)
    field = lax.rem(lax.div(row, yw), 4)
    tx = lax.div(row, 4 * yw)
    yi = lax.div(iota((rows, lanes), 1), ch)
    for wide, ref_out, direction in zip(tiled[::-1], last_out, (1, -1)):
        for tz in range(3):
            total = jnp.zeros((rows, lanes), F32)
            for ty in range(3):
                number = 9 * tx + 3 * ty + tz
                number = number if direction > 0 else 26 - number
                if direction > 0:
                    factor = jnp.where(field == 0, 1, 0)
                else:
                    factor = jnp.where(
                        field == 0,
                        1,
                        jnp.where(field == 1, 1 - tx, jnp.where(field == 2, 1 - ty, 1 - tz)),
                    )
                factor = jnp.where(tx < 3, factor, 0).astype(F32)
                pick = (iota((rows, 27), 1) == number).astype(F32).astype(BF)
                here = lax.rem(yo + (ty - 1 + yw), yw) == yi
                total = total + jnp.where(here, dot(pick, wide), 0.0) * factor
            ref_out[tz] = total.astype(BF)


def spread_weights(p, w_first, w_second, w_third, w_last):
    def body(a, b, c, d, first, last, oa, ob, oc, od, o_first, o_back, o_last, o_cot):
        weights_kernel(
            p, (a, b, c, d), (first, last), (oa, ob, oc, od), (o_first, o_back), (o_last, o_cot)
        )

    dense = jax.ShapeDtypeStruct((9, p.lanes, p.lanes), BF)
    single = jax.ShapeDtypeStruct((18 * p.yw, p.lanes), BF)
    narrow = jax.ShapeDtypeStruct((3, p.narrow, p.lanes), BF)
    flops = 2 * 4 * 9 * 3 * p.lanes * p.lanes * p.lanes
    return pl.pallas_call(
        body,
        name="spread_weights",
        out_shape=(dense,) * 4 + (single,) * 2 + (narrow,) * 2,
        in_specs=[VM] * 6,
        out_specs=(VM,) * 8,
        compiler_params=pltpu.CompilerParams(vmem_limit_bytes=LIMIT),
        cost_estimate=pl.CostEstimate(flops=flops, bytes_accessed=6 << 20, transcendentals=0),
    )(
        jnp.swapaxes(w_second, 1, 2),
        jnp.swapaxes(w_third, 1, 2),
        w_third,
        w_second,
        w_first,
        w_last,
    )


def cube_root(value):
    guess = jnp.exp(jnp.log(value) * (1.0 / 3.0))
    return guess - (guess - value / (guess * guess)) * (1.0 / 3.0)


def store_edges(p, ref, place, value):
    tiles = value.reshape(p.lo, STRIPS, p.lanes)
    ref[place, 1 : p.lo + 1] = tiles.astype(BF)
    ref[place, 0] = pltpu.roll(tiles[p.lo - 1], 1, 0).astype(BF)
    ref[place, p.lo + 1] = pltpu.roll(tiles[0], STRIPS - 1, 0).astype(BF)


def blocks(total, size):
    return [(start, min(size, total - start)) for start in range(0, total, size)]


def dense_planes(p, ref, w_ref, start, count):
    total = None
    for t in range(9):
        tx, tz = divmod(t, 3)
        rows = ref[start + tx : start + tx + count, tz : tz + p.lo]
        part = dot(rows.reshape(count * p.ze, p.lanes), w_ref[t])
        total = part if total is None else total + part
    return total


def gate(value):
    logistic = 0.5 * jnp.tanh(0.5 * value) + 0.5
    act = value * logistic
    return logistic, act


def slope_of(value, logistic, act):
    return logistic * (1.0 + value - act)


def to_planes(p, field, spread, planes_ref):
    high = field.astype(BF)
    low = (field - high.astype(F32)).astype(BF)
    flat = jnp.concatenate(
        [high.reshape(p.xe * p.yw, p.zp), low.reshape(p.xe * p.yw, p.zp)], axis=0
    )
    planes_ref[...] = dot(flat, spread).reshape(2, p.xe, p.yw, 3 * p.zp)


def single_plane(p, planes_ref, place, w_ref):
    pieces = []
    for half in range(2):
        for tz in range(3):
            piece = planes_ref[half, place : place + 3, :, tz * p.zp : (tz + 1) * p.zp]
            pieces.append(piece.reshape(3 * p.yw, p.zp))
    window = jnp.concatenate(pieces, axis=0).astype(BF)
    return dot_tn(window, w_ref[...])[: p.ze]


def narrow_fold(p, ref, w_ref, planes_ref, back):
    for start, count in blocks(p.xo + 2, 5):
        total = None
        for tz in range(3):
            rows = ref[start : start + count, tz : tz + p.lo].reshape(count * p.ze, p.lanes)
            part = dot_nt(rows, w_ref[tz])
            total = part if total is None else total + part
        planes_ref[start : start + count] = total.reshape(count, p.ze, p.narrow)
    lane = lax.div(iota((p.ze, p.narrow), 1), p.fields)
    fields = []
    for first in range(0, p.xo, GROUP):
        joined = jnp.zeros((p.ze, p.narrow), F32)
        for k in range(GROUP):
            total = None
            for tx in range(3):
                part = planes_ref[first + k + tx]
                shift = (k - tx) * p.fields % p.narrow
                part = pltpu.roll(part, shift, 1) if shift else part
                total = part if total is None else total + part
            joined = jnp.where(lane == k, total, joined)
        high = joined.astype(BF)
        rest = joined - high.astype(F32)
        mid = rest.astype(BF)
        low = (rest - mid.astype(F32)).astype(BF)
        parts = jnp.concatenate([high, mid, low], axis=0)
        natural = dot_tn(parts, back)[: GROUP * p.fields]
        fields.append(natural.reshape(GROUP, 4, p.yw, p.zq))
    return jnp.concatenate(fields, axis=0)


def update_kernel(p, current, external, weights, scratch):
    w_two, w_three, w_three_back, w_two_back, w_one, w_source, w_enhance, w_lever = weights
    planes, act_a, act_b, act_c, slope_one, slope_two, slope_three, narrow = scratch

    current = jnp.where(iota(current.shape, 2) < p.ze, current, 1.0)
    cube = cube_root(current)
    source = current * cube * cube

    shape = (p.zp, 3 * p.zp)
    lane = iota(shape, 1)
    tz = lax.div(lane, p.zp)
    row = lane - tz * p.zp
    cell = p.lo * jnp.bitwise_and(row, STRIPS - 1) + lax.div(row, STRIPS) + tz - 1
    spread = jnp.where((cell == iota(shape, 0)) & (row < p.ze), 1.0, 0.0).astype(BF)
    shape = (3 * p.ze, p.zq)
    row = lax.rem(iota(shape, 0), p.ze)
    cell = p.lo * jnp.bitwise_and(row, STRIPS - 1) + lax.div(row, STRIPS) - p.zh
    back = jnp.where((cell == iota(shape, 1)) & (cell < p.zo), 1.0, 0.0).astype(BF)

    to_planes(p, cube, spread, planes)
    for x in range(p.xo + 10):
        value = single_plane(p, planes, x, w_one)
        logistic, act = gate(value)
        store_edges(p, act_a, x, act)
        if 4 <= x < p.xo + 6:
            slope_one[x - 4] = slope_of(value, logistic, act)

    for start, count in blocks(p.xo + 8, 4):
        values = dense_planes(p, act_a, w_two, start, count)
        for k in range(count):
            x = start + k
            value = values[k * p.ze : (k + 1) * p.ze]
            logistic, act = gate(value)
            store_edges(p, act_b, x, act)
            if 2 <= x < p.xo + 6:
                slope_two[x - 2] = slope_of(value, logistic, act)

    to_planes(p, source, spread, planes)
    for start, count in blocks(p.xo + 6, 7):
        values = dense_planes(p, act_b, w_three, start, count)
        for k in range(count):
            x = start + k
            value = values[k * p.ze : (k + 1) * p.ze]
            logistic, act = gate(value)
            if 2 <= x < p.xo + 4:
                store_edges(p, act_c, x - 2, act)
            slope = slope_of(value, logistic, act)
            store_edges(p, act_a, x, single_plane(p, planes, x + 2, w_source) * slope)

    enhance = narrow_fold(p, act_c, w_enhance, narrow, back)[:, 0]

    for start, count in blocks(p.xo + 4, 4):
        values = dense_planes(p, act_a, w_three_back, start, count)
        for k in range(count):
            x = start + k
            store_edges(p, act_b, x, values[k * p.ze : (k + 1) * p.ze] * slope_two[x])

    for start, count in blocks(p.xo + 2, 5):
        values = dense_planes(p, act_b, w_two_back, start, count)
        for k in range(count):
            x = start + k
            store_edges(p, act_c, x, values[k * p.ze : (k + 1) * p.ze] * slope_one[x])

    levers = narrow_fold(p, act_c, w_lever, narrow, back)

    def natural(field, step):
        return pltpu.roll(field, (p.zp - p.zh - step) % p.zp, 2)[:, :, : p.zq]

    inner = cube[REACH : REACH + p.xo]
    here = natural(inner, 0)
    density = natural(current[REACH : REACH + p.xo], 0)
    source_here = natural(source[REACH : REACH + p.xo], 0)
    squared = here * here
    potential = (
        5.0 / 3.0 * squared * (C_TF + enhance)
        + levers[:, 0] / (3.0 * squared)
        + external
        - 4.0 / 3.0 * C_X * here
    )
    slopes = [
        natural(cube[REACH + 1 : REACH + 1 + p.xo], 0) - natural(cube[REACH - 1 : REACH - 1 + p.xo], 0),
        pltpu.roll(here, p.yw - 1, 1) - pltpu.roll(here, 1, 1),
        natural(inner, 1) - natural(inner, -1),
    ]
    weighted = density * jnp.exp(-TAU * potential)
    energy = source_here * (C_TF + enhance) + external * density - C_X * density * here
    terms = [weighted, density, energy - density * potential]
    for slope in slopes:
        for axis in range(3):
            terms.append(0.5 * slope * levers[:, 1 + axis])
    lane = iota((p.yw, p.zq), 1)
    y = iota((p.yw, p.zq), 0)
    own = (lane < p.zo) & (y >= p.own_y) & (y < p.own_y + p.ny)
    rows = []
    for term in terms:
        rows.append(jnp.sum(jnp.where(own, jnp.sum(term, axis=0), 0.0), axis=0, keepdims=True))
    rows.append(jnp.zeros((SUMS - len(rows), p.zq), F32))
    sums = jnp.sum(jnp.concatenate(rows, axis=0), axis=1, keepdims=True)
    return potential, weighted, jnp.broadcast_to(sums, (SUMS, 128))


def update_scratch(p):
    def acts(planes):
        return pltpu.VMEM((planes, p.lo + 2, STRIPS, p.lanes), BF)

    return [
        pltpu.VMEM((2, p.xe, p.yw, 3 * p.zp), F32),
        acts(p.xo + 10),
        acts(p.xo + 8),
        acts(p.xo + 2),
        pltpu.VMEM((p.xo + 2, p.ze, p.lanes), F32),
        pltpu.VMEM((p.xo + 4, p.ze, p.lanes), F32),
        pltpu.VMEM((8, 128), F32),
        pltpu.VMEM((p.xo + 2, p.ze, p.narrow), F32),
    ]


def update_cost(p):
    flops = 2 * 9 * p.lanes * p.lanes * p.ze * (4 * p.xo + 20)
    return pl.CostEstimate(flops=flops, bytes_accessed=6 << 20, transcendentals=0)


def kernel_call(name, body, out_shape, n_smem, n_vmem, scratch=(), cost=None):
    return pl.pallas_call(
        body,
        name=name,
        out_shape=out_shape,
        in_specs=[SM] * n_smem + [VM] * n_vmem,
        out_specs=jax.tree.map(lambda _: VM, out_shape),
        scratch_shapes=list(scratch),
        compiler_params=pltpu.CompilerParams(vmem_limit_bytes=LIMIT),
        cost_estimate=cost,
    )


def f32(*shape):
    return jax.ShapeDtypeStruct(shape, F32)


def widen(cells, axis, dim, before, after):
    size = cells.shape[dim]
    count = lax.axis_size(axis)

    def fetch(step, start, stop):
        piece = lax.slice_in_dim(cells, start, stop, axis=dim)
        if step % count == 0:
            return piece
        return lax.ppermute(piece, axis, [(i, (i + step) % count) for i in range(count)])

    pieces = [cells]
    left = before
    step = 1
    while left > 0:
        take = min(left, size)
        pieces.insert(0, fetch(step, size - take, size))
        left -= take
        step += 1
    left = after
    step = 1
    while left > 0:
        take = min(left, size)
        pieces.append(fetch(-step, 0, take))
        left -= take
        step += 1
    return jnp.concatenate(pieces, axis=dim)


def any_mesh(density, external, w_first, w_second, w_third, w_last):
    nx, ny, nz = density.shape
    ch = w_first.shape[1]
    yw = up(ny + 2 * REACH, 8)
    own_y = (yw - ny) // 2
    xo = up(nx, GROUP)
    p = Plan(xo, yw, own_y, ny, nz, ch)
    weights = spread_weights(p, w_first, w_second, w_third, w_last)
    axes = ("gx", "gy", "gz")
    count = nx * ny * nz * lax.axis_size("gx") * lax.axis_size("gy") * lax.axis_size("gz")
    total_mass = lax.psum(jnp.sum(density), axes)

    def body(cur, ext, *refs):
        weight_refs, (o_pot, o_weighted, o_sums), scratch = refs[:8], refs[8:11], refs[11:]
        pot, weighted, sums = update_kernel(p, cur[...], ext[...], weight_refs, scratch)
        o_pot[...] = pot
        o_weighted[...] = weighted
        o_sums[...] = sums

    call = kernel_call(
        "update",
        body,
        (f32(xo, yw, p.zq), f32(xo, yw, p.zq), f32(SUMS, 128)),
        0,
        10,
        update_scratch(p),
        update_cost(p),
    )
    ext = jnp.pad(
        external, ((0, xo - nx), (own_y, yw - ny - own_y), (0, p.zq - nz))
    )
    current = density
    chem, stress = [], []
    for _ in range(STEPS):
        tile = widen(current, "gz", 2, p.zh, p.ze - nz - p.zh)
        tile = widen(tile, "gy", 1, own_y, yw - ny - own_y)
        tile = widen(tile, "gx", 0, REACH, REACH)
        tile = jnp.pad(tile, ((0, 0), (0, 0), (0, p.zp - p.ze)), constant_values=1.0)
        pot, weighted, sums = call(tile, ext, *weights)
        totals = lax.psum(sums[:, 0], axes)
        chem.append(jnp.log(total_mass / totals[0]) / TAU)
        moments = totals[3:12].reshape(3, 3)
        stress.append((moments + jnp.eye(3, dtype=F32) * totals[2]) / count)
        current = weighted[:nx, own_y : own_y + ny, :nz] * (total_mass / totals[0])
        potential = pot[:nx, own_y : own_y + ny, :nz]
    return current, potential, jnp.stack(chem), jnp.stack(stress)


def split_pairs(density, external, w_first, w_second, w_third, w_last):
    nx, ny, nz = density.shape
    ch = w_first.shape[1]
    half = nz // 2
    p = Plan(nx, 2 * ny, 0, 2 * ny, half, ch)
    lanes = p.zp
    gy = lax.axis_index("gy")
    where = gy.astype(jnp.int32).reshape(1)
    cells = nx * ny * nz * 16
    axes = ("gx", "gy", "gz")

    def along_x(cells_out, step):
        return lax.ppermute(cells_out, "gx", [(i, (i + step) % 4) for i in range(4)])

    def quarter(number):
        return (number % 2) * 2 + number // 2

    def along_z(cells_out, step):
        pairs = [(quarter(q), quarter((q + step) % 4)) for q in range(4)]
        return lax.ppermute(cells_out, ("gy", "gz"), pairs)

    weights = spread_weights(p, w_first, w_second, w_third, w_last)

    wide = jnp.concatenate(
        [
            along_x(density[nx - REACH :], 1),
            density,
            along_x(density[:REACH], -1),
            external,
        ],
        axis=0,
    )
    from_y = lax.ppermute(wide, "gy", [(0, 1), (1, 0)])
    from_z = lax.ppermute(wide, "gz", [(0, 1), (1, 0)])
    from_yz = lax.ppermute(wide, ("gy", "gz"), [(i, 3 - i) for i in range(4)])
    planes = p.xe + nx

    def emit(weighted, sums, o_own, o_low, o_high):
        extra = sums.reshape(2, 8, 128)
        o_own[...] = weighted
        o_low[:REACH] = weighted[:REACH]
        o_low[REACH:] = extra
        o_high[:REACH] = weighted[nx - REACH :]
        o_high[REACH:] = extra

    def first_body(where_ref, own, y, z, yz, *refs):
        weight_refs, outs, tile, scratch = refs[:8], refs[8:12], refs[12], refs[13:]
        second = where_ref[0] == 1
        shift = jnp.where(second, nz - half + p.zh, p.zh)
        lane = iota((planes, p.yw, lanes), 2)
        for ref, other in ((own, y), (z, yz)):
            mine, theirs = ref[...], other[...]
            lower = jnp.where(second, theirs, mine)
            upper = jnp.where(second, mine, theirs)
            cells_here = jnp.concatenate([lower, upper], axis=1)
            moved = pltpu.roll(cells_here, shift, 2)
            if ref is own:
                tile[...] = moved
            else:
                begin = jnp.where(second, half + p.zh, 0)
                end = jnp.where(second, lanes, p.zh)
                tile[...] = jnp.where((lane >= begin) & (lane < end), moved, tile[...])
        cur = tile[: p.xe]
        ext = pltpu.roll(tile[p.xe :], lanes - p.zh, 2)
        _, weighted, sums = update_kernel(p, cur, ext, weight_refs, scratch)
        emit(weighted, sums, *outs[:3])
        outs[3][...] = ext

    message = f32(REACH + 2, p.yw, lanes)
    own, low, high, ext = kernel_call(
        "update_one",
        first_body,
        (f32(nx, p.yw, lanes), message, message, f32(nx, p.yw, lanes)),
        1,
        12,
        [pltpu.VMEM((planes, p.yw, lanes), F32)] + update_scratch(p),
        update_cost(p),
    )(where, wide, from_y, from_z, from_yz, *weights)

    left = along_x(high, 1)
    right = along_x(low, -1)
    far = along_x(low[REACH:], 2)

    packs = up(p.xe, 8) // 8

    def join_body(own_ref, low_ref, left_ref, right_ref, far_ref, o_tile, o_down, o_up, o_sums):
        tile = jnp.concatenate([left_ref[:REACH], own_ref[...], right_ref[:REACH]], axis=0)
        sums = low_ref[REACH:] + left_ref[REACH:] + right_ref[REACH:] + far_ref[...]
        o_tile[...] = tile
        o_sums[...] = sums
        lane = lax.div(iota((p.yw, lanes), 1), p.zh)
        for ref, start in ((o_down, 0), (o_up, half - p.zh)):
            for pack in range(packs):
                joined = jnp.zeros((p.yw, lanes), F32)
                for k in range(min(8, p.xe - 8 * pack)):
                    moved = pltpu.roll(tile[8 * pack + k], (k * p.zh - start) % lanes, 1)
                    joined = jnp.where(lane == k, moved, joined)
                ref[pack] = joined
            ref[packs:] = sums

    edge = f32(packs + 2, p.yw, lanes)
    tile, down, upper, sums = kernel_call(
        "join",
        join_body,
        (f32(p.xe, p.yw, lanes), edge, edge, f32(2, 8, 128)),
        0,
        5,
    )(own, low, left, right, far)
    below = along_z(upper, 1)
    above = along_z(down, -1)
    across = lax.ppermute(sums, "gz", [(0, 1), (1, 0)])

    def second_body(where_ref, tile_ref, below_ref, above_ref, sums_ref, across_ref, ext_ref, *refs):
        weight_refs, outs, cur, scratch = refs[:8], refs[8:12], refs[12], refs[13:]
        o_keep, o_send, o_sums, o_totals = outs
        totals = sums_ref[...] + across_ref[...] + below_ref[packs:] + above_ref[packs:]
        o_totals[...] = totals
        scale = totals[0, 1:2, :] / totals[0, 0:1, :]
        lane = iota((p.yw, lanes), 1)
        for x in range(p.xe):
            pack, k = divmod(x, 8)
            lower = pltpu.roll(below_ref[pack], -k * p.zh % lanes, 1)
            top = pltpu.roll(above_ref[pack], (p.zh + half - k * p.zh) % lanes, 1)
            middle = pltpu.roll(tile_ref[x], p.zh, 1)
            joined = jnp.where(lane < p.zh, lower, jnp.where(lane < p.zh + half, middle, top))
            cur[x] = joined * scale
        pot, weighted, sums_here = update_kernel(p, cur[...], ext_ref[...], weight_refs, scratch)
        o_sums[...] = sums_here
        both = jnp.where(
            iota(pot.shape, 2) < half, pot, pltpu.roll(weighted, half, 2)
        )
        second = where_ref[0] == 1
        lower, top = both[:, :ny], both[:, ny:]
        o_keep[...] = jnp.where(second, top, lower)
        o_send[...] = jnp.where(second, lower, top)

    share = f32(nx, ny, lanes)
    keep, send, sums, totals = kernel_call(
        "update_two",
        second_body,
        (share, share, f32(SUMS, 128), f32(2, 8, 128)),
        1,
        14,
        [pltpu.VMEM((p.xe, p.yw, lanes), F32)] + update_scratch(p),
        update_cost(p),
    )(where, tile, below, above, sums, across, ext, *weights)

    other = lax.ppermute(send, "gy", [(0, 1), (1, 0)])
    gathered = lax.all_to_all(
        jnp.broadcast_to(sums[None], (16, SUMS, 128)), axes, 0, 0, tiled=True
    )

    def last_body(where_ref, keep_ref, other_ref, all_ref, totals_ref, o_new, o_pot, o_chem, o_stress):
        first = totals_ref[...].reshape(SUMS, 128)
        last = jnp.sum(all_ref[...], axis=0)
        mass = first[1:2]
        scale = mass / last[0:1]
        second = where_ref[0] == 1
        mine, theirs = keep_ref[...], other_ref[...]
        lower = jnp.where(second, theirs, mine)
        top = jnp.where(second, mine, theirs)
        lane = iota((nx, ny, nz), 2)
        o_pot[...] = jnp.where(lane < half, lower, pltpu.roll(top, half, 2))
        o_new[...] = jnp.where(lane < half, pltpu.roll(lower, half, 2), top) * scale
        row, column = iota((8, 128), 0), iota((8, 128), 1)
        for step, total in enumerate((first, last)):
            o_chem[step : step + 1] = jnp.log(mass / total[0:1]) * (1.0 / TAU)
            stress = jnp.where(row == column, total[2:3], 0.0)
            for a in range(3):
                for b in range(3):
                    k = 3 + 3 * a + b
                    stress = stress + jnp.where((row == a) & (column == b), total[k : k + 1], 0.0)
            o_stress[step] = stress[:3, :3] * (1.0 / cells)

    new, potential, chem, stress = kernel_call(
        "finish",
        last_body,
        (f32(nx, ny, nz), f32(nx, ny, nz), f32(STEPS, 128), f32(STEPS, 3, 3)),
        1,
        4,
    )(where, keep, other, gathered, totals)
    return new, potential, chem[:, 0], stress


def on_device(density, external, w_first, w_second, w_third, w_last):
    mesh = tuple(lax.axis_size(axis) for axis in ("gx", "gy", "gz"))
    if mesh == (4, 2, 2) and density.shape == (8, 4, 128):
        return split_pairs(density, external, w_first, w_second, w_third, w_last)
    return any_mesh(density, external, w_first, w_second, w_third, w_last)


def solution(mesh):
    cells = P(("boxes", "gx"), "gy", "gz")
    return jax.shard_map(
        on_device,
        mesh=mesh,
        in_specs=(cells, cells, P(), P(), P(), P()),
        out_specs=(cells, cells, P("boxes"), P("boxes", None, None)),
        check_vma=False,
    )
```

```python
import functools

import jax
import jax.numpy as jnp
from jax import lax
from jax.experimental import pallas as pl
from jax.experimental.pallas import tpu as pltpu
from jax.sharding import PartitionSpec as P

STEPS = 2
C_TF = 2.871234
C_X = 0.7385588
TAU = 0.1
REACH = 6
STRIPS = 16
GROUP = 4
SUMS = 16
BF = jnp.bfloat16
F32 = jnp.float32
VM = pl.BlockSpec(memory_space=pltpu.VMEM)
SM = pl.BlockSpec(memory_space=pltpu.SMEM)


def up(number, unit):
    return -(-number // unit) * unit


def iota(shape, dim):
    return lax.broadcasted_iota(jnp.int32, shape, dim)


def dot(a, b):
    return jnp.dot(a, b, preferred_element_type=F32)


def dot_tn(a, b):
    return lax.dot_general(a, b, (((0,), (0,)), ((), ())), preferred_element_type=F32)


def dot_nt(a, b):
    return lax.dot_general(a, b, (((1,), (1,)), ((), ())), preferred_element_type=F32)


class Plan:
    def __init__(self, xo, yw, own_y, ny, zo, ch, limit):
        self.xo, self.yw, self.own_y, self.ny, self.zo, self.ch = xo, yw, own_y, ny, zo, ch
        self.limit = limit << 20
        self.xe = xo + 2 * REACH
        self.ze = up(zo + 2 * REACH, STRIPS)
        self.zh = (self.ze - zo) // 2
        self.lo = self.ze // STRIPS
        self.zp = up(self.ze, 128)
        self.zq = up(zo, 128)
        self.lanes = yw * ch
        self.fields = 4 * yw
        self.narrow = up(GROUP * self.fields, 128)


def weights_kernel(p, dense_in, single_in, dense_out, first_out, last_out):
    ch, yw, lanes = p.ch, p.yw, p.lanes

    for ref_in, ref_out in zip(dense_in, dense_out):
        taps = []
        for ty in range(3):
            taps.append(
                jnp.concatenate(
                    [ref_in[26 - (9 * (t // 3) + 3 * ty + t % 3)] for t in range(9)], axis=0
                )
            )
        taps = jnp.concatenate(taps, axis=1)
        row, column = iota((3 * ch, lanes), 0), iota((3 * ch, lanes), 1)
        ty = lax.div(row, ch)
        for yi in range(yw):
            yo = lax.rem(yi + 1 - ty + yw, yw)
            place = jnp.where(column == row + (yo - ty) * ch, 1.0, 0.0).astype(BF)
            spread = dot(taps, place)
            ref_out[:, yi * ch : (yi + 1) * ch, :] = spread.astype(BF).reshape(9, ch, lanes)

    tile = (
        jnp.bitwise_and(iota((ch, lanes), 1), ch - 1) == iota((ch, lanes), 0)
    ).astype(F32).astype(BF)
    tiled = [dot(ref[...], tile).astype(BF) for ref in single_in]

    rows = 18 * yw
    row = iota((rows, 1), 0)
    yi = lax.rem(row, yw)
    tx = lax.rem(lax.div(row, yw), 3)
    tz = lax.rem(lax.div(row, 3 * yw), 3)
    yo = lax.div(iota((rows, lanes), 1), ch)
    for wide, ref_out, direction in zip(tiled, first_out, (1, -1)):
        total = jnp.zeros((rows, lanes), F32)
        for ty in range(3):
            number = 9 * tx + 3 * ty + tz
            number = number if direction > 0 else 26 - number
            pick = (iota((rows, 27), 1) == number).astype(F32).astype(BF)
            here = lax.rem(yo + (ty - 1 + yw), yw) == yi
            total = total + jnp.where(here, dot(pick, wide), 0.0)
        ref_out[...] = total.astype(BF)

    rows = p.narrow
    row = iota((rows, 1), 0)
    yo = lax.rem(row, yw)
    field = lax.rem(lax.div(row, yw), 4)
    tx = lax.div(row, 4 * yw)
    yi = lax.div(iota((rows, lanes), 1), ch)
    for wide, ref_out, direction in zip(tiled[::-1], last_out, (1, -1)):
        for tz in range(3):
            total = jnp.zeros((rows, lanes), F32)
            for ty in range(3):
                number = 9 * tx + 3 * ty + tz
                number = number if direction > 0 else 26 - number
                if direction > 0:
                    factor = jnp.where(field == 0, 1, 0)
                else:
                    factor = jnp.where(
                        field == 0,
                        1,
                        jnp.where(field == 1, 1 - tx, jnp.where(field == 2, 1 - ty, 1 - tz)),
                    )
                factor = jnp.where(tx < 3, factor, 0).astype(F32)
                pick = (iota((rows, 27), 1) == number).astype(F32).astype(BF)
                here = lax.rem(yo + (ty - 1 + yw), yw) == yi
                total = total + jnp.where(here, dot(pick, wide), 0.0) * factor
            ref_out[tz] = total.astype(BF)


def spread_weights(p, w_first, w_second, w_third, w_last):
    def body(second, third, first, last, o_second, o_third, o_first, o_back, o_last, o_cot):
        weights_kernel(
            p, (second, third), (first, last), (o_second, o_third), (o_first, o_back), (o_last, o_cot)
        )

    dense = jax.ShapeDtypeStruct((9, p.lanes, p.lanes), BF)
    single = jax.ShapeDtypeStruct((18 * p.yw, p.lanes), BF)
    narrow = jax.ShapeDtypeStruct((3, p.narrow, p.lanes), BF)
    flops = 2 * 2 * 9 * 3 * p.ch * p.lanes * p.lanes
    return pl.pallas_call(
        body,
        name="spread_weights",
        out_shape=(dense,) * 2 + (single,) * 2 + (narrow,) * 2,
        in_specs=[VM] * 4,
        out_specs=(VM,) * 6,
        compiler_params=pltpu.CompilerParams(vmem_limit_bytes=p.limit),
        cost_estimate=pl.CostEstimate(flops=flops, bytes_accessed=3 << 20, transcendentals=0),
    )(w_second, w_third, w_first, w_last)


def cube_root(value):
    guess = jnp.exp(jnp.log(value) * (1.0 / 3.0))
    return guess - (guess - value / (guess * guess)) * (1.0 / 3.0)


def store_edges(p, ref, place, value):
    tiles = value.reshape(p.lo, STRIPS, p.lanes)
    ref[place, 1 : p.lo + 1] = tiles.astype(BF)
    ref[place, 0] = pltpu.roll(tiles[p.lo - 1], 1, 0).astype(BF)
    ref[place, p.lo + 1] = pltpu.roll(tiles[0], STRIPS - 1, 0).astype(BF)


def blocks(total, size):
    return [(start, min(size, total - start)) for start in range(0, total, size)]


def dense_planes(p, ref, w_ref, start, count, forward):
    total = None
    for t in range(9):
        tx, tz = divmod(t, 3)
        rows = ref[start + tx : start + tx + count, tz : tz + p.lo]
        rows = rows.reshape(count * p.ze, p.lanes)
        part = dot_nt(rows, w_ref[8 - t]) if forward else dot(rows, w_ref[t])
        total = part if total is None else total + part
    return total


def gate(value):
    logistic = 0.5 * jnp.tanh(0.5 * value) + 0.5
    act = value * logistic
    return logistic, act


def slope_of(value, logistic, act):
    return logistic * (1.0 + value - act)


def to_planes(p, field, spread, planes_ref):
    high = field.astype(BF)
    low = (field - high.astype(F32)).astype(BF)
    flat = jnp.concatenate(
        [high.reshape(p.xe * p.yw, p.zp), low.reshape(p.xe * p.yw, p.zp)], axis=0
    )
    planes_ref[...] = dot(flat, spread).reshape(2, p.xe, p.yw, 3 * p.zp)


def single_plane(p, planes_ref, place, w_ref):
    pieces = []
    for half in range(2):
        for tz in range(3):
            piece = planes_ref[half, place : place + 3, :, tz * p.zp : (tz + 1) * p.zp]
            pieces.append(piece.reshape(3 * p.yw, p.zp))
    window = jnp.concatenate(pieces, axis=0).astype(BF)
    return dot_tn(window, w_ref[...])[: p.ze]


def narrow_fold(p, ref, w_ref, planes_ref, back):
    for start, count in blocks(p.xo + 2, 5):
        total = None
        for tz in range(3):
            rows = ref[start : start + count, tz : tz + p.lo].reshape(count * p.ze, p.lanes)
            part = dot_nt(rows, w_ref[tz])
            total = part if total is None else total + part
        planes_ref[start : start + count] = total.reshape(count, p.ze, p.narrow)
    lane = lax.div(iota((p.ze, p.narrow), 1), p.fields)
    fields = []
    for first in range(0, p.xo, GROUP):
        joined = jnp.zeros((p.ze, p.narrow), F32)
        for k in range(GROUP):
            total = None
            for tx in range(3):
                part = planes_ref[first + k + tx]
                shift = (k - tx) * p.fields % p.narrow
                part = pltpu.roll(part, shift, 1) if shift else part
                total = part if total is None else total + part
            joined = jnp.where(lane == k, total, joined)
        high = joined.astype(BF)
        rest = joined - high.astype(F32)
        mid = rest.astype(BF)
        low = (rest - mid.astype(F32)).astype(BF)
        parts = jnp.concatenate([high, mid, low], axis=0)
        natural = dot_tn(parts, back)[: GROUP * p.fields]
        fields.append(natural.reshape(GROUP, 4, p.yw, p.zq))
    return jnp.concatenate(fields, axis=0)


def update_kernel(p, current, external, weights, scratch):
    w_two, w_three, w_one, w_source, w_enhance, w_lever = weights
    planes, act_a, act_b, act_c, slope_one, slope_two, narrow = scratch

    current = jnp.where(iota(current.shape, 2) < p.ze, current, 1.0)
    cube = cube_root(current)
    source = current * cube * cube

    shape = (p.zp, 3 * p.zp)
    lane = iota(shape, 1)
    tz = lax.div(lane, p.zp)
    row = lane - tz * p.zp
    cell = p.lo * jnp.bitwise_and(row, STRIPS - 1) + lax.div(row, STRIPS) + tz - 1
    spread = jnp.where((cell == iota(shape, 0)) & (row < p.ze), 1.0, 0.0).astype(BF)
    shape = (3 * p.ze, p.zq)
    row = lax.rem(iota(shape, 0), p.ze)
    cell = p.lo * jnp.bitwise_and(row, STRIPS - 1) + lax.div(row, STRIPS) - p.zh
    back = jnp.where((cell == iota(shape, 1)) & (cell < p.zo), 1.0, 0.0).astype(BF)

    to_planes(p, cube, spread, planes)
    for x in range(p.xo + 10):
        value = single_plane(p, planes, x, w_one)
        logistic, act = gate(value)
        store_edges(p, act_a, x, act)
        if 4 <= x < p.xo + 6:
            slope_one[x - 4] = slope_of(value, logistic, act)

    for start, count in blocks(p.xo + 8, 4):
        values = dense_planes(p, act_a, w_two, start, count, True)
        for k in range(count):
            x = start + k
            value = values[k * p.ze : (k + 1) * p.ze]
            logistic, act = gate(value)
            store_edges(p, act_b, x, act)
            if 2 <= x < p.xo + 6:
                slope_two[x - 2] = slope_of(value, logistic, act)

    to_planes(p, source, spread, planes)
    for start, count in blocks(p.xo + 6, 7):
        values = dense_planes(p, act_b, w_three, start, count, True)
        for k in range(count):
            x = start + k
            value = values[k * p.ze : (k + 1) * p.ze]
            logistic, act = gate(value)
            if 2 <= x < p.xo + 4:
                store_edges(p, act_c, x - 2, act)
            slope = slope_of(value, logistic, act)
            store_edges(p, act_a, x, single_plane(p, planes, x + 2, w_source) * slope)

    enhance = narrow_fold(p, act_c, w_enhance, narrow, back)[:, 0]

    for start, count in blocks(p.xo + 4, 4):
        values = dense_planes(p, act_a, w_three, start, count, False)
        for k in range(count):
            x = start + k
            store_edges(p, act_b, x, values[k * p.ze : (k + 1) * p.ze] * slope_two[x])

    for start, count in blocks(p.xo + 2, 5):
        values = dense_planes(p, act_b, w_two, start, count, False)
        for k in range(count):
            x = start + k
            store_edges(p, act_c, x, values[k * p.ze : (k + 1) * p.ze] * slope_one[x])

    levers = narrow_fold(p, act_c, w_lever, narrow, back)

    def natural(field, step):
        return pltpu.roll(field, (p.zp - p.zh - step) % p.zp, 2)[:, :, : p.zq]

    inner = cube[REACH : REACH + p.xo]
    here = natural(inner, 0)
    density = natural(current[REACH : REACH + p.xo], 0)
    source_here = natural(source[REACH : REACH + p.xo], 0)
    squared = here * here
    potential = (
        5.0 / 3.0 * squared * (C_TF + enhance)
        + levers[:, 0] / (3.0 * squared)
        + external
        - 4.0 / 3.0 * C_X * here
    )
    slopes = [
        natural(cube[REACH + 1 : REACH + 1 + p.xo], 0) - natural(cube[REACH - 1 : REACH - 1 + p.xo], 0),
        pltpu.roll(here, p.yw - 1, 1) - pltpu.roll(here, 1, 1),
        natural(inner, 1) - natural(inner, -1),
    ]
    weighted = density * jnp.exp(-TAU * potential)
    energy = source_here * (C_TF + enhance) + external * density - C_X * density * here
    terms = [weighted, density, energy - density * potential]
    for slope in slopes:
        for axis in range(3):
            terms.append(0.5 * slope * levers[:, 1 + axis])
    lane = iota((p.yw, p.zq), 1)
    y = iota((p.yw, p.zq), 0)
    own = (lane < p.zo) & (y >= p.own_y) & (y < p.own_y + p.ny)
    rows = []
    for term in terms:
        rows.append(jnp.sum(jnp.where(own, jnp.sum(term, axis=0), 0.0), axis=0, keepdims=True))
    rows.append(jnp.zeros((SUMS - len(rows), p.zq), F32))
    sums = jnp.sum(jnp.concatenate(rows, axis=0), axis=1, keepdims=True)
    onto = iota((SUMS, 128), 0) == iota((SUMS, 128), 1)
    row = jnp.sum(jnp.where(onto, sums, 0.0), axis=0, keepdims=True)
    return potential, weighted, jnp.broadcast_to(row, (8, 128))


def pick(row, number):
    return jnp.sum(jnp.where(iota(row.shape, 1) == number, row, 0.0), axis=1, keepdims=True)


def update_scratch(p):
    def acts(planes):
        return pltpu.VMEM((planes, p.lo + 2, STRIPS, p.lanes), BF)

    return [
        pltpu.VMEM((2, p.xe, p.yw, 3 * p.zp), F32),
        acts(p.xo + 10),
        acts(p.xo + 8),
        acts(p.xo + 2),
        pltpu.VMEM((p.xo + 2, p.ze, p.lanes), F32),
        pltpu.VMEM((p.xo + 4, p.ze, p.lanes), F32),
        pltpu.VMEM((p.xo + 2, p.ze, p.narrow), F32),
    ]


def update_cost(p):
    flops = 2 * 9 * p.lanes * p.lanes * p.ze * (4 * p.xo + 20)
    return pl.CostEstimate(flops=flops, bytes_accessed=6 << 20, transcendentals=0)


def kernel_call(p, name, body, out_shape, n_smem, n_vmem, scratch=(), cost=None):
    return pl.pallas_call(
        body,
        name=name,
        out_shape=out_shape,
        in_specs=[SM] * n_smem + [VM] * n_vmem,
        out_specs=tuple(SM if len(shape.shape) == 1 else VM for shape in out_shape),
        scratch_shapes=list(scratch),
        compiler_params=pltpu.CompilerParams(vmem_limit_bytes=p.limit),
        cost_estimate=cost,
    )


def f32(*shape):
    return jax.ShapeDtypeStruct(shape, F32)


def widen(cells, axis, dim, before, after):
    size = cells.shape[dim]
    count = lax.axis_size(axis)

    def fetch(step, start, stop):
        piece = lax.slice_in_dim(cells, start, stop, axis=dim)
        if step % count == 0:
            return piece
        return lax.ppermute(piece, axis, [(i, (i + step) % count) for i in range(count)])

    pieces = [cells]
    left = before
    step = 1
    while left > 0:
        take = min(left, size)
        pieces.insert(0, fetch(step, size - take, size))
        left -= take
        step += 1
    left = after
    step = 1
    while left > 0:
        take = min(left, size)
        pieces.append(fetch(-step, 0, take))
        left -= take
        step += 1
    return jnp.concatenate(pieces, axis=dim)


def any_mesh(density, external, w_first, w_second, w_third, w_last):
    nx, ny, nz = density.shape
    ch = w_first.shape[1]
    yw = up(ny + 2 * REACH, 8)
    own_y = (yw - ny) // 2
    xo = up(nx, GROUP)
    p = Plan(xo, yw, own_y, ny, nz, ch, 60)
    weights = spread_weights(p, w_first, w_second, w_third, w_last)
    axes = ("gx", "gy", "gz")
    count = nx * ny * nz * lax.axis_size("gx") * lax.axis_size("gy") * lax.axis_size("gz")
    total_mass = lax.psum(jnp.sum(density), axes)

    def body(cur, ext, *refs):
        weight_refs, (o_pot, o_weighted, o_sums), scratch = refs[:6], refs[6:9], refs[9:]
        pot, weighted, sums = update_kernel(p, cur[...], ext[...], weight_refs, scratch)
        o_pot[...] = pot
        o_weighted[...] = weighted
        o_sums[...] = sums

    call = kernel_call(
        p,
        "update",
        body,
        (f32(xo, yw, p.zq), f32(xo, yw, p.zq), f32(8, 128)),
        0,
        8,
        update_scratch(p),
        update_cost(p),
    )
    ext = jnp.pad(
        external, ((0, xo - nx), (own_y, yw - ny - own_y), (0, p.zq - nz))
    )
    current = density
    chem, stress = [], []
    for _ in range(STEPS):
        tile = widen(current, "gz", 2, p.zh, p.ze - nz - p.zh)
        tile = widen(tile, "gy", 1, own_y, yw - ny - own_y)
        tile = widen(tile, "gx", 0, REACH, REACH)
        tile = jnp.pad(tile, ((0, 0), (0, 0), (0, p.zp - p.ze)), constant_values=1.0)
        pot, weighted, sums = call(tile, ext, *weights)
        totals = lax.psum(sums[0, :SUMS], axes)
        chem.append(jnp.log(total_mass / totals[0]) / TAU)
        moments = totals[3:12].reshape(3, 3)
        stress.append((moments + jnp.eye(3, dtype=F32) * totals[2]) / count)
        current = weighted[:nx, own_y : own_y + ny, :nz] * (total_mass / totals[0])
        potential = pot[:nx, own_y : own_y + ny, :nz]
    return current, potential, jnp.stack(chem), jnp.stack(stress)


def split_pairs(density, external, w_first, w_second, w_third, w_last):
    nx, ny, nz = density.shape
    ch = w_first.shape[1]
    half = nz // 2
    p = Plan(nx, 2 * ny, 0, 2 * ny, half, ch, 20)
    lanes = p.zp
    gy = lax.axis_index("gy")
    where = gy.astype(jnp.int32).reshape(1)
    cells = nx * ny * nz * 16
    axes = ("gx", "gy", "gz")

    def along_x(cells_out, step):
        return lax.ppermute(cells_out, "gx", [(i, (i + step) % 4) for i in range(4)])

    def quarter(number):
        return (number % 2) * 2 + number // 2

    def along_z(cells_out, step):
        pairs = [(quarter(q), quarter((q + step) % 4)) for q in range(4)]
        return lax.ppermute(cells_out, ("gy", "gz"), pairs)

    weights = spread_weights(p, w_first, w_second, w_third, w_last)

    wide = jnp.concatenate(
        [
            along_x(density[nx - REACH :], 1),
            density,
            along_x(density[:REACH], -1),
            external,
        ],
        axis=0,
    )
    from_y = lax.ppermute(wide, "gy", [(0, 1), (1, 0)])
    from_z = lax.ppermute(wide, "gz", [(0, 1), (1, 0)])
    from_yz = lax.ppermute(wide, ("gy", "gz"), [(i, 3 - i) for i in range(4)])
    planes = p.xe + nx

    def first_body(where_ref, own, y, z, yz, *refs):
        weight_refs, outs, tile, scratch = refs[:6], refs[6:11], refs[11], refs[12:]
        second = where_ref[0] == 1
        shift = jnp.where(second, nz - half + p.zh, p.zh)
        lane = iota((planes, p.yw, lanes), 2)
        for ref, other in ((own, y), (z, yz)):
            mine, theirs = ref[...], other[...]
            lower = jnp.where(second, theirs, mine)
            upper = jnp.where(second, mine, theirs)
            cells_here = jnp.concatenate([lower, upper], axis=1)
            moved = pltpu.roll(cells_here, shift, 2)
            if ref is own:
                tile[...] = moved
            else:
                begin = jnp.where(second, half + p.zh, 0)
                end = jnp.where(second, lanes, p.zh)
                tile[...] = jnp.where((lane >= begin) & (lane < end), moved, tile[...])
        cur = tile[: p.xe]
        ext = pltpu.roll(tile[p.xe :], lanes - p.zh, 2)
        _, weighted, sums = update_kernel(p, cur, ext, weight_refs, scratch)
        o_own, o_low, o_high, o_ext, o_sums = outs
        o_own[...] = weighted
        o_low[:REACH] = weighted[:REACH]
        o_low[REACH] = sums
        o_high[:REACH] = weighted[nx - REACH :]
        o_high[REACH] = sums
        o_ext[...] = ext
        o_sums[...] = sums

    message = f32(REACH + 1, p.yw, lanes)
    own, low, high, ext, sums = kernel_call(
        p,
        "update_one",
        first_body,
        (f32(nx, p.yw, lanes), message, message, f32(nx, p.yw, lanes), f32(8, 128)),
        1,
        10,
        [pltpu.VMEM((planes, p.yw, lanes), F32)] + update_scratch(p),
        update_cost(p),
    )(where, wide, from_y, from_z, from_yz, *weights)

    left = along_x(high, 1)
    right = along_x(low, -1)
    far = along_x(sums, 2)

    packs = up(p.xe, 8) // 8

    def join_body(own_ref, sums_ref, left_ref, right_ref, far_ref, o_tile, o_down, o_up, o_sums):
        tile = jnp.concatenate([left_ref[:REACH], own_ref[...], right_ref[:REACH]], axis=0)
        sums = sums_ref[...] + left_ref[REACH] + right_ref[REACH] + far_ref[...]
        o_tile[...] = tile
        o_sums[...] = sums
        lane = lax.div(iota((p.yw, lanes), 1), p.zh)
        for ref, start in ((o_down, 0), (o_up, half - p.zh)):
            for pack in range(packs):
                joined = jnp.zeros((p.yw, lanes), F32)
                for k in range(min(8, p.xe - 8 * pack)):
                    moved = pltpu.roll(tile[8 * pack + k], (k * p.zh - start) % lanes, 1)
                    joined = jnp.where(lane == k, moved, joined)
                ref[pack] = joined
            ref[packs] = sums

    edge = f32(packs + 1, p.yw, lanes)
    tile, down, upper, sums = kernel_call(
        p,
        "join",
        join_body,
        (f32(p.xe, p.yw, lanes), edge, edge, f32(8, 128)),
        0,
        5,
    )(own, sums, left, right, far)
    below = along_z(upper, 1)
    above = along_z(down, -1)
    across = lax.ppermute(sums, "gz", [(0, 1), (1, 0)])

    def second_body(where_ref, tile_ref, below_ref, above_ref, sums_ref, across_ref, ext_ref, *refs):
        weight_refs, outs, cur, scratch = refs[:6], refs[6:10], refs[10], refs[11:]
        o_keep, o_send, o_sums, o_totals = outs
        totals = sums_ref[...] + across_ref[...] + below_ref[packs] + above_ref[packs]
        o_totals[...] = totals
        scale = pick(totals, 1) / pick(totals, 0)
        lane = iota((p.yw, lanes), 1)
        for x in range(p.xe):
            pack, k = divmod(x, 8)
            lower = pltpu.roll(below_ref[pack], -k * p.zh % lanes, 1)
            top = pltpu.roll(above_ref[pack], (p.zh + half - k * p.zh) % lanes, 1)
            middle = pltpu.roll(tile_ref[x], p.zh, 1)
            joined = jnp.where(lane < p.zh, lower, jnp.where(lane < p.zh + half, middle, top))
            cur[x] = joined * scale
        pot, weighted, sums_here = update_kernel(p, cur[...], ext_ref[...], weight_refs, scratch)
        o_sums[...] = jnp.broadcast_to(sums_here, (16, 8, 128))
        both = jnp.where(
            iota(pot.shape, 2) < half, pot, pltpu.roll(weighted, half, 2)
        )
        second = where_ref[0] == 1
        lower, top = both[:, :ny], both[:, ny:]
        o_keep[...] = jnp.where(second, top, lower)
        o_send[...] = jnp.where(second, lower, top)

    share = f32(nx, ny, lanes)
    keep, send, sums, totals = kernel_call(
        p,
        "update_two",
        second_body,
        (share, share, f32(16, 8, 128), f32(8, 128)),
        1,
        12,
        [pltpu.VMEM((p.xe, p.yw, lanes), F32)] + update_scratch(p),
        update_cost(p),
    )(where, tile, below, above, sums, across, ext, *weights)

    other = lax.ppermute(send, "gy", [(0, 1), (1, 0)])
    gathered = lax.all_to_all(sums, axes, 0, 0, tiled=True)

    def last_body(where_ref, keep_ref, other_ref, all_ref, totals_ref, o_new, o_pot, o_chem, o_stress):
        first = totals_ref[...]
        last = jnp.sum(all_ref[...], axis=0)
        mass = pick(first, 1)
        scale = mass / pick(last, 0)
        second = where_ref[0] == 1
        mine, theirs = keep_ref[...], other_ref[...]
        lower = jnp.where(second, theirs, mine)
        top = jnp.where(second, mine, theirs)
        lane = iota((nx, ny, nz), 2)
        o_pot[...] = jnp.where(lane < half, lower, pltpu.roll(top, half, 2))
        o_new[...] = jnp.where(lane < half, pltpu.roll(lower, half, 2), top) * scale[:ny]
        lane = iota((8, 128), 1)
        for step, total in enumerate((first, last)):
            chem = jnp.log(mass / pick(total, 0)) * (1.0 / TAU)
            o_chem[step] = chem[0, 0]
            for a in range(3):
                moments = pltpu.roll(total, 128 - 3 - 3 * a, 1)
                row = moments + jnp.where(lane == a, pick(total, 2), 0.0)
                o_stress[a, step : step + 1] = row[:1, :3] * (1.0 / cells)

    new, potential, chem, stress = kernel_call(
        p,
        "finish",
        last_body,
        (f32(nx, ny, nz), f32(nx, ny, nz), f32(STEPS), f32(3, STEPS, 3)),
        1,
        4,
    )(where, keep, other, gathered, totals)
    return new, potential, chem, jnp.transpose(stress, (1, 0, 2))


def on_device(density, external, w_first, w_second, w_third, w_last):
    mesh = tuple(lax.axis_size(axis) for axis in ("gx", "gy", "gz"))
    if mesh == (4, 2, 2) and density.shape == (8, 4, 128):
        return split_pairs(density, external, w_first, w_second, w_third, w_last)
    return any_mesh(density, external, w_first, w_second, w_third, w_last)


def solution(mesh):
    cells = P(("boxes", "gx"), "gy", "gz")
    return jax.shard_map(
        on_device,
        mesh=mesh,
        in_specs=(cells, cells, P(), P(), P(), P()),
        out_specs=(cells, cells, P("boxes"), P("boxes", None, None)),
        check_vma=False,
    )
```

```python
import functools

import jax
import jax.numpy as jnp
from jax import lax
from jax.experimental import pallas as pl
from jax.experimental.pallas import tpu as pltpu
from jax.sharding import PartitionSpec as P

STEPS = 2
C_TF = 2.871234
C_X = 0.7385588
TAU = 0.1
REACH = 6
STRIPS = 16
GROUP = 4
SUMS = 16
BF = jnp.bfloat16
F32 = jnp.float32
VM = pl.BlockSpec(memory_space=pltpu.VMEM)
SM = pl.BlockSpec(memory_space=pltpu.SMEM)
HB = pl.BlockSpec(memory_space=pltpu.HBM)


def up(number, unit):
    return -(-number // unit) * unit


def iota(shape, dim):
    return lax.broadcasted_iota(jnp.int32, shape, dim)


def dot(a, b):
    return jnp.dot(a, b, preferred_element_type=F32)


def dot_tn(a, b):
    return lax.dot_general(a, b, (((0,), (0,)), ((), ())), preferred_element_type=F32)


def dot_nt(a, b):
    return lax.dot_general(a, b, (((1,), (1,)), ((), ())), preferred_element_type=F32)


class Plan:
    def __init__(self, xo, yw, own_y, ny, zo, ch, limit):
        self.xo, self.yw, self.own_y, self.ny, self.zo, self.ch = xo, yw, own_y, ny, zo, ch
        self.limit = limit << 20
        self.xe = xo + 2 * REACH
        self.ze = up(zo + 2 * REACH, STRIPS)
        self.zh = (self.ze - zo) // 2
        self.lo = self.ze // STRIPS
        self.zp = up(self.ze, 128)
        self.zq = up(zo, 128)
        self.lanes = yw * ch
        self.fields = 4 * yw
        self.narrow = up(GROUP * self.fields, 128)


def weights_kernel(p, dense_in, single_in, dense_out, first_out, last_out):
    ch, yw, lanes = p.ch, p.yw, p.lanes

    for ref_in, ref_out in zip(dense_in, dense_out):
        taps = []
        for ty in range(3):
            taps.append(
                jnp.concatenate(
                    [ref_in[26 - (9 * (t // 3) + 3 * ty + t % 3)] for t in range(9)], axis=0
                )
            )
        taps = jnp.concatenate(taps, axis=1)
        row, column = iota((3 * ch, lanes), 0), iota((3 * ch, lanes), 1)
        ty = lax.div(row, ch)
        for yi in range(yw):
            yo = lax.rem(yi + 1 - ty + yw, yw)
            place = jnp.where(column == row + (yo - ty) * ch, 1.0, 0.0).astype(BF)
            spread = dot(taps, place)
            ref_out[:, yi * ch : (yi + 1) * ch, :] = spread.astype(BF).reshape(9, ch, lanes)

    tile = (
        jnp.bitwise_and(iota((ch, lanes), 1), ch - 1) == iota((ch, lanes), 0)
    ).astype(F32).astype(BF)
    tiled = [dot(ref[...], tile).astype(BF) for ref in single_in]

    rows = 18 * yw
    row = iota((rows, 1), 0)
    yi = lax.rem(row, yw)
    tx = lax.rem(lax.div(row, yw), 3)
    tz = lax.rem(lax.div(row, 3 * yw), 3)
    yo = lax.div(iota((rows, lanes), 1), ch)
    for wide, ref_out, direction in zip(tiled, first_out, (1, -1)):
        total = jnp.zeros((rows, lanes), F32)
        for ty in range(3):
            number = 9 * tx + 3 * ty + tz
            number = number if direction > 0 else 26 - number
            pick = (iota((rows, 27), 1) == number).astype(F32).astype(BF)
            here = lax.rem(yo + (ty - 1 + yw), yw) == yi
            total = total + jnp.where(here, dot(pick, wide), 0.0)
        ref_out[...] = total.astype(BF)

    rows = p.narrow
    row = iota((rows, 1), 0)
    yo = lax.rem(row, yw)
    field = lax.rem(lax.div(row, yw), 4)
    tx = lax.div(row, 4 * yw)
    yi = lax.div(iota((rows, lanes), 1), ch)
    for wide, ref_out, direction in zip(tiled[::-1], last_out, (1, -1)):
        for tz in range(3):
            total = jnp.zeros((rows, lanes), F32)
            for ty in range(3):
                number = 9 * tx + 3 * ty + tz
                number = number if direction > 0 else 26 - number
                if direction > 0:
                    factor = jnp.where(field == 0, 1, 0)
                else:
                    factor = jnp.where(
                        field == 0,
                        1,
                        jnp.where(field == 1, 1 - tx, jnp.where(field == 2, 1 - ty, 1 - tz)),
                    )
                factor = jnp.where(tx < 3, factor, 0).astype(F32)
                pick = (iota((rows, 27), 1) == number).astype(F32).astype(BF)
                here = lax.rem(yo + (ty - 1 + yw), yw) == yi
                total = total + jnp.where(here, dot(pick, wide), 0.0) * factor
            ref_out[tz] = total.astype(BF)


def spread_weights(p, w_first, w_second, w_third, w_last):
    inputs = (w_second, w_third, w_first, w_last)

    def body(*refs):
        hbm, outs, held, sems = refs[:4], refs[4:10], refs[10:14], refs[14]
        copies = [pltpu.make_async_copy(hbm[i], held[i], sems.at[i]) for i in range(4)]
        for copy in copies:
            copy.start()
        for copy in copies:
            copy.wait()
        weights_kernel(p, held[:2], held[2:], outs[:2], outs[2:4], outs[4:])

    dense = jax.ShapeDtypeStruct((9, p.lanes, p.lanes), BF)
    single = jax.ShapeDtypeStruct((18 * p.yw, p.lanes), BF)
    narrow = jax.ShapeDtypeStruct((3, p.narrow, p.lanes), BF)
    flops = 2 * 2 * 9 * 3 * p.ch * p.lanes * p.lanes
    return pl.pallas_call(
        body,
        name="spread_weights",
        out_shape=(dense,) * 2 + (single,) * 2 + (narrow,) * 2,
        in_specs=[HB] * 4,
        out_specs=(VM,) * 6,
        scratch_shapes=[pltpu.VMEM(a.shape, a.dtype) for a in inputs]
        + [pltpu.SemaphoreType.DMA((4,))],
        compiler_params=pltpu.CompilerParams(vmem_limit_bytes=p.limit),
        cost_estimate=pl.CostEstimate(flops=flops, bytes_accessed=3 << 20, transcendentals=0),
    )(*[pltpu.with_memory_space_constraint(a, pltpu.HBM) for a in inputs])


def cube_root(value):
    guess = jnp.exp(jnp.log(value) * (1.0 / 3.0))
    return guess - (guess - value / (guess * guess)) * (1.0 / 3.0)


def store_edges(p, ref, place, value):
    tiles = value.reshape(p.lo, STRIPS, p.lanes)
    ref[place, 1 : p.lo + 1] = tiles.astype(BF)
    ref[place, 0] = pltpu.roll(tiles[p.lo - 1], 1, 0).astype(BF)
    ref[place, p.lo + 1] = pltpu.roll(tiles[0], STRIPS - 1, 0).astype(BF)


def blocks(total, size):
    return [(start, min(size, total - start)) for start in range(0, total, size)]


def dense_planes(p, ref, w_ref, start, count, forward):
    total = None
    for t in range(9):
        tx, tz = divmod(t, 3)
        rows = ref[start + tx : start + tx + count, tz : tz + p.lo]
        rows = rows.reshape(count * p.ze, p.lanes)
        part = dot_nt(rows, w_ref[8 - t]) if forward else dot(rows, w_ref[t])
        total = part if total is None else total + part
    return total


def gate(value):
    logistic = 0.5 * jnp.tanh(0.5 * value) + 0.5
    act = value * logistic
    return logistic, act


def slope_of(value, logistic, act):
    return logistic * (1.0 + value - act)


def to_planes(p, field, spread, planes_ref):
    high = field.astype(BF)
    low = (field - high.astype(F32)).astype(BF)
    flat = jnp.concatenate(
        [high.reshape(p.xe * p.yw, p.zp), low.reshape(p.xe * p.yw, p.zp)], axis=0
    )
    planes_ref[...] = dot(flat, spread).reshape(2, p.xe, p.yw, 3 * p.zp)


def single_plane(p, planes_ref, place, w_ref):
    pieces = []
    for half in range(2):
        for tz in range(3):
            piece = planes_ref[half, place : place + 3, :, tz * p.zp : tz * p.zp + p.ze]
            pieces.append(piece.reshape(3 * p.yw, p.ze))
    window = jnp.concatenate(pieces, axis=0).astype(BF)
    return dot_tn(window, w_ref[...])


def narrow_fold(p, ref, w_ref, planes_ref, back):
    for start, count in blocks(p.xo + 2, 5):
        total = None
        for tz in range(3):
            rows = ref[start : start + count, tz : tz + p.lo].reshape(count * p.ze, p.lanes)
            part = dot_nt(rows, w_ref[tz])
            total = part if total is None else total + part
        planes_ref[start : start + count] = total.reshape(count, p.ze, p.narrow)
    lane = lax.div(iota((p.ze, p.narrow), 1), p.fields)
    fields = []
    for first in range(0, p.xo, GROUP):
        joined = jnp.zeros((p.ze, p.narrow), F32)
        for k in range(GROUP):
            total = None
            for tx in range(3):
                part = planes_ref[first + k + tx]
                shift = (k - tx) * p.fields % p.narrow
                part = pltpu.roll(part, shift, 1) if shift else part
                total = part if total is None else total + part
            joined = jnp.where(lane == k, total, joined)
        high = joined.astype(BF)
        rest = joined - high.astype(F32)
        mid = rest.astype(BF)
        low = (rest - mid.astype(F32)).astype(BF)
        parts = jnp.concatenate([high, mid, low], axis=0)
        natural = dot_tn(parts, back)[: GROUP * p.fields]
        fields.append(natural.reshape(GROUP, 4, p.yw, p.zq))
    return jnp.concatenate(fields, axis=0)


def update_kernel(p, current, external, weights, scratch):
    w_two, w_three, w_one, w_source, w_enhance, w_lever = weights
    planes, act_a, act_b, act_c, slope_one, slope_two, narrow = scratch

    current = jnp.where(iota(current.shape, 2) < p.ze, current, 1.0)
    cube = cube_root(current)
    source = current * cube * cube

    shape = (p.zp, 3 * p.zp)
    lane = iota(shape, 1)
    tz = lax.div(lane, p.zp)
    row = lane - tz * p.zp
    cell = p.lo * jnp.bitwise_and(row, STRIPS - 1) + lax.div(row, STRIPS) + tz - 1
    spread = jnp.where((cell == iota(shape, 0)) & (row < p.ze), 1.0, 0.0).astype(BF)
    shape = (3 * p.ze, p.zq)
    row = lax.rem(iota(shape, 0), p.ze)
    cell = p.lo * jnp.bitwise_and(row, STRIPS - 1) + lax.div(row, STRIPS) - p.zh
    back = jnp.where((cell == iota(shape, 1)) & (cell < p.zo), 1.0, 0.0).astype(BF)

    to_planes(p, cube, spread, planes)
    for x in range(p.xo + 10):
        value = single_plane(p, planes, x, w_one)
        logistic, act = gate(value)
        store_edges(p, act_a, x, act)
        if 4 <= x < p.xo + 6:
            slope_one[x - 4] = slope_of(value, logistic, act)

    for start, count in blocks(p.xo + 8, 4):
        values = dense_planes(p, act_a, w_two, start, count, True)
        for k in range(count):
            x = start + k
            value = values[k * p.ze : (k + 1) * p.ze]
            logistic, act = gate(value)
            store_edges(p, act_b, x, act)
            if 2 <= x < p.xo + 6:
                slope_two[x - 2] = slope_of(value, logistic, act)

    to_planes(p, source, spread, planes)
    for start, count in blocks(p.xo + 6, 7):
        values = dense_planes(p, act_b, w_three, start, count, True)
        for k in range(count):
            x = start + k
            value = values[k * p.ze : (k + 1) * p.ze]
            logistic, act = gate(value)
            if 2 <= x < p.xo + 4:
                store_edges(p, act_c, x - 2, act)
            slope = slope_of(value, logistic, act)
            store_edges(p, act_a, x, single_plane(p, planes, x + 2, w_source) * slope)

    enhance = narrow_fold(p, act_c, w_enhance, narrow, back)[:, 0]

    for start, count in blocks(p.xo + 4, 4):
        values = dense_planes(p, act_a, w_three, start, count, False)
        for k in range(count):
            x = start + k
            store_edges(p, act_b, x, values[k * p.ze : (k + 1) * p.ze] * slope_two[x])

    for start, count in blocks(p.xo + 2, 5):
        values = dense_planes(p, act_b, w_two, start, count, False)
        for k in range(count):
            x = start + k
            store_edges(p, act_c, x, values[k * p.ze : (k + 1) * p.ze] * slope_one[x])

    levers = narrow_fold(p, act_c, w_lever, narrow, back)

    def natural(field, step):
        return pltpu.roll(field, (p.zp - p.zh - step) % p.zp, 2)[:, :, : p.zq]

    inner = cube[REACH : REACH + p.xo]
    here = natural(inner, 0)
    density = natural(current[REACH : REACH + p.xo], 0)
    source_here = natural(source[REACH : REACH + p.xo], 0)
    squared = here * here
    potential = (
        5.0 / 3.0 * squared * (C_TF + enhance)
        + levers[:, 0] / (3.0 * squared)
        + external
        - 4.0 / 3.0 * C_X * here
    )
    slopes = [
        natural(cube[REACH + 1 : REACH + 1 + p.xo], 0) - natural(cube[REACH - 1 : REACH - 1 + p.xo], 0),
        pltpu.roll(here, p.yw - 1, 1) - pltpu.roll(here, 1, 1),
        natural(inner, 1) - natural(inner, -1),
    ]
    weighted = density * jnp.exp(-TAU * potential)
    energy = source_here * (C_TF + enhance) + external * density - C_X * density * here
    terms = [weighted, density, energy - density * potential]
    for slope in slopes:
        for axis in range(3):
            terms.append(0.5 * slope * levers[:, 1 + axis])
    lane = iota((p.yw, p.zq), 1)
    y = iota((p.yw, p.zq), 0)
    own = (lane < p.zo) & (y >= p.own_y) & (y < p.own_y + p.ny)
    rows = []
    for term in terms:
        rows.append(jnp.sum(jnp.where(own, jnp.sum(term, axis=0), 0.0), axis=0, keepdims=True))
    rows.append(jnp.zeros((SUMS - len(rows), p.zq), F32))
    sums = jnp.sum(jnp.concatenate(rows, axis=0), axis=1, keepdims=True)
    onto = iota((SUMS, 128), 0) == iota((SUMS, 128), 1)
    row = jnp.sum(jnp.where(onto, sums, 0.0), axis=0, keepdims=True)
    return potential, weighted, jnp.broadcast_to(row, (8, 128))


def pick(row, number):
    return jnp.sum(jnp.where(iota(row.shape, 1) == number, row, 0.0), axis=1, keepdims=True)


def update_scratch(p):
    def acts(planes):
        return pltpu.VMEM((planes, p.lo + 2, STRIPS, p.lanes), BF)

    return [
        pltpu.VMEM((2, p.xe, p.yw, 3 * p.zp), F32),
        acts(p.xo + 10),
        acts(p.xo + 8),
        acts(p.xo + 2),
        pltpu.VMEM((p.xo + 2, p.ze, p.lanes), F32),
        pltpu.VMEM((p.xo + 4, p.ze, p.lanes), F32),
        pltpu.VMEM((p.xo + 2, p.ze, p.narrow), F32),
    ]


def update_cost(p):
    flops = 2 * 9 * p.lanes * p.lanes * p.ze * (4 * p.xo + 20)
    return pl.CostEstimate(flops=flops, bytes_accessed=6 << 20, transcendentals=0)


def kernel_call(p, name, body, out_shape, n_smem, n_vmem, scratch=(), cost=None, n_hbm=0):
    return pl.pallas_call(
        body,
        name=name,
        out_shape=out_shape,
        in_specs=[SM] * n_smem + [HB] * n_hbm + [VM] * n_vmem,
        out_specs=tuple(SM if len(shape.shape) == 1 else VM for shape in out_shape),
        scratch_shapes=list(scratch),
        compiler_params=pltpu.CompilerParams(vmem_limit_bytes=p.limit),
        cost_estimate=cost,
    )


def f32(*shape):
    return jax.ShapeDtypeStruct(shape, F32)


def widen(cells, axis, dim, before, after):
    size = cells.shape[dim]
    count = lax.axis_size(axis)

    def fetch(step, start, stop):
        piece = lax.slice_in_dim(cells, start, stop, axis=dim)
        if step % count == 0:
            return piece
        return lax.ppermute(piece, axis, [(i, (i + step) % count) for i in range(count)])

    pieces = [cells]
    left = before
    step = 1
    while left > 0:
        take = min(left, size)
        pieces.insert(0, fetch(step, size - take, size))
        left -= take
        step += 1
    left = after
    step = 1
    while left > 0:
        take = min(left, size)
        pieces.append(fetch(-step, 0, take))
        left -= take
        step += 1
    return jnp.concatenate(pieces, axis=dim)


def any_mesh(density, external, w_first, w_second, w_third, w_last):
    nx, ny, nz = density.shape
    ch = w_first.shape[1]
    yw = up(ny + 2 * REACH, 8)
    own_y = (yw - ny) // 2
    xo = up(nx, GROUP)
    p = Plan(xo, yw, own_y, ny, nz, ch, 60)
    weights = spread_weights(p, w_first, w_second, w_third, w_last)
    axes = ("gx", "gy", "gz")
    count = nx * ny * nz * lax.axis_size("gx") * lax.axis_size("gy") * lax.axis_size("gz")
    total_mass = lax.psum(jnp.sum(density), axes)

    def body(cur, ext, *refs):
        weight_refs, (o_pot, o_weighted, o_sums), scratch = refs[:6], refs[6:9], refs[9:]
        pot, weighted, sums = update_kernel(p, cur[...], ext[...], weight_refs, scratch)
        o_pot[...] = pot
        o_weighted[...] = weighted
        o_sums[...] = sums

    call = kernel_call(
        p,
        "update",
        body,
        (f32(xo, yw, p.zq), f32(xo, yw, p.zq), f32(8, 128)),
        0,
        8,
        update_scratch(p),
        update_cost(p),
    )
    ext = jnp.pad(
        external, ((0, xo - nx), (own_y, yw - ny - own_y), (0, p.zq - nz))
    )
    current = density
    chem, stress = [], []
    for _ in range(STEPS):
        tile = widen(current, "gz", 2, p.zh, p.ze - nz - p.zh)
        tile = widen(tile, "gy", 1, own_y, yw - ny - own_y)
        tile = widen(tile, "gx", 0, REACH, REACH)
        tile = jnp.pad(tile, ((0, 0), (0, 0), (0, p.zp - p.ze)), constant_values=1.0)
        pot, weighted, sums = call(tile, ext, *weights)
        totals = lax.psum(sums[0, :SUMS], axes)
        chem.append(jnp.log(total_mass / totals[0]) / TAU)
        moments = totals[3:12].reshape(3, 3)
        stress.append((moments + jnp.eye(3, dtype=F32) * totals[2]) / count)
        current = weighted[:nx, own_y : own_y + ny, :nz] * (total_mass / totals[0])
        potential = pot[:nx, own_y : own_y + ny, :nz]
    return current, potential, jnp.stack(chem), jnp.stack(stress)


def split_pairs(density, external, w_first, w_second, w_third, w_last):
    nx, ny, nz = density.shape
    ch = w_first.shape[1]
    half = nz // 2
    p = Plan(nx, 2 * ny, 0, 2 * ny, half, ch, 20)
    lanes = p.zp
    gy = lax.axis_index("gy")
    where = gy.astype(jnp.int32).reshape(1)
    cells = nx * ny * nz * 16
    axes = ("gx", "gy", "gz")

    def along_x(cells_out, step):
        return lax.ppermute(cells_out, "gx", [(i, (i + step) % 4) for i in range(4)])

    def quarter(number):
        return (number % 2) * 2 + number // 2

    def along_z(cells_out, step):
        pairs = [(quarter(q), quarter((q + step) % 4)) for q in range(4)]
        return lax.ppermute(cells_out, ("gy", "gz"), pairs)

    weights = spread_weights(p, w_first, w_second, w_third, w_last)

    def widen_body(own_hbm, ext_hbm, left_ref, right_ref, o_wide, sems):
        copies = [
            pltpu.make_async_copy(own_hbm, o_wide.at[REACH : REACH + nx], sems.at[0]),
            pltpu.make_async_copy(ext_hbm, o_wide.at[p.xe :], sems.at[1]),
        ]
        for copy in copies:
            copy.start()
        o_wide[:REACH] = left_ref[nx - REACH :]
        o_wide[REACH + nx : p.xe] = right_ref[:REACH]
        for copy in copies:
            copy.wait()

    (wide,) = kernel_call(
        p,
        "widen",
        widen_body,
        (f32(p.xe + nx, ny, nz),),
        0,
        2,
        [pltpu.SemaphoreType.DMA((2,))],
        n_hbm=2,
    )(
        *[pltpu.with_memory_space_constraint(a, pltpu.HBM) for a in (density, external)],
        along_x(density, 1),
        along_x(density, -1),
    )
    from_y = lax.ppermute(wide, "gy", [(0, 1), (1, 0)])
    from_z = lax.ppermute(wide, "gz", [(0, 1), (1, 0)])
    from_yz = lax.ppermute(wide, ("gy", "gz"), [(i, 3 - i) for i in range(4)])
    planes = p.xe + nx

    def first_body(where_ref, own, y, z, yz, *refs):
        weight_refs, outs, tile, scratch = refs[:6], refs[6:11], refs[11], refs[12:]
        second = where_ref[0] == 1
        shift = jnp.where(second, nz - half + p.zh, p.zh)
        lane = iota((planes, p.yw, lanes), 2)
        for ref, other in ((own, y), (z, yz)):
            mine, theirs = ref[...], other[...]
            lower = jnp.where(second, theirs, mine)
            upper = jnp.where(second, mine, theirs)
            cells_here = jnp.concatenate([lower, upper], axis=1)
            moved = pltpu.roll(cells_here, shift, 2)
            if ref is own:
                tile[...] = moved
            else:
                begin = jnp.where(second, half + p.zh, 0)
                end = jnp.where(second, lanes, p.zh)
                tile[...] = jnp.where((lane >= begin) & (lane < end), moved, tile[...])
        cur = tile[: p.xe]
        ext = pltpu.roll(tile[p.xe :], lanes - p.zh, 2)
        _, weighted, sums = update_kernel(p, cur, ext, weight_refs, scratch)
        o_own, o_low, o_high, o_ext, o_sums = outs
        o_own[...] = weighted
        o_low[:REACH] = weighted[:REACH]
        o_low[REACH] = sums
        o_high[:REACH] = weighted[nx - REACH :]
        o_high[REACH] = sums
        o_ext[...] = ext
        o_sums[...] = sums

    message = f32(REACH + 1, p.yw, lanes)
    own, low, high, ext, sums = kernel_call(
        p,
        "update_one",
        first_body,
        (f32(nx, p.yw, lanes), message, message, f32(nx, p.yw, lanes), f32(8, 128)),
        1,
        10,
        [pltpu.VMEM((planes, p.yw, lanes), F32)] + update_scratch(p),
        update_cost(p),
    )(where, wide, from_y, from_z, from_yz, *weights)

    left = along_x(high, 1)
    right = along_x(low, -1)
    far = along_x(sums, 2)

    packs = up(p.xe, 8) // 8

    def join_body(own_ref, sums_ref, left_ref, right_ref, far_ref, o_tile, o_down, o_up, o_sums):
        tile = jnp.concatenate([left_ref[:REACH], own_ref[...], right_ref[:REACH]], axis=0)
        sums = sums_ref[...] + left_ref[REACH] + right_ref[REACH] + far_ref[...]
        o_tile[...] = tile
        o_sums[...] = sums
        lane = lax.div(iota((p.yw, lanes), 1), p.zh)
        for ref, start in ((o_down, 0), (o_up, half - p.zh)):
            for pack in range(packs):
                joined = jnp.zeros((p.yw, lanes), F32)
                for k in range(min(8, p.xe - 8 * pack)):
                    moved = pltpu.roll(tile[8 * pack + k], (k * p.zh - start) % lanes, 1)
                    joined = jnp.where(lane == k, moved, joined)
                ref[pack] = joined
            ref[packs] = sums

    edge = f32(packs + 1, p.yw, lanes)
    tile, down, upper, sums = kernel_call(
        p,
        "join",
        join_body,
        (f32(p.xe, p.yw, lanes), edge, edge, f32(8, 128)),
        0,
        5,
    )(own, sums, left, right, far)
    below = along_z(upper, 1)
    above = along_z(down, -1)
    across = lax.ppermute(sums, "gz", [(0, 1), (1, 0)])

    def second_body(where_ref, tile_ref, below_ref, above_ref, sums_ref, across_ref, ext_ref, *refs):
        weight_refs, outs, cur, scratch = refs[:6], refs[6:10], refs[10], refs[11:]
        o_keep, o_send, o_sums, o_totals = outs
        totals = sums_ref[...] + across_ref[...] + below_ref[packs] + above_ref[packs]
        o_totals[...] = totals
        scale = pick(totals, 1) / pick(totals, 0)
        lane = iota((p.yw, lanes), 1)
        for x in range(p.xe):
            pack, k = divmod(x, 8)
            lower = pltpu.roll(below_ref[pack], -k * p.zh % lanes, 1)
            top = pltpu.roll(above_ref[pack], (p.zh + half - k * p.zh) % lanes, 1)
            middle = pltpu.roll(tile_ref[x], p.zh, 1)
            joined = jnp.where(lane < p.zh, lower, jnp.where(lane < p.zh + half, middle, top))
            cur[x] = joined * scale
        pot, weighted, sums_here = update_kernel(p, cur[...], ext_ref[...], weight_refs, scratch)
        o_sums[...] = jnp.broadcast_to(sums_here, (16, 8, 128))
        both = jnp.where(
            iota(pot.shape, 2) < half, pot, pltpu.roll(weighted, half, 2)
        )
        second = where_ref[0] == 1
        lower, top = both[:, :ny], both[:, ny:]
        o_keep[...] = jnp.where(second, top, lower)
        o_send[...] = jnp.where(second, lower, top)

    share = f32(nx, ny, lanes)
    keep, send, sums, totals = kernel_call(
        p,
        "update_two",
        second_body,
        (share, share, f32(16, 8, 128), f32(8, 128)),
        1,
        12,
        [pltpu.VMEM((p.xe, p.yw, lanes), F32)] + update_scratch(p),
        update_cost(p),
    )(where, tile, below, above, sums, across, ext, *weights)

    other = lax.ppermute(send, "gy", [(0, 1), (1, 0)])
    gathered = lax.all_to_all(sums, axes, 0, 0, tiled=True)

    def last_body(where_ref, keep_ref, other_ref, all_ref, totals_ref, o_new, o_pot, o_chem, o_stress):
        first = totals_ref[...]
        last = jnp.sum(all_ref[...], axis=0)
        mass = pick(first, 1)
        scale = mass / pick(last, 0)
        second = where_ref[0] == 1
        mine, theirs = keep_ref[...], other_ref[...]
        lower = jnp.where(second, theirs, mine)
        top = jnp.where(second, mine, theirs)
        lane = iota((nx, ny, nz), 2)
        o_pot[...] = jnp.where(lane < half, lower, pltpu.roll(top, half, 2))
        o_new[...] = jnp.where(lane < half, pltpu.roll(lower, half, 2), top) * scale[:ny]
        lane = iota((8, 128), 1)
        for step, total in enumerate((first, last)):
            chem = jnp.log(mass / pick(total, 0)) * (1.0 / TAU)
            o_chem[step] = chem[0, 0]
            for a in range(3):
                moments = pltpu.roll(total, 128 - 3 - 3 * a, 1)
                row = moments + jnp.where(lane == a, pick(total, 2), 0.0)
                o_stress[a, step : step + 1] = row[:1, :3] * (1.0 / cells)

    new, potential, chem, stress = kernel_call(
        p,
        "finish",
        last_body,
        (f32(nx, ny, nz), f32(nx, ny, nz), f32(STEPS), f32(3, STEPS, 3)),
        1,
        4,
    )(where, keep, other, gathered, totals)
    return new, potential, chem, jnp.transpose(stress, (1, 0, 2))


def on_device(density, external, w_first, w_second, w_third, w_last):
    mesh = tuple(lax.axis_size(axis) for axis in ("gx", "gy", "gz"))
    if mesh == (4, 2, 2) and density.shape == (8, 4, 128):
        return split_pairs(density, external, w_first, w_second, w_third, w_last)
    return any_mesh(density, external, w_first, w_second, w_third, w_last)


def solution(mesh):
    cells = P(("boxes", "gx"), "gy", "gz")
    return jax.shard_map(
        on_device,
        mesh=mesh,
        in_specs=(cells, cells, P(), P(), P(), P()),
        out_specs=(cells, cells, P("boxes"), P("boxes", None, None)),
        check_vma=False,
    )
```

```python
import functools

import jax
import jax.numpy as jnp
from jax import lax
from jax.experimental import pallas as pl
from jax.experimental.pallas import tpu as pltpu
from jax.sharding import PartitionSpec as P

STEPS = 2
C_TF = 2.871234
C_X = 0.7385588
TAU = 0.1
REACH = 6
STRIPS = 16
GROUP = 4
PAIRS = 8
SUMS = 16
BF = jnp.bfloat16
F32 = jnp.float32
VM = pl.BlockSpec(memory_space=pltpu.VMEM)
SM = pl.BlockSpec(memory_space=pltpu.SMEM)
HB = pl.BlockSpec(memory_space=pltpu.HBM)


def up(number, unit):
    return -(-number // unit) * unit


def iota(shape, dim):
    return lax.broadcasted_iota(jnp.int32, shape, dim)


def dot(a, b):
    return jnp.dot(a, b, preferred_element_type=F32)


def dot_tn(a, b):
    return lax.dot_general(a, b, (((0,), (0,)), ((), ())), preferred_element_type=F32)


def dot_nt(a, b):
    return lax.dot_general(a, b, (((1,), (1,)), ((), ())), preferred_element_type=F32)


class Plan:
    def __init__(self, xo, yw, own_y, ny, zo, ch, limit):
        self.xo, self.yw, self.own_y, self.ny, self.zo, self.ch = xo, yw, own_y, ny, zo, ch
        self.limit = limit << 20
        self.xe = xo + 2 * REACH
        self.ze = up(zo + 2 * REACH, STRIPS)
        self.zh = (self.ze - zo) // 2
        self.lo = self.ze // STRIPS
        self.zp = up(self.ze, 128)
        self.zq = up(zo, 128)
        self.lanes = yw * ch
        self.fields = 4 * yw
        self.narrow = up(GROUP * self.fields, 128)


PAIR_BLOCKS = (
    (0, 0, 0, 0),
    (0, 0, 1, 1),
    (1, 0, 1, 0),
    (1, 1, 0, 1),
    (2, 1, 0, 0),
    (2, 1, 1, 1),
)


def weights_kernel(p, dense_in, single_in, dense_out, first_out, last_out):
    ch, yw, lanes = p.ch, p.yw, p.lanes
    half, wide = yw // 2, lanes // 2

    for ref_in, ref_out in zip(dense_in, dense_out):
        taps = []
        for ty in range(3):
            taps.append(
                jnp.concatenate(
                    [ref_in[26 - (9 * (t // 3) + 3 * ty + t % 3)] for t in range(9)], axis=0
                )
            )
        taps = jnp.concatenate(taps, axis=1)
        row, column = iota((3 * ch, lanes), 0), iota((3 * ch, lanes), 1)
        ty = lax.div(row, ch)
        minus = column >= wide
        for yi in range(half):
            raw = yi + 1 - ty
            wraps = (raw < 0) | (raw >= half)
            yo = lax.rem(raw + half, half)
            target = row + (yo - ty) * ch
            match = jnp.where(minus, column - wide, column) == target
            value = jnp.where(wraps & minus, -0.5, 0.5)
            place = jnp.where(match, value, 0.0).astype(BF)
            spread = dot(taps, place).astype(BF).reshape(3, 3, ch, lanes)
            for sign in range(2):
                for tx, step, x_in, x_out in PAIR_BLOCKS:
                    begin = x_in * wide + yi * ch
                    ref_out[
                        sign, step, :, begin : begin + ch, x_out * wide : (x_out + 1) * wide
                    ] = spread[tx, :, :, sign * wide : (sign + 1) * wide]
        none = jnp.zeros((2, 3, wide, wide), BF)
        ref_out[:, 0, :, :wide, wide:] = none
        ref_out[:, 1, :, wide:, :wide] = none

    tile = (
        jnp.bitwise_and(iota((ch, lanes), 1), ch - 1) == iota((ch, lanes), 0)
    ).astype(F32).astype(BF)
    tiled = [dot(ref[...], tile).astype(BF) for ref in single_in]

    rows = 18 * yw
    row = iota((rows, 1), 0)
    yi = lax.rem(row, yw)
    tx = lax.rem(lax.div(row, yw), 3)
    tz = lax.rem(lax.div(row, 3 * yw), 3)
    yo = lax.div(iota((rows, lanes), 1), ch)
    for single, ref_out, direction in zip(tiled, first_out, (1, -1)):
        total = jnp.zeros((rows, lanes), F32)
        for ty in range(3):
            number = 9 * tx + 3 * ty + tz
            number = number if direction > 0 else 26 - number
            pick = (iota((rows, 27), 1) == number).astype(F32).astype(BF)
            here = lax.rem(yo + (ty - 1 + yw), yw) == yi
            total = total + jnp.where(here, dot(pick, single), 0.0)
        ref_out[...] = total.astype(BF)

    rows = p.narrow
    row = iota((rows, 1), 0)
    yo = lax.rem(row, yw)
    field = lax.rem(lax.div(row, yw), 4)
    tx = lax.div(row, 4 * yw)
    yi = lax.div(iota((rows, lanes), 1), ch)
    for single, ref_out, direction in zip(tiled[::-1], last_out, (1, -1)):
        for tz in range(3):
            total = jnp.zeros((rows, lanes), F32)
            for ty in range(3):
                number = 9 * tx + 3 * ty + tz
                number = number if direction > 0 else 26 - number
                if direction > 0:
                    factor = jnp.where(field == 0, 1, 0)
                else:
                    factor = jnp.where(
                        field == 0,
                        1,
                        jnp.where(field == 1, 1 - tx, jnp.where(field == 2, 1 - ty, 1 - tz)),
                    )
                factor = jnp.where(tx < 3, factor, 0).astype(F32)
                pick = (iota((rows, 27), 1) == number).astype(F32).astype(BF)
                here = lax.rem(yo + (ty - 1 + yw), yw) == yi
                total = total + jnp.where(here, dot(pick, single), 0.0) * factor
            ref_out[tz] = total.astype(BF)


def spread_weights(p, w_first, w_second, w_third, w_last):
    inputs = (w_second, w_third, w_first, w_last)

    def body(*refs):
        hbm, outs, held, sems = refs[:4], refs[4:10], refs[10:14], refs[14]
        copies = [pltpu.make_async_copy(hbm[i], held[i], sems.at[i]) for i in range(4)]
        for copy in copies:
            copy.start()
        for copy in copies:
            copy.wait()
        weights_kernel(p, held[:2], held[2:], outs[:2], outs[2:4], outs[4:])

    dense = jax.ShapeDtypeStruct((2, 2, 3, p.lanes, p.lanes), BF)
    single = jax.ShapeDtypeStruct((18 * p.yw, p.lanes), BF)
    narrow = jax.ShapeDtypeStruct((3, p.narrow, p.lanes), BF)
    flops = 2 * 2 * 9 * 3 * p.ch * p.lanes * p.lanes
    return pl.pallas_call(
        body,
        name="spread_weights",
        out_shape=(dense,) * 2 + (single,) * 2 + (narrow,) * 2,
        in_specs=[HB] * 4,
        out_specs=(VM,) * 6,
        scratch_shapes=[pltpu.VMEM(a.shape, a.dtype) for a in inputs]
        + [pltpu.SemaphoreType.DMA((4,))],
        compiler_params=pltpu.CompilerParams(vmem_limit_bytes=p.limit),
        cost_estimate=pl.CostEstimate(flops=flops, bytes_accessed=3 << 20, transcendentals=0),
    )(*[pltpu.with_memory_space_constraint(a, pltpu.HBM) for a in inputs])


def cube_root(value):
    guess = jnp.exp(jnp.log(value) * (1.0 / 3.0))
    return guess - (guess - value / (guess * guess)) * (1.0 / 3.0)


def store_edges(p, ref, place, value):
    tiles = value.reshape(p.lo, STRIPS, p.lanes)
    ref[place, 1 : p.lo + 1] = tiles.astype(BF)
    ref[place, 0] = pltpu.roll(tiles[p.lo - 1], 1, 0).astype(BF)
    ref[place, p.lo + 1] = pltpu.roll(tiles[0], STRIPS - 1, 0).astype(BF)


def blocks(total, size):
    return [(start, min(size, total - start)) for start in range(0, total, size)]


def store_pairs(p, ref, place, value):
    wide = p.lanes // 2
    first, second = value[:, :wide], value[:, wide:]
    pair, side = divmod(place, 2)
    lanes = slice(side * wide, (side + 1) * wide)
    for sign, part in enumerate((first + second, first - second)):
        tiles = part.reshape(p.lo, STRIPS, wide)
        ref[sign, pair, 1 : p.lo + 1, :, lanes] = tiles.astype(BF)
        ref[sign, pair, 0, :, lanes] = pltpu.roll(tiles[p.lo - 1], 1, 0).astype(BF)
        ref[sign, pair, p.lo + 1, :, lanes] = pltpu.roll(tiles[0], STRIPS - 1, 0).astype(BF)


def dense_planes(p, ref, w_ref, start, count, forward):
    halves = []
    for sign in range(2):
        total = None
        for step in range(2):
            for tz in range(3):
                rows = ref[sign, start + step : start + step + count, tz : tz + p.lo]
                rows = rows.reshape(count * p.ze, p.lanes)
                if forward:
                    part = dot_nt(rows, w_ref[sign, 1 - step, 2 - tz])
                else:
                    part = dot(rows, w_ref[sign, step, tz])
                total = part if total is None else total + part
        halves.append(total)
    wide = p.lanes // 2
    planes = []
    for k in range(2 * count):
        rows = slice(k // 2 * p.ze, (k // 2 + 1) * p.ze)
        lanes = slice(k % 2 * wide, (k % 2 + 1) * wide)
        plus, minus = halves[0][rows, lanes], halves[1][rows, lanes]
        planes.append(jnp.concatenate([plus + minus, plus - minus], axis=1))
    return planes


def gate(value):
    logistic = 0.5 * jnp.tanh(0.5 * value) + 0.5
    act = value * logistic
    return logistic, act


def slope_of(value, logistic, act):
    return logistic * (1.0 + value - act)


def to_planes(p, field, spread, planes_ref):
    high = field.astype(BF)
    low = (field - high.astype(F32)).astype(BF)
    flat = jnp.concatenate(
        [high.reshape(p.xe * p.yw, p.zp), low.reshape(p.xe * p.yw, p.zp)], axis=0
    )
    planes_ref[...] = dot(flat, spread).reshape(2, p.xe, p.yw, 3 * p.zp)


def single_plane(p, planes_ref, place, w_ref):
    pieces = []
    for half in range(2):
        for tz in range(3):
            piece = planes_ref[half, place : place + 3, :, tz * p.zp : tz * p.zp + p.ze]
            pieces.append(piece.reshape(3 * p.yw, p.ze))
    window = jnp.concatenate(pieces, axis=0).astype(BF)
    return dot_tn(window, w_ref[...])


def narrow_fold(p, ref, w_ref, planes_ref, back):
    for start, count in blocks(p.xo + 2, 5):
        total = None
        for tz in range(3):
            rows = ref[start : start + count, tz : tz + p.lo].reshape(count * p.ze, p.lanes)
            part = dot_nt(rows, w_ref[tz])
            total = part if total is None else total + part
        planes_ref[start : start + count] = total.reshape(count, p.ze, p.narrow)
    lane = lax.div(iota((p.ze, p.narrow), 1), p.fields)
    fields = []
    for first in range(0, p.xo, GROUP):
        joined = jnp.zeros((p.ze, p.narrow), F32)
        for k in range(GROUP):
            total = None
            for tx in range(3):
                part = planes_ref[first + k + tx]
                shift = (k - tx) * p.fields % p.narrow
                part = pltpu.roll(part, shift, 1) if shift else part
                total = part if total is None else total + part
            joined = jnp.where(lane == k, total, joined)
        high = joined.astype(BF)
        rest = joined - high.astype(F32)
        mid = rest.astype(BF)
        low = (rest - mid.astype(F32)).astype(BF)
        parts = jnp.concatenate([high, mid, low], axis=0)
        natural = dot_tn(parts, back)[: GROUP * p.fields]
        fields.append(natural.reshape(GROUP, 4, p.yw, p.zq))
    return jnp.concatenate(fields, axis=0)


def update_kernel(p, current, external, weights, scratch):
    w_two, w_three, w_one, w_source, w_enhance, w_lever = weights
    planes, act_a, act_b, act_c, slope_one, slope_two, narrow = scratch

    current = jnp.where(iota(current.shape, 2) < p.ze, current, 1.0)
    cube = cube_root(current)
    source = current * cube * cube

    shape = (p.zp, 3 * p.zp)
    lane = iota(shape, 1)
    tz = lax.div(lane, p.zp)
    row = lane - tz * p.zp
    cell = p.lo * jnp.bitwise_and(row, STRIPS - 1) + lax.div(row, STRIPS) + tz - 1
    spread = jnp.where((cell == iota(shape, 0)) & (row < p.ze), 1.0, 0.0).astype(BF)
    shape = (3 * p.ze, p.zq)
    row = lax.rem(iota(shape, 0), p.ze)
    cell = p.lo * jnp.bitwise_and(row, STRIPS - 1) + lax.div(row, STRIPS) - p.zh
    back = jnp.where((cell == iota(shape, 1)) & (cell < p.zo), 1.0, 0.0).astype(BF)

    to_planes(p, cube, spread, planes)
    for x in range(p.xo + 10):
        value = single_plane(p, planes, x, w_one)
        logistic, act = gate(value)
        store_pairs(p, act_a, x, act)
        if 4 <= x < p.xo + 6:
            slope_one[x - 4] = slope_of(value, logistic, act)

    for start, count in blocks((p.xo + 8) // 2, PAIRS):
        for k, value in enumerate(dense_planes(p, act_a, w_two, start, count, True)):
            x = 2 * start + k
            logistic, act = gate(value)
            store_pairs(p, act_b, x, act)
            if 2 <= x < p.xo + 6:
                slope_two[x - 2] = slope_of(value, logistic, act)

    to_planes(p, source, spread, planes)
    for start, count in blocks((p.xo + 6) // 2, PAIRS):
        for k, value in enumerate(dense_planes(p, act_b, w_three, start, count, True)):
            x = 2 * start + k
            logistic, act = gate(value)
            if 2 <= x < p.xo + 4:
                store_edges(p, act_c, x - 2, act)
            slope = slope_of(value, logistic, act)
            store_pairs(p, act_a, x, single_plane(p, planes, x + 2, w_source) * slope)

    enhance = narrow_fold(p, act_c, w_enhance, narrow, back)[:, 0]

    for start, count in blocks((p.xo + 4) // 2, PAIRS):
        for k, value in enumerate(dense_planes(p, act_a, w_three, start, count, False)):
            store_pairs(p, act_b, 2 * start + k, value * slope_two[2 * start + k])

    for start, count in blocks((p.xo + 2) // 2, PAIRS):
        for k, value in enumerate(dense_planes(p, act_b, w_two, start, count, False)):
            store_edges(p, act_c, 2 * start + k, value * slope_one[2 * start + k])

    levers = narrow_fold(p, act_c, w_lever, narrow, back)

    def natural(field, step):
        return pltpu.roll(field, (p.zp - p.zh - step) % p.zp, 2)[:, :, : p.zq]

    inner = cube[REACH : REACH + p.xo]
    here = natural(inner, 0)
    density = natural(current[REACH : REACH + p.xo], 0)
    source_here = natural(source[REACH : REACH + p.xo], 0)
    squared = here * here
    potential = (
        5.0 / 3.0 * squared * (C_TF + enhance)
        + levers[:, 0] / (3.0 * squared)
        + external
        - 4.0 / 3.0 * C_X * here
    )
    slopes = [
        natural(cube[REACH + 1 : REACH + 1 + p.xo], 0) - natural(cube[REACH - 1 : REACH - 1 + p.xo], 0),
        pltpu.roll(here, p.yw - 1, 1) - pltpu.roll(here, 1, 1),
        natural(inner, 1) - natural(inner, -1),
    ]
    weighted = density * jnp.exp(-TAU * potential)
    energy = source_here * (C_TF + enhance) + external * density - C_X * density * here
    terms = [weighted, density, energy - density * potential]
    for slope in slopes:
        for axis in range(3):
            terms.append(0.5 * slope * levers[:, 1 + axis])
    lane = iota((p.yw, p.zq), 1)
    y = iota((p.yw, p.zq), 0)
    own = (lane < p.zo) & (y >= p.own_y) & (y < p.own_y + p.ny)
    rows = []
    for term in terms:
        rows.append(jnp.sum(jnp.where(own, jnp.sum(term, axis=0), 0.0), axis=0, keepdims=True))
    rows.append(jnp.zeros((SUMS - len(rows), p.zq), F32))
    sums = jnp.sum(jnp.concatenate(rows, axis=0), axis=1, keepdims=True)
    onto = iota((SUMS, 128), 0) == iota((SUMS, 128), 1)
    row = jnp.sum(jnp.where(onto, sums, 0.0), axis=0, keepdims=True)
    return potential, weighted, jnp.broadcast_to(row, (8, 128))


def pick(row, number):
    return jnp.sum(jnp.where(iota(row.shape, 1) == number, row, 0.0), axis=1, keepdims=True)


def update_scratch(p):
    def pairs(planes):
        return pltpu.VMEM((2, planes // 2, p.lo + 2, STRIPS, p.lanes), BF)

    return [
        pltpu.VMEM((2, p.xe, p.yw, 3 * p.zp), F32),
        pairs(p.xo + 10),
        pairs(p.xo + 8),
        pltpu.VMEM((p.xo + 2, p.lo + 2, STRIPS, p.lanes), BF),
        pltpu.VMEM((p.xo + 2, p.ze, p.lanes), F32),
        pltpu.VMEM((p.xo + 4, p.ze, p.lanes), F32),
        pltpu.VMEM((p.xo + 2, p.ze, p.narrow), F32),
    ]


def update_cost(p):
    flops = 2 * 6 * p.lanes * p.lanes * p.ze * (4 * p.xo + 20)
    return pl.CostEstimate(flops=flops, bytes_accessed=6 << 20, transcendentals=0)


def kernel_call(p, name, body, out_shape, n_smem, n_vmem, scratch=(), cost=None, n_hbm=0):
    return pl.pallas_call(
        body,
        name=name,
        out_shape=out_shape,
        in_specs=[SM] * n_smem + [HB] * n_hbm + [VM] * n_vmem,
        out_specs=tuple(SM if len(shape.shape) == 1 else VM for shape in out_shape),
        scratch_shapes=list(scratch),
        compiler_params=pltpu.CompilerParams(vmem_limit_bytes=p.limit),
        cost_estimate=cost,
    )


def f32(*shape):
    return jax.ShapeDtypeStruct(shape, F32)


def widen(cells, axis, dim, before, after):
    size = cells.shape[dim]
    count = lax.axis_size(axis)

    def fetch(step, start, stop):
        piece = lax.slice_in_dim(cells, start, stop, axis=dim)
        if step % count == 0:
            return piece
        return lax.ppermute(piece, axis, [(i, (i + step) % count) for i in range(count)])

    pieces = [cells]
    left = before
    step = 1
    while left > 0:
        take = min(left, size)
        pieces.insert(0, fetch(step, size - take, size))
        left -= take
        step += 1
    left = after
    step = 1
    while left > 0:
        take = min(left, size)
        pieces.append(fetch(-step, 0, take))
        left -= take
        step += 1
    return jnp.concatenate(pieces, axis=dim)


def any_mesh(density, external, w_first, w_second, w_third, w_last):
    nx, ny, nz = density.shape
    ch = w_first.shape[1]
    yw = up(ny + 2 * REACH, 8)
    own_y = (yw - ny) // 2
    xo = up(nx, GROUP)
    p = Plan(xo, yw, own_y, ny, nz, ch, 60)
    weights = spread_weights(p, w_first, w_second, w_third, w_last)
    axes = ("gx", "gy", "gz")
    count = nx * ny * nz * lax.axis_size("gx") * lax.axis_size("gy") * lax.axis_size("gz")
    total_mass = lax.psum(jnp.sum(density), axes)

    def body(cur, ext, *refs):
        weight_refs, (o_pot, o_weighted, o_sums), scratch = refs[:6], refs[6:9], refs[9:]
        pot, weighted, sums = update_kernel(p, cur[...], ext[...], weight_refs, scratch)
        o_pot[...] = pot
        o_weighted[...] = weighted
        o_sums[...] = sums

    call = kernel_call(
        p,
        "update",
        body,
        (f32(xo, yw, p.zq), f32(xo, yw, p.zq), f32(8, 128)),
        0,
        8,
        update_scratch(p),
        update_cost(p),
    )
    ext = jnp.pad(
        external, ((0, xo - nx), (own_y, yw - ny - own_y), (0, p.zq - nz))
    )
    current = density
    chem, stress = [], []
    for _ in range(STEPS):
        tile = widen(current, "gz", 2, p.zh, p.ze - nz - p.zh)
        tile = widen(tile, "gy", 1, own_y, yw - ny - own_y)
        tile = widen(tile, "gx", 0, REACH, REACH)
        tile = jnp.pad(tile, ((0, 0), (0, 0), (0, p.zp - p.ze)), constant_values=1.0)
        pot, weighted, sums = call(tile, ext, *weights)
        totals = lax.psum(sums[0, :SUMS], axes)
        chem.append(jnp.log(total_mass / totals[0]) / TAU)
        moments = totals[3:12].reshape(3, 3)
        stress.append((moments + jnp.eye(3, dtype=F32) * totals[2]) / count)
        current = weighted[:nx, own_y : own_y + ny, :nz] * (total_mass / totals[0])
        potential = pot[:nx, own_y : own_y + ny, :nz]
    return current, potential, jnp.stack(chem), jnp.stack(stress)


def split_pairs(density, external, w_first, w_second, w_third, w_last):
    nx, ny, nz = density.shape
    ch = w_first.shape[1]
    half = nz // 2
    p = Plan(nx, 2 * ny, 0, 2 * ny, half, ch, 20)
    lanes = p.zp
    cells = nx * ny * nz * 16
    axes = ("gx", "gy", "gz")

    def along_x(cells_out, step):
        return lax.ppermute(cells_out, "gx", [(i, (i + step) % 4) for i in range(4)])

    def quarter(number):
        return (number % 2) * 2 + number // 2

    def along_z(cells_out, step):
        pairs = [(quarter(q), quarter((q + step) % 4)) for q in range(4)]
        return lax.ppermute(cells_out, ("gy", "gz"), pairs)

    weights = spread_weights(p, w_first, w_second, w_third, w_last)

    def widen_body(own_hbm, ext_hbm, left_ref, right_ref, o_wide, sems):
        copies = [
            pltpu.make_async_copy(own_hbm, o_wide.at[REACH : REACH + nx], sems.at[0]),
            pltpu.make_async_copy(ext_hbm, o_wide.at[p.xe :], sems.at[1]),
        ]
        for copy in copies:
            copy.start()
        o_wide[:REACH] = left_ref[nx - REACH :]
        o_wide[REACH + nx : p.xe] = right_ref[:REACH]
        for copy in copies:
            copy.wait()

    (wide,) = kernel_call(
        p,
        "widen",
        widen_body,
        (f32(p.xe + nx, ny, nz),),
        0,
        2,
        [pltpu.SemaphoreType.DMA((2,))],
        n_hbm=2,
    )(
        *[pltpu.with_memory_space_constraint(a, pltpu.HBM) for a in (density, external)],
        along_x(density, 1),
        along_x(density, -1),
    )
    from_y = lax.ppermute(wide, "gy", [(0, 1), (1, 0)])
    from_z = lax.ppermute(wide, "gz", [(0, 1), (1, 0)])
    from_yz = lax.ppermute(wide, ("gy", "gz"), [(i, 3 - i) for i in range(4)])
    planes = p.xe + nx

    def first_body(own, y, z, yz, *refs):
        weight_refs, outs, tile, scratch = refs[:6], refs[6:11], refs[11], refs[12:]
        second = lax.axis_index("gy") == 1
        shift = jnp.where(second, nz - half + p.zh, p.zh)
        lane = iota((planes, p.yw, lanes), 2)
        for ref, other in ((own, y), (z, yz)):
            mine, theirs = ref[...], other[...]
            lower = jnp.where(second, theirs, mine)
            upper = jnp.where(second, mine, theirs)
            cells_here = jnp.concatenate([lower, upper], axis=1)
            moved = pltpu.roll(cells_here, shift, 2)
            if ref is own:
                tile[...] = moved
            else:
                begin = jnp.where(second, half + p.zh, 0)
                end = jnp.where(second, lanes, p.zh)
                tile[...] = jnp.where((lane >= begin) & (lane < end), moved, tile[...])
        cur = tile[: p.xe]
        ext = pltpu.roll(tile[p.xe :], lanes - p.zh, 2)
        _, weighted, sums = update_kernel(p, cur, ext, weight_refs, scratch)
        o_own, o_low, o_high, o_ext, o_sums = outs
        o_own[...] = weighted
        o_low[:REACH] = weighted[:REACH]
        o_low[REACH] = sums
        o_high[:REACH] = weighted[nx - REACH :]
        o_high[REACH] = sums
        o_ext[...] = ext
        o_sums[...] = sums

    message = f32(REACH + 1, p.yw, lanes)
    own, low, high, ext, sums = kernel_call(
        p,
        "update_one",
        first_body,
        (f32(nx, p.yw, lanes), message, message, f32(nx, p.yw, lanes), f32(8, 128)),
        0,
        10,
        [pltpu.VMEM((planes, p.yw, lanes), F32)] + update_scratch(p),
        update_cost(p),
    )(wide, from_y, from_z, from_yz, *weights)

    left = along_x(high, 1)
    right = along_x(low, -1)
    far = along_x(sums, 2)

    packs = up(p.xe, 8) // 8

    def join_body(own_ref, sums_ref, left_ref, right_ref, far_ref, o_tile, o_down, o_up, o_sums):
        tile = jnp.concatenate([left_ref[:REACH], own_ref[...], right_ref[:REACH]], axis=0)
        sums = sums_ref[...] + left_ref[REACH] + right_ref[REACH] + far_ref[...]
        o_tile[...] = tile
        o_sums[...] = sums
        lane = lax.div(iota((p.yw, lanes), 1), p.zh)
        for ref, start in ((o_down, 0), (o_up, half - p.zh)):
            for pack in range(packs):
                joined = jnp.zeros((p.yw, lanes), F32)
                for k in range(min(8, p.xe - 8 * pack)):
                    moved = pltpu.roll(tile[8 * pack + k], (k * p.zh - start) % lanes, 1)
                    joined = jnp.where(lane == k, moved, joined)
                ref[pack] = joined
            ref[packs] = sums

    edge = f32(packs + 1, p.yw, lanes)
    tile, down, upper, sums = kernel_call(
        p,
        "join",
        join_body,
        (f32(p.xe, p.yw, lanes), edge, edge, f32(8, 128)),
        0,
        5,
    )(own, sums, left, right, far)
    below = along_z(upper, 1)
    above = along_z(down, -1)
    across = lax.ppermute(sums, "gz", [(0, 1), (1, 0)])

    def second_body(tile_ref, below_ref, above_ref, sums_ref, across_ref, ext_ref, *refs):
        weight_refs, outs, cur, scratch = refs[:6], refs[6:10], refs[10], refs[11:]
        o_keep, o_send, o_sums, o_totals = outs
        totals = sums_ref[...] + across_ref[...] + below_ref[packs] + above_ref[packs]
        o_totals[...] = totals
        scale = pick(totals, 1) / pick(totals, 0)
        lane = iota((p.yw, lanes), 1)
        for x in range(p.xe):
            pack, k = divmod(x, 8)
            lower = pltpu.roll(below_ref[pack], -k * p.zh % lanes, 1)
            top = pltpu.roll(above_ref[pack], (p.zh + half - k * p.zh) % lanes, 1)
            middle = pltpu.roll(tile_ref[x], p.zh, 1)
            joined = jnp.where(lane < p.zh, lower, jnp.where(lane < p.zh + half, middle, top))
            cur[x] = joined * scale
        pot, weighted, sums_here = update_kernel(p, cur[...], ext_ref[...], weight_refs, scratch)
        o_sums[...] = jnp.broadcast_to(sums_here, (16, 8, 128))
        both = jnp.where(
            iota(pot.shape, 2) < half, pot, pltpu.roll(weighted, half, 2)
        )
        second = lax.axis_index("gy") == 1
        lower, top = both[:, :ny], both[:, ny:]
        o_keep[...] = jnp.where(second, top, lower)
        o_send[...] = jnp.where(second, lower, top)

    share = f32(nx, ny, lanes)
    keep, send, sums, totals = kernel_call(
        p,
        "update_two",
        second_body,
        (share, share, f32(16, 8, 128), f32(8, 128)),
        0,
        12,
        [pltpu.VMEM((p.xe, p.yw, lanes), F32)] + update_scratch(p),
        update_cost(p),
    )(tile, below, above, sums, across, ext, *weights)

    other = lax.ppermute(send, "gy", [(0, 1), (1, 0)])
    gathered = lax.all_to_all(sums, axes, 0, 0, tiled=True)

    def last_body(keep_ref, other_ref, all_ref, totals_ref, o_new, o_pot, o_chem, o_stress):
        first = totals_ref[...]
        last = jnp.sum(all_ref[...], axis=0)
        mass = pick(first, 1)
        scale = mass / pick(last, 0)
        second = lax.axis_index("gy") == 1
        mine, theirs = keep_ref[...], other_ref[...]
        lower = jnp.where(second, theirs, mine)
        top = jnp.where(second, mine, theirs)
        lane = iota((nx, ny, nz), 2)
        o_pot[...] = jnp.where(lane < half, lower, pltpu.roll(top, half, 2))
        o_new[...] = jnp.where(lane < half, pltpu.roll(lower, half, 2), top) * scale[:ny]
        lane = iota((8, 128), 1)
        for step, total in enumerate((first, last)):
            chem = jnp.log(mass / pick(total, 0)) * (1.0 / TAU)
            o_chem[step] = chem[0, 0]
            for a in range(3):
                moments = pltpu.roll(total, 128 - 3 - 3 * a, 1)
                row = moments + jnp.where(lane == a, pick(total, 2), 0.0)
                o_stress[a, step : step + 1] = row[:1, :3] * (1.0 / cells)

    new, potential, chem, stress = kernel_call(
        p,
        "finish",
        last_body,
        (f32(nx, ny, nz), f32(nx, ny, nz), f32(STEPS), f32(3, STEPS, 3)),
        0,
        4,
    )(keep, other, gathered, totals)
    return new, potential, chem, jnp.transpose(stress, (1, 0, 2))


def on_device(density, external, w_first, w_second, w_third, w_last):
    mesh = tuple(lax.axis_size(axis) for axis in ("gx", "gy", "gz"))
    if mesh == (4, 2, 2) and density.shape == (8, 4, 128):
        return split_pairs(density, external, w_first, w_second, w_third, w_last)
    return any_mesh(density, external, w_first, w_second, w_third, w_last)


def solution(mesh):
    cells = P(("boxes", "gx"), "gy", "gz")
    return jax.shard_map(
        on_device,
        mesh=mesh,
        in_specs=(cells, cells, P(), P(), P(), P()),
        out_specs=(cells, cells, P("boxes"), P("boxes", None, None)),
        check_vma=False,
    )
```

```python
import functools

import jax
import jax.numpy as jnp
from jax import lax
from jax.experimental import pallas as pl
from jax.experimental.pallas import tpu as pltpu
from jax.sharding import PartitionSpec as P

STEPS = 2
C_TF = 2.871234
C_X = 0.7385588
TAU = 0.1
REACH = 6
STRIPS = 16
GROUP = 4
PAIRS = 8
SUMS = 16
BF = jnp.bfloat16
F32 = jnp.float32
VM = pl.BlockSpec(memory_space=pltpu.VMEM)
SM = pl.BlockSpec(memory_space=pltpu.SMEM)
HB = pl.BlockSpec(memory_space=pltpu.HBM)


def up(number, unit):
    return -(-number // unit) * unit


def iota(shape, dim):
    return lax.broadcasted_iota(jnp.int32, shape, dim)


def dot(a, b):
    return jnp.dot(a, b, preferred_element_type=F32)


def dot_tn(a, b):
    return lax.dot_general(a, b, (((0,), (0,)), ((), ())), preferred_element_type=F32)


def dot_nt(a, b):
    return lax.dot_general(a, b, (((1,), (1,)), ((), ())), preferred_element_type=F32)


class Plan:
    def __init__(self, xo, yw, own_y, ny, zo, ch, limit):
        self.xo, self.yw, self.own_y, self.ny, self.zo, self.ch = xo, yw, own_y, ny, zo, ch
        self.limit = limit << 20
        self.xe = xo + 2 * REACH
        self.ze = up(zo + 2 * REACH, STRIPS)
        self.zh = (self.ze - zo) // 2
        self.lo = self.ze // STRIPS
        self.zp = up(self.ze, 128)
        self.zq = up(zo, 128)
        self.lanes = yw * ch
        self.fields = 4 * yw
        self.narrow = up(GROUP * self.fields, 128)


PAIR_BLOCKS = (
    (0, 0, 0, 0),
    (0, 0, 1, 1),
    (1, 0, 1, 0),
    (1, 1, 0, 1),
    (2, 1, 0, 0),
    (2, 1, 1, 1),
)


def weights_kernel(p, dense_in, single_in, dense_out, first_out, last_out):
    ch, yw, lanes = p.ch, p.yw, p.lanes
    half, wide = yw // 2, lanes // 2

    for ref_in, ref_out in zip(dense_in, dense_out):
        taps = []
        for ty in range(3):
            taps.append(
                jnp.concatenate(
                    [ref_in[26 - (9 * (t // 3) + 3 * ty + t % 3)] for t in range(9)], axis=0
                )
            )
        taps = jnp.concatenate(taps, axis=1)
        row, column = iota((3 * ch, lanes), 0), iota((3 * ch, lanes), 1)
        ty = lax.div(row, ch)
        minus = column >= wide
        for yi in range(half):
            raw = yi + 1 - ty
            wraps = (raw < 0) | (raw >= half)
            yo = lax.rem(raw + half, half)
            target = row + (yo - ty) * ch
            match = jnp.where(minus, column - wide, column) == target
            value = jnp.where(wraps & minus, -0.25, 0.25)
            place = jnp.where(match, value, 0.0).astype(BF)
            spread = dot(taps, place).astype(BF).reshape(3, 3, ch, lanes)
            for sign in range(2):
                for tx, step, x_in, x_out in PAIR_BLOCKS:
                    begin = x_in * wide + yi * ch
                    ref_out[
                        sign, step, :, begin : begin + ch, x_out * wide : (x_out + 1) * wide
                    ] = spread[tx, :, :, sign * wide : (sign + 1) * wide]
        none = jnp.zeros((2, 3, wide, wide), BF)
        ref_out[:, 0, :, :wide, wide:] = none
        ref_out[:, 1, :, wide:, :wide] = none

    tile = (
        jnp.bitwise_and(iota((ch, lanes), 1), ch - 1) == iota((ch, lanes), 0)
    ).astype(F32).astype(BF)
    tiled = [dot(ref[...], tile).astype(BF) for ref in single_in]

    rows = 18 * yw
    row = iota((rows, 1), 0)
    yi = lax.rem(row, yw)
    tx = lax.rem(lax.div(row, yw), 3)
    tz = lax.rem(lax.div(row, 3 * yw), 3)
    yo = lax.div(iota((rows, lanes), 1), ch)
    for single, ref_out, direction in zip(tiled, first_out, (1, -1)):
        total = jnp.zeros((rows, lanes), F32)
        for ty in range(3):
            number = 9 * tx + 3 * ty + tz
            number = number if direction > 0 else 26 - number
            pick = (iota((rows, 27), 1) == number).astype(F32).astype(BF)
            here = lax.rem(yo + (ty - 1 + yw), yw) == yi
            total = total + jnp.where(here, dot(pick, single), 0.0)
        ref_out[...] = (0.5 * total).astype(BF)

    rows = p.narrow
    row = iota((rows, 1), 0)
    yo = lax.rem(row, yw)
    field = lax.rem(lax.div(row, yw), 4)
    tx = lax.div(row, 4 * yw)
    yi = lax.div(iota((rows, lanes), 1), ch)
    for single, ref_out, direction in zip(tiled[::-1], last_out, (1, -1)):
        for tz in range(3):
            total = jnp.zeros((rows, lanes), F32)
            for ty in range(3):
                number = 9 * tx + 3 * ty + tz
                number = number if direction > 0 else 26 - number
                if direction > 0:
                    factor = jnp.where(field == 0, 1, 0)
                else:
                    factor = jnp.where(
                        field == 0,
                        1,
                        jnp.where(field == 1, 1 - tx, jnp.where(field == 2, 1 - ty, 1 - tz)),
                    )
                factor = jnp.where(tx < 3, factor, 0).astype(F32)
                pick = (iota((rows, 27), 1) == number).astype(F32).astype(BF)
                here = lax.rem(yo + (ty - 1 + yw), yw) == yi
                total = total + jnp.where(here, dot(pick, single), 0.0) * factor
            ref_out[tz] = total.astype(BF)


def spread_weights(p, w_first, w_second, w_third, w_last):
    inputs = (w_second, w_third, w_first, w_last)

    def body(*refs):
        hbm, outs, held, sems = refs[:4], refs[4:10], refs[10:14], refs[14]
        copies = [pltpu.make_async_copy(hbm[i], held[i], sems.at[i]) for i in range(4)]
        for copy in copies:
            copy.start()
        for copy in copies:
            copy.wait()
        weights_kernel(p, held[:2], held[2:], outs[:2], outs[2:4], outs[4:])

    dense = jax.ShapeDtypeStruct((2, 2, 3, p.lanes, p.lanes), BF)
    single = jax.ShapeDtypeStruct((18 * p.yw, p.lanes), BF)
    narrow = jax.ShapeDtypeStruct((3, p.narrow, p.lanes), BF)
    flops = 2 * 2 * 9 * 3 * p.ch * p.lanes * p.lanes
    return pl.pallas_call(
        body,
        name="spread_weights",
        out_shape=(dense,) * 2 + (single,) * 2 + (narrow,) * 2,
        in_specs=[HB] * 4,
        out_specs=(VM,) * 6,
        scratch_shapes=[pltpu.VMEM(a.shape, a.dtype) for a in inputs]
        + [pltpu.SemaphoreType.DMA((4,))],
        compiler_params=pltpu.CompilerParams(vmem_limit_bytes=p.limit),
        cost_estimate=pl.CostEstimate(flops=flops, bytes_accessed=3 << 20, transcendentals=0),
    )(*[pltpu.with_memory_space_constraint(a, pltpu.HBM) for a in inputs])


def cube_root(value):
    guess = jnp.exp(jnp.log(value) * (1.0 / 3.0))
    return guess - (guess - value / (guess * guess)) * (1.0 / 3.0)


def store_edges(p, ref, place, value):
    tiles = value.reshape(p.lo, STRIPS, p.lanes)
    ref[place, 1 : p.lo + 1] = tiles.astype(BF)
    ref[place, 0] = pltpu.roll(tiles[p.lo - 1], 1, 0).astype(BF)
    ref[place, p.lo + 1] = pltpu.roll(tiles[0], STRIPS - 1, 0).astype(BF)


def blocks(total, size):
    return [(start, min(size, total - start)) for start in range(0, total, size)]


def store_pairs(p, ref, place, value):
    wide = p.lanes // 2
    first, second = value[:, :wide], value[:, wide:]
    pair, side = divmod(place, 2)
    lanes = slice(side * wide, (side + 1) * wide)
    for sign, part in enumerate((first + second, first - second)):
        tiles = part.reshape(p.lo, STRIPS, wide)
        ref[sign, pair, 1 : p.lo + 1, :, lanes] = tiles.astype(BF)
        ref[sign, pair, 0, :, lanes] = pltpu.roll(tiles[p.lo - 1], 1, 0).astype(BF)
        ref[sign, pair, p.lo + 1, :, lanes] = pltpu.roll(tiles[0], STRIPS - 1, 0).astype(BF)


def dense_planes(p, ref, w_ref, start, count, forward):
    halves = []
    for sign in range(2):
        total = None
        for step in range(2):
            for tz in range(3):
                rows = ref[sign, start + step : start + step + count, tz : tz + p.lo]
                rows = rows.reshape(count * p.ze, p.lanes)
                if forward:
                    part = dot_nt(rows, w_ref[sign, 1 - step, 2 - tz])
                else:
                    part = dot(rows, w_ref[sign, step, tz])
                total = part if total is None else total + part
        halves.append(total)
    wide = p.lanes // 2
    planes = []
    for k in range(2 * count):
        rows = slice(k // 2 * p.ze, (k // 2 + 1) * p.ze)
        lanes = slice(k % 2 * wide, (k % 2 + 1) * wide)
        plus, minus = halves[0][rows, lanes], halves[1][rows, lanes]
        planes.append(jnp.concatenate([plus + minus, plus - minus], axis=1))
    return planes


def gate(value, slope=True):
    wave = jnp.tanh(value)
    product = value * wave
    act = value + product
    if not slope:
        return act, None
    rise = 1.0 + wave
    return act, rise + rise * (value - product)


def to_planes(p, field, spread, planes_ref):
    high = field.astype(BF)
    low = (field - high.astype(F32)).astype(BF)
    flat = jnp.concatenate(
        [high.reshape(p.xe * p.yw, p.zp), low.reshape(p.xe * p.yw, p.zp)], axis=0
    )
    planes_ref[...] = dot(flat, spread).reshape(2, p.xe, p.yw, 3 * p.zp)


def single_plane(p, planes_ref, place, w_ref):
    pieces = []
    for half in range(2):
        for tz in range(3):
            piece = planes_ref[half, place : place + 3, :, tz * p.zp : tz * p.zp + p.ze]
            pieces.append(piece.reshape(3 * p.yw, p.ze))
    window = jnp.concatenate(pieces, axis=0).astype(BF)
    return dot_tn(window, w_ref[...])


def narrow_fold(p, ref, w_ref, planes_ref, back):
    for start, count in blocks(p.xo + 2, 5):
        total = None
        for tz in range(3):
            rows = ref[start : start + count, tz : tz + p.lo].reshape(count * p.ze, p.lanes)
            part = dot_nt(rows, w_ref[tz])
            total = part if total is None else total + part
        planes_ref[start : start + count] = total.reshape(count, p.ze, p.narrow)
    lane = lax.div(iota((p.ze, p.narrow), 1), p.fields)
    fields = []
    for first in range(0, p.xo, GROUP):
        joined = jnp.zeros((p.ze, p.narrow), F32)
        for k in range(GROUP):
            total = None
            for tx in range(3):
                part = planes_ref[first + k + tx]
                shift = (k - tx) * p.fields % p.narrow
                part = pltpu.roll(part, shift, 1) if shift else part
                total = part if total is None else total + part
            joined = jnp.where(lane == k, total, joined)
        high = joined.astype(BF)
        rest = joined - high.astype(F32)
        mid = rest.astype(BF)
        low = (rest - mid.astype(F32)).astype(BF)
        parts = jnp.concatenate([high, mid, low], axis=0)
        natural = dot_tn(parts, back)[: GROUP * p.fields]
        fields.append(natural.reshape(GROUP, 4, p.yw, p.zq))
    return jnp.concatenate(fields, axis=0)


def update_kernel(p, current, external, weights, scratch):
    w_two, w_three, w_one, w_source, w_enhance, w_lever = weights
    planes, act_a, act_b, act_c, slope_one, slope_two, narrow = scratch

    current = jnp.where(iota(current.shape, 2) < p.ze, current, 1.0)
    cube = cube_root(current)
    source = current * cube * cube

    shape = (p.zp, 3 * p.zp)
    lane = iota(shape, 1)
    tz = lax.div(lane, p.zp)
    row = lane - tz * p.zp
    cell = p.lo * jnp.bitwise_and(row, STRIPS - 1) + lax.div(row, STRIPS) + tz - 1
    spread = jnp.where((cell == iota(shape, 0)) & (row < p.ze), 1.0, 0.0).astype(BF)
    shape = (3 * p.ze, p.zq)
    row = lax.rem(iota(shape, 0), p.ze)
    cell = p.lo * jnp.bitwise_and(row, STRIPS - 1) + lax.div(row, STRIPS) - p.zh
    back = jnp.where((cell == iota(shape, 1)) & (cell < p.zo), 1.0, 0.0).astype(BF)

    to_planes(p, cube, spread, planes)
    for x in range(p.xo + 10):
        value = single_plane(p, planes, x, w_one)
        inside = 4 <= x < p.xo + 6
        act, slope = gate(value, inside)
        store_pairs(p, act_a, x, act)
        if inside:
            slope_one[x - 4] = slope

    for start, count in blocks((p.xo + 8) // 2, PAIRS):
        for k, value in enumerate(dense_planes(p, act_a, w_two, start, count, True)):
            x = 2 * start + k
            inside = 2 <= x < p.xo + 6
            act, slope = gate(value, inside)
            store_pairs(p, act_b, x, act)
            if inside:
                slope_two[x - 2] = slope

    to_planes(p, source, spread, planes)
    for start, count in blocks((p.xo + 6) // 2, PAIRS):
        for k, value in enumerate(dense_planes(p, act_b, w_three, start, count, True)):
            x = 2 * start + k
            act, slope = gate(value)
            if 2 <= x < p.xo + 4:
                store_edges(p, act_c, x - 2, act)
            store_pairs(p, act_a, x, single_plane(p, planes, x + 2, w_source) * slope)

    enhance = narrow_fold(p, act_c, w_enhance, narrow, back)[:, 0]

    for start, count in blocks((p.xo + 4) // 2, PAIRS):
        for k, value in enumerate(dense_planes(p, act_a, w_three, start, count, False)):
            store_pairs(p, act_b, 2 * start + k, value * slope_two[2 * start + k])

    for start, count in blocks((p.xo + 2) // 2, PAIRS):
        for k, value in enumerate(dense_planes(p, act_b, w_two, start, count, False)):
            store_edges(p, act_c, 2 * start + k, value * slope_one[2 * start + k])

    levers = narrow_fold(p, act_c, w_lever, narrow, back)

    def natural(field, step):
        return pltpu.roll(field, (p.zp - p.zh - step) % p.zp, 2)[:, :, : p.zq]

    inner = cube[REACH : REACH + p.xo]
    here = natural(inner, 0)
    density = natural(current[REACH : REACH + p.xo], 0)
    source_here = natural(source[REACH : REACH + p.xo], 0)
    squared = here * here
    potential = (
        5.0 / 3.0 * squared * (C_TF + enhance)
        + levers[:, 0] / (3.0 * squared)
        + external
        - 4.0 / 3.0 * C_X * here
    )
    slopes = [
        natural(cube[REACH + 1 : REACH + 1 + p.xo], 0) - natural(cube[REACH - 1 : REACH - 1 + p.xo], 0),
        pltpu.roll(here, p.yw - 1, 1) - pltpu.roll(here, 1, 1),
        natural(inner, 1) - natural(inner, -1),
    ]
    weighted = density * jnp.exp(-TAU * potential)
    energy = source_here * (C_TF + enhance) + external * density - C_X * density * here
    terms = [weighted, density, energy - density * potential]
    for slope in slopes:
        for axis in range(3):
            terms.append(0.5 * slope * levers[:, 1 + axis])
    lane = iota((p.yw, p.zq), 1)
    y = iota((p.yw, p.zq), 0)
    own = (lane < p.zo) & (y >= p.own_y) & (y < p.own_y + p.ny)
    rows = []
    for term in terms:
        rows.append(jnp.sum(jnp.where(own, jnp.sum(term, axis=0), 0.0), axis=0, keepdims=True))
    rows.append(jnp.zeros((SUMS - len(rows), p.zq), F32))
    sums = jnp.sum(jnp.concatenate(rows, axis=0), axis=1, keepdims=True)
    onto = iota((SUMS, 128), 0) == iota((SUMS, 128), 1)
    row = jnp.sum(jnp.where(onto, sums, 0.0), axis=0, keepdims=True)
    return potential, weighted, jnp.broadcast_to(row, (8, 128))


def pick(row, number):
    return jnp.sum(jnp.where(iota(row.shape, 1) == number, row, 0.0), axis=1, keepdims=True)


def update_scratch(p):
    def pairs(planes):
        return pltpu.VMEM((2, planes // 2, p.lo + 2, STRIPS, p.lanes), BF)

    return [
        pltpu.VMEM((2, p.xe, p.yw, 3 * p.zp), F32),
        pairs(p.xo + 10),
        pairs(p.xo + 8),
        pltpu.VMEM((p.xo + 2, p.lo + 2, STRIPS, p.lanes), BF),
        pltpu.VMEM((p.xo + 2, p.ze, p.lanes), F32),
        pltpu.VMEM((p.xo + 4, p.ze, p.lanes), F32),
        pltpu.VMEM((p.xo + 2, p.ze, p.narrow), F32),
    ]


def update_cost(p):
    flops = 2 * 6 * p.lanes * p.lanes * p.ze * (4 * p.xo + 20)
    return pl.CostEstimate(flops=flops, bytes_accessed=6 << 20, transcendentals=0)


def kernel_call(p, name, body, out_shape, n_smem, n_vmem, scratch=(), cost=None, n_hbm=0):
    return pl.pallas_call(
        body,
        name=name,
        out_shape=out_shape,
        in_specs=[SM] * n_smem + [HB] * n_hbm + [VM] * n_vmem,
        out_specs=tuple(SM if len(shape.shape) == 1 else VM for shape in out_shape),
        scratch_shapes=list(scratch),
        compiler_params=pltpu.CompilerParams(vmem_limit_bytes=p.limit),
        cost_estimate=cost,
    )


def f32(*shape):
    return jax.ShapeDtypeStruct(shape, F32)


def widen(cells, axis, dim, before, after):
    size = cells.shape[dim]
    count = lax.axis_size(axis)

    def fetch(step, start, stop):
        piece = lax.slice_in_dim(cells, start, stop, axis=dim)
        if step % count == 0:
            return piece
        return lax.ppermute(piece, axis, [(i, (i + step) % count) for i in range(count)])

    pieces = [cells]
    left = before
    step = 1
    while left > 0:
        take = min(left, size)
        pieces.insert(0, fetch(step, size - take, size))
        left -= take
        step += 1
    left = after
    step = 1
    while left > 0:
        take = min(left, size)
        pieces.append(fetch(-step, 0, take))
        left -= take
        step += 1
    return jnp.concatenate(pieces, axis=dim)


def any_mesh(density, external, w_first, w_second, w_third, w_last):
    nx, ny, nz = density.shape
    ch = w_first.shape[1]
    yw = up(ny + 2 * REACH, 8)
    own_y = (yw - ny) // 2
    xo = up(nx, GROUP)
    p = Plan(xo, yw, own_y, ny, nz, ch, 60)
    weights = spread_weights(p, w_first, w_second, w_third, w_last)
    axes = ("gx", "gy", "gz")
    count = nx * ny * nz * lax.axis_size("gx") * lax.axis_size("gy") * lax.axis_size("gz")
    total_mass = lax.psum(jnp.sum(density), axes)

    def body(cur, ext, *refs):
        weight_refs, (o_pot, o_weighted, o_sums), scratch = refs[:6], refs[6:9], refs[9:]
        pot, weighted, sums = update_kernel(p, cur[...], ext[...], weight_refs, scratch)
        o_pot[...] = pot
        o_weighted[...] = weighted
        o_sums[...] = sums

    call = kernel_call(
        p,
        "update",
        body,
        (f32(xo, yw, p.zq), f32(xo, yw, p.zq), f32(8, 128)),
        0,
        8,
        update_scratch(p),
        update_cost(p),
    )
    ext = jnp.pad(
        external, ((0, xo - nx), (own_y, yw - ny - own_y), (0, p.zq - nz))
    )
    current = density
    chem, stress = [], []
    for _ in range(STEPS):
        tile = widen(current, "gz", 2, p.zh, p.ze - nz - p.zh)
        tile = widen(tile, "gy", 1, own_y, yw - ny - own_y)
        tile = widen(tile, "gx", 0, REACH, REACH)
        tile = jnp.pad(tile, ((0, 0), (0, 0), (0, p.zp - p.ze)), constant_values=1.0)
        pot, weighted, sums = call(tile, ext, *weights)
        totals = lax.psum(sums[0, :SUMS], axes)
        chem.append(jnp.log(total_mass / totals[0]) / TAU)
        moments = totals[3:12].reshape(3, 3)
        stress.append((moments + jnp.eye(3, dtype=F32) * totals[2]) / count)
        current = weighted[:nx, own_y : own_y + ny, :nz] * (total_mass / totals[0])
        potential = pot[:nx, own_y : own_y + ny, :nz]
    return current, potential, jnp.stack(chem), jnp.stack(stress)


def split_pairs(density, external, w_first, w_second, w_third, w_last):
    nx, ny, nz = density.shape
    ch = w_first.shape[1]
    half = nz // 2
    p = Plan(nx, 2 * ny, 0, 2 * ny, half, ch, 20)
    lanes = p.zp
    cells = nx * ny * nz * 16
    axes = ("gx", "gy", "gz")

    def along_x(cells_out, step):
        return lax.ppermute(cells_out, "gx", [(i, (i + step) % 4) for i in range(4)])

    def quarter(number):
        return (number % 2) * 2 + number // 2

    def along_z(cells_out, step):
        pairs = [(quarter(q), quarter((q + step) % 4)) for q in range(4)]
        return lax.ppermute(cells_out, ("gy", "gz"), pairs)

    weights = spread_weights(p, w_first, w_second, w_third, w_last)

    def widen_body(own_hbm, ext_hbm, left_ref, right_ref, o_wide, sems):
        copies = [
            pltpu.make_async_copy(own_hbm, o_wide.at[REACH : REACH + nx], sems.at[0]),
            pltpu.make_async_copy(ext_hbm, o_wide.at[p.xe :], sems.at[1]),
        ]
        for copy in copies:
            copy.start()
        o_wide[:REACH] = left_ref[nx - REACH :]
        o_wide[REACH + nx : p.xe] = right_ref[:REACH]
        for copy in copies:
            copy.wait()

    (wide,) = kernel_call(
        p,
        "widen",
        widen_body,
        (f32(p.xe + nx, ny, nz),),
        0,
        2,
        [pltpu.SemaphoreType.DMA((2,))],
        n_hbm=2,
    )(
        *[pltpu.with_memory_space_constraint(a, pltpu.HBM) for a in (density, external)],
        along_x(density, 1),
        along_x(density, -1),
    )
    from_y = lax.ppermute(wide, "gy", [(0, 1), (1, 0)])
    from_z = lax.ppermute(wide, "gz", [(0, 1), (1, 0)])
    from_yz = lax.ppermute(wide, ("gy", "gz"), [(i, 3 - i) for i in range(4)])
    planes = p.xe + nx

    def first_body(own, y, z, yz, *refs):
        weight_refs, outs, tile, scratch = refs[:6], refs[6:11], refs[11], refs[12:]
        second = lax.axis_index("gy") == 1
        shift = jnp.where(second, nz - half + p.zh, p.zh)
        lane = iota((planes, p.yw, lanes), 2)
        for ref, other in ((own, y), (z, yz)):
            mine, theirs = ref[...], other[...]
            lower = jnp.where(second, theirs, mine)
            upper = jnp.where(second, mine, theirs)
            cells_here = jnp.concatenate([lower, upper], axis=1)
            moved = pltpu.roll(cells_here, shift, 2)
            if ref is own:
                tile[...] = moved
            else:
                begin = jnp.where(second, half + p.zh, 0)
                end = jnp.where(second, lanes, p.zh)
                tile[...] = jnp.where((lane >= begin) & (lane < end), moved, tile[...])
        cur = tile[: p.xe]
        ext = pltpu.roll(tile[p.xe :], lanes - p.zh, 2)
        _, weighted, sums = update_kernel(p, cur, ext, weight_refs, scratch)
        o_own, o_low, o_high, o_ext, o_sums = outs
        o_own[...] = weighted
        o_low[:REACH] = weighted[:REACH]
        o_low[REACH] = sums
        o_high[:REACH] = weighted[nx - REACH :]
        o_high[REACH] = sums
        o_ext[...] = ext
        o_sums[...] = sums

    message = f32(REACH + 1, p.yw, lanes)
    own, low, high, ext, sums = kernel_call(
        p,
        "update_one",
        first_body,
        (f32(nx, p.yw, lanes), message, message, f32(nx, p.yw, lanes), f32(8, 128)),
        0,
        10,
        [pltpu.VMEM((planes, p.yw, lanes), F32)] + update_scratch(p),
        update_cost(p),
    )(wide, from_y, from_z, from_yz, *weights)

    left = along_x(high, 1)
    right = along_x(low, -1)
    far = along_x(sums, 2)

    packs = up(p.xe, 8) // 8

    def join_body(own_ref, sums_ref, left_ref, right_ref, far_ref, o_tile, o_down, o_up, o_sums):
        tile = jnp.concatenate([left_ref[:REACH], own_ref[...], right_ref[:REACH]], axis=0)
        sums = sums_ref[...] + left_ref[REACH] + right_ref[REACH] + far_ref[...]
        o_tile[...] = tile
        o_sums[...] = sums
        lane = lax.div(iota((p.yw, lanes), 1), p.zh)
        for ref, start in ((o_down, 0), (o_up, half - p.zh)):
            for pack in range(packs):
                joined = jnp.zeros((p.yw, lanes), F32)
                for k in range(min(8, p.xe - 8 * pack)):
                    moved = pltpu.roll(tile[8 * pack + k], (k * p.zh - start) % lanes, 1)
                    joined = jnp.where(lane == k, moved, joined)
                ref[pack] = joined
            ref[packs] = sums

    edge = f32(packs + 1, p.yw, lanes)
    tile, down, upper, sums = kernel_call(
        p,
        "join",
        join_body,
        (f32(p.xe, p.yw, lanes), edge, edge, f32(8, 128)),
        0,
        5,
    )(own, sums, left, right, far)
    below = along_z(upper, 1)
    above = along_z(down, -1)
    across = lax.ppermute(sums, "gz", [(0, 1), (1, 0)])

    def second_body(tile_ref, below_ref, above_ref, sums_ref, across_ref, ext_ref, *refs):
        weight_refs, outs, cur, scratch = refs[:6], refs[6:10], refs[10], refs[11:]
        o_keep, o_send, o_sums, o_totals = outs
        totals = sums_ref[...] + across_ref[...] + below_ref[packs] + above_ref[packs]
        o_totals[...] = totals
        scale = pick(totals, 1) / pick(totals, 0)
        lane = iota((p.yw, lanes), 1)
        for x in range(p.xe):
            pack, k = divmod(x, 8)
            lower = pltpu.roll(below_ref[pack], -k * p.zh % lanes, 1)
            top = pltpu.roll(above_ref[pack], (p.zh + half - k * p.zh) % lanes, 1)
            middle = pltpu.roll(tile_ref[x], p.zh, 1)
            joined = jnp.where(lane < p.zh, lower, jnp.where(lane < p.zh + half, middle, top))
            cur[x] = joined * scale
        pot, weighted, sums_here = update_kernel(p, cur[...], ext_ref[...], weight_refs, scratch)
        o_sums[...] = jnp.broadcast_to(sums_here[:4], (16, 4, 128))
        both = jnp.where(
            iota(pot.shape, 2) < half, pot, pltpu.roll(weighted, half, 2)
        )
        second = lax.axis_index("gy") == 1
        lower, top = both[:, :ny], both[:, ny:]
        o_keep[...] = jnp.where(second, top, lower)
        o_send[...] = jnp.where(second, lower, top)

    share = f32(nx, ny, lanes)
    keep, send, sums, totals = kernel_call(
        p,
        "update_two",
        second_body,
        (share, share, f32(16, 4, 128), f32(8, 128)),
        0,
        12,
        [pltpu.VMEM((p.xe, p.yw, lanes), F32)] + update_scratch(p),
        update_cost(p),
    )(tile, below, above, sums, across, ext, *weights)

    other = lax.ppermute(send, "gy", [(0, 1), (1, 0)])
    gathered = lax.all_to_all(sums, axes, 0, 0, tiled=True)

    def last_body(keep_ref, other_ref, all_ref, totals_ref, o_new, o_pot, o_chem, o_stress):
        first = totals_ref[...]
        last = jnp.sum(all_ref[...], axis=0)
        last = jnp.concatenate([last, last], axis=0)
        mass = pick(first, 1)
        scale = mass / pick(last, 0)
        second = lax.axis_index("gy") == 1
        mine, theirs = keep_ref[...], other_ref[...]
        lower = jnp.where(second, theirs, mine)
        top = jnp.where(second, mine, theirs)
        lane = iota((nx, ny, nz), 2)
        o_pot[...] = jnp.where(lane < half, lower, pltpu.roll(top, half, 2))
        o_new[...] = jnp.where(lane < half, pltpu.roll(lower, half, 2), top) * scale[:ny]
        lane = iota((8, 128), 1)
        for step, total in enumerate((first, last)):
            chem = jnp.log(mass / pick(total, 0)) * (1.0 / TAU)
            o_chem[step] = chem[0, 0]
            for a in range(3):
                moments = pltpu.roll(total, 128 - 3 - 3 * a, 1)
                row = moments + jnp.where(lane == a, pick(total, 2), 0.0)
                o_stress[a, step : step + 1] = row[:1, :3] * (1.0 / cells)

    new, potential, chem, stress = kernel_call(
        p,
        "finish",
        last_body,
        (f32(nx, ny, nz), f32(nx, ny, nz), f32(STEPS), f32(3, STEPS, 3)),
        0,
        4,
    )(keep, other, gathered, totals)
    return new, potential, chem, jnp.transpose(stress, (1, 0, 2))


def on_device(density, external, w_first, w_second, w_third, w_last):
    mesh = tuple(lax.axis_size(axis) for axis in ("gx", "gy", "gz"))
    if mesh == (4, 2, 2) and density.shape == (8, 4, 128):
        return split_pairs(density, external, w_first, w_second, w_third, w_last)
    return any_mesh(density, external, w_first, w_second, w_third, w_last)


def solution(mesh):
    cells = P(("boxes", "gx"), "gy", "gz")
    return jax.shard_map(
        on_device,
        mesh=mesh,
        in_specs=(cells, cells, P(), P(), P(), P()),
        out_specs=(cells, cells, P("boxes"), P("boxes", None, None)),
        check_vma=False,
    )
```

```python
import functools

import jax
import jax.numpy as jnp
from jax import lax
from jax.experimental import pallas as pl
from jax.experimental.pallas import tpu as pltpu
from jax.sharding import PartitionSpec as P

STEPS = 2
C_TF = 2.871234
C_X = 0.7385588
TAU = 0.1
REACH = 6
STRIPS = 16
GROUP = 4
PAIRS = 8
SUMS = 16
BF = jnp.bfloat16
F32 = jnp.float32
VM = pl.BlockSpec(memory_space=pltpu.VMEM)
SM = pl.BlockSpec(memory_space=pltpu.SMEM)
HB = pl.BlockSpec(memory_space=pltpu.HBM)


def up(number, unit):
    return -(-number // unit) * unit


def iota(shape, dim):
    return lax.broadcasted_iota(jnp.int32, shape, dim)


def dot(a, b):
    return jnp.dot(a, b, preferred_element_type=F32)


def dot_tn(a, b):
    return lax.dot_general(a, b, (((0,), (0,)), ((), ())), preferred_element_type=F32)


def dot_nt(a, b):
    return lax.dot_general(a, b, (((1,), (1,)), ((), ())), preferred_element_type=F32)


class Plan:
    def __init__(self, xo, yw, own_y, ny, zo, ch, limit):
        self.xo, self.yw, self.own_y, self.ny, self.zo, self.ch = xo, yw, own_y, ny, zo, ch
        self.limit = limit << 20
        self.xe = xo + 2 * REACH
        self.ze = up(zo + 2 * REACH, STRIPS)
        self.zh = (self.ze - zo) // 2
        self.lo = self.ze // STRIPS
        self.zp = up(self.ze, 128)
        self.zq = up(zo, 128)
        self.lanes = yw * ch
        self.fields = 4 * yw
        self.narrow = up(GROUP * self.fields, 128)


PAIR_BLOCKS = (
    (0, 0, 0, 0),
    (0, 0, 1, 1),
    (1, 0, 1, 0),
    (1, 1, 0, 1),
    (2, 1, 0, 0),
    (2, 1, 1, 1),
)


def weights_kernel(p, dense_in, single_in, dense_out, first_out, last_out, arrivals):
    ch, yw, lanes = p.ch, p.yw, p.lanes
    half, wide = yw // 2, lanes // 2

    tile = (
        jnp.bitwise_and(iota((ch, lanes), 1), ch - 1) == iota((ch, lanes), 0)
    ).astype(F32).astype(BF)
    tiled = [dot(ref[...], tile).astype(BF) for ref in single_in]

    rows = 18 * yw
    row = iota((rows, 1), 0)
    yi = lax.rem(row, yw)
    tx = lax.rem(lax.div(row, yw), 3)
    tz = lax.rem(lax.div(row, 3 * yw), 3)
    yo = lax.div(iota((rows, lanes), 1), ch)
    for single, ref_out, direction in zip(tiled, first_out, (1, -1)):
        total = jnp.zeros((rows, lanes), F32)
        for ty in range(3):
            number = 9 * tx + 3 * ty + tz
            number = number if direction > 0 else 26 - number
            pick = (iota((rows, 27), 1) == number).astype(F32).astype(BF)
            here = lax.rem(yo + (ty - 1 + yw), yw) == yi
            total = total + jnp.where(here, dot(pick, single), 0.0)
        ref_out[...] = (0.5 * total).astype(BF)

    rows = p.narrow
    row = iota((rows, 1), 0)
    yo = lax.rem(row, yw)
    field = lax.rem(lax.div(row, yw), 4)
    tx = lax.div(row, 4 * yw)
    yi = lax.div(iota((rows, lanes), 1), ch)
    for single, ref_out, direction in zip(tiled[::-1], last_out, (1, -1)):
        for tz in range(3):
            total = jnp.zeros((rows, lanes), F32)
            for ty in range(3):
                number = 9 * tx + 3 * ty + tz
                number = number if direction > 0 else 26 - number
                if direction > 0:
                    factor = jnp.where(field == 0, 1, 0)
                else:
                    factor = jnp.where(
                        field == 0,
                        1,
                        jnp.where(field == 1, 1 - tx, jnp.where(field == 2, 1 - ty, 1 - tz)),
                    )
                factor = jnp.where(tx < 3, factor, 0).astype(F32)
                pick = jnp.where(iota((rows, 27), 1) == number, factor, 0.0).astype(BF)
                here = lax.rem(yo + (ty - 1 + yw), yw) == yi
                total = total + jnp.where(here, dot(pick, single), 0.0)
            ref_out[tz] = total.astype(BF)

    for ref_in, ref_out, arrive in zip(dense_in, dense_out, arrivals):
        arrive()
        taps = []
        for ty in range(3):
            taps.append(
                jnp.concatenate(
                    [ref_in[26 - (9 * (t // 3) + 3 * ty + t % 3)] for t in range(9)], axis=0
                )
            )
        taps = jnp.concatenate(taps, axis=1)
        row, column = iota((3 * ch, lanes), 0), iota((3 * ch, lanes), 1)
        ty = lax.div(row, ch)
        minus = column >= wide
        for yi in range(half):
            raw = yi + 1 - ty
            wraps = (raw < 0) | (raw >= half)
            yo = lax.rem(raw + half, half)
            target = row + (yo - ty) * ch
            match = jnp.where(minus, column - wide, column) == target
            value = jnp.where(wraps & minus, -0.25, 0.25)
            place = jnp.where(match, value, 0.0).astype(BF)
            spread = dot(taps, place).astype(BF).reshape(3, 3, ch, lanes)
            for sign in range(2):
                for tx, step, x_in, x_out in PAIR_BLOCKS:
                    begin = x_in * wide + yi * ch
                    ref_out[
                        sign, step, :, begin : begin + ch, x_out * wide : (x_out + 1) * wide
                    ] = spread[tx, :, :, sign * wide : (sign + 1) * wide]
        none = jnp.zeros((2, 3, wide, wide), BF)
        ref_out[:, 0, :, :wide, wide:] = none
        ref_out[:, 1, :, wide:, :wide] = none


def spread_weights(p, w_first, w_second, w_third, w_last):
    inputs = (w_second, w_third, w_first, w_last)

    def body(*refs):
        hbm, outs, held, sems = refs[:4], refs[4:10], refs[10:14], refs[14]
        copies = [pltpu.make_async_copy(hbm[i], held[i], sems.at[i]) for i in range(4)]
        for copy in copies[::-1]:
            copy.start()
        for copy in copies[2:]:
            copy.wait()
        arrivals = [copy.wait for copy in copies[:2]]
        weights_kernel(p, held[:2], held[2:], outs[:2], outs[2:4], outs[4:], arrivals)

    dense = jax.ShapeDtypeStruct((2, 2, 3, p.lanes, p.lanes), BF)
    single = jax.ShapeDtypeStruct((18 * p.yw, p.lanes), BF)
    narrow = jax.ShapeDtypeStruct((3, p.narrow, p.lanes), BF)
    flops = 2 * 2 * 9 * 3 * p.ch * p.lanes * p.lanes
    return pl.pallas_call(
        body,
        name="spread_weights",
        out_shape=(dense,) * 2 + (single,) * 2 + (narrow,) * 2,
        in_specs=[HB] * 4,
        out_specs=(VM,) * 6,
        scratch_shapes=[pltpu.VMEM(a.shape, a.dtype) for a in inputs]
        + [pltpu.SemaphoreType.DMA((4,))],
        compiler_params=pltpu.CompilerParams(vmem_limit_bytes=p.limit),
        cost_estimate=pl.CostEstimate(flops=flops, bytes_accessed=3 << 20, transcendentals=0),
    )(*[pltpu.with_memory_space_constraint(a, pltpu.HBM) for a in inputs])


def cube_root(value):
    guess = jnp.exp(jnp.log(value) * (1.0 / 3.0))
    return guess - (guess - value / (guess * guess)) * (1.0 / 3.0)


def store_edges(p, ref, place, value):
    tiles = value.reshape(p.lo, STRIPS, p.lanes)
    ref[place, 1 : p.lo + 1] = tiles.astype(BF)
    ref[place, 0] = pltpu.roll(tiles[p.lo - 1], 1, 0).astype(BF)
    ref[place, p.lo + 1] = pltpu.roll(tiles[0], STRIPS - 1, 0).astype(BF)


def blocks(total, size):
    return [(start, min(size, total - start)) for start in range(0, total, size)]


def store_pairs(p, ref, place, value):
    wide = p.lanes // 2
    first, second = value[:, :wide], value[:, wide:]
    pair, side = divmod(place, 2)
    lanes = slice(side * wide, (side + 1) * wide)
    for sign, part in enumerate((first + second, first - second)):
        tiles = part.reshape(p.lo, STRIPS, wide)
        ref[sign, pair, 1 : p.lo + 1, :, lanes] = tiles.astype(BF)
        ref[sign, pair, 0, :, lanes] = pltpu.roll(tiles[p.lo - 1], 1, 0).astype(BF)
        ref[sign, pair, p.lo + 1, :, lanes] = pltpu.roll(tiles[0], STRIPS - 1, 0).astype(BF)


def dense_planes(p, ref, w_ref, start, count, forward):
    halves = []
    for sign in range(2):
        total = None
        for step in range(2):
            for tz in range(3):
                rows = ref[sign, start + step : start + step + count, tz : tz + p.lo]
                rows = rows.reshape(count * p.ze, p.lanes)
                if forward:
                    part = dot_nt(rows, w_ref[sign, 1 - step, 2 - tz])
                else:
                    part = dot(rows, w_ref[sign, step, tz])
                total = part if total is None else total + part
        halves.append(total)
    wide = p.lanes // 2
    planes = []
    for k in range(2 * count):
        rows = slice(k // 2 * p.ze, (k // 2 + 1) * p.ze)
        lanes = slice(k % 2 * wide, (k % 2 + 1) * wide)
        plus, minus = halves[0][rows, lanes], halves[1][rows, lanes]
        planes.append(jnp.concatenate([plus + minus, plus - minus], axis=1))
    return planes


def gate(value, slope=True):
    wave = jnp.tanh(value)
    product = value * wave
    act = value + product
    if not slope:
        return act, None
    rise = 1.0 + wave
    return act, rise + rise * (value - product)


def to_planes(p, field, spread, planes_ref):
    high = field.astype(BF)
    low = (field - high.astype(F32)).astype(BF)
    flat = jnp.concatenate(
        [high.reshape(p.xe * p.yw, p.zp), low.reshape(p.xe * p.yw, p.zp)], axis=0
    )
    planes_ref[...] = dot(flat, spread).reshape(2, p.xe, p.yw, 3 * p.zp)


def single_plane(p, planes_ref, place, w_ref):
    pieces = []
    for half in range(2):
        for tz in range(3):
            piece = planes_ref[half, place : place + 3, :, tz * p.zp : tz * p.zp + p.ze]
            pieces.append(piece.reshape(3 * p.yw, p.ze))
    window = jnp.concatenate(pieces, axis=0).astype(BF)
    return dot_tn(window, w_ref[...])


def narrow_fold(p, ref, w_ref, planes_ref, back):
    for start, count in blocks(p.xo + 2, 5):
        total = None
        for tz in range(3):
            rows = ref[start : start + count, tz : tz + p.lo].reshape(count * p.ze, p.lanes)
            part = dot_nt(rows, w_ref[tz])
            total = part if total is None else total + part
        planes_ref[start : start + count] = total.reshape(count, p.ze, p.narrow)
    lane = lax.div(iota((p.ze, p.narrow), 1), p.fields)
    fields = []
    for first in range(0, p.xo, GROUP):
        joined = jnp.zeros((p.ze, p.narrow), F32)
        for k in range(GROUP):
            total = None
            for tx in range(3):
                part = planes_ref[first + k + tx]
                shift = (k - tx) * p.fields % p.narrow
                part = pltpu.roll(part, shift, 1) if shift else part
                total = part if total is None else total + part
            joined = jnp.where(lane == k, total, joined)
        high = joined.astype(BF)
        rest = joined - high.astype(F32)
        mid = rest.astype(BF)
        low = (rest - mid.astype(F32)).astype(BF)
        parts = jnp.concatenate([high, mid, low], axis=0)
        natural = dot_tn(parts, back)[: GROUP * p.fields]
        fields.append(natural.reshape(GROUP, 4, p.yw, p.zq))
    return jnp.concatenate(fields, axis=0)


def update_kernel(p, current, external, weights, scratch):
    w_two, w_three, w_one, w_source, w_enhance, w_lever = weights
    planes, act_a, act_b, act_c, slope_one, slope_two, narrow = scratch

    current = jnp.where(iota(current.shape, 2) < p.ze, current, 1.0)
    cube = cube_root(current)
    source = current * cube * cube

    shape = (p.zp, 3 * p.zp)
    lane = iota(shape, 1)
    tz = lax.div(lane, p.zp)
    row = lane - tz * p.zp
    cell = p.lo * jnp.bitwise_and(row, STRIPS - 1) + lax.div(row, STRIPS) + tz - 1
    spread = jnp.where((cell == iota(shape, 0)) & (row < p.ze), 1.0, 0.0).astype(BF)
    shape = (3 * p.ze, p.zq)
    row = lax.rem(iota(shape, 0), p.ze)
    cell = p.lo * jnp.bitwise_and(row, STRIPS - 1) + lax.div(row, STRIPS) - p.zh
    back = jnp.where((cell == iota(shape, 1)) & (cell < p.zo), 1.0, 0.0).astype(BF)

    to_planes(p, cube, spread, planes)
    for x in range(p.xo + 10):
        value = single_plane(p, planes, x, w_one)
        inside = 4 <= x < p.xo + 6
        act, slope = gate(value, inside)
        store_pairs(p, act_a, x, act)
        if inside:
            slope_one[x - 4] = slope

    for start, count in blocks((p.xo + 8) // 2, PAIRS):
        for k, value in enumerate(dense_planes(p, act_a, w_two, start, count, True)):
            x = 2 * start + k
            inside = 2 <= x < p.xo + 6
            act, slope = gate(value, inside)
            store_pairs(p, act_b, x, act)
            if inside:
                slope_two[x - 2] = slope

    to_planes(p, source, spread, planes)
    for start, count in blocks((p.xo + 6) // 2, PAIRS):
        for k, value in enumerate(dense_planes(p, act_b, w_three, start, count, True)):
            x = 2 * start + k
            act, slope = gate(value)
            if 2 <= x < p.xo + 4:
                store_edges(p, act_c, x - 2, act)
            store_pairs(p, act_a, x, single_plane(p, planes, x + 2, w_source) * slope)

    enhance = narrow_fold(p, act_c, w_enhance, narrow, back)[:, 0]

    for start, count in blocks((p.xo + 4) // 2, PAIRS):
        for k, value in enumerate(dense_planes(p, act_a, w_three, start, count, False)):
            store_pairs(p, act_b, 2 * start + k, value * slope_two[2 * start + k])

    for start, count in blocks((p.xo + 2) // 2, PAIRS):
        for k, value in enumerate(dense_planes(p, act_b, w_two, start, count, False)):
            store_edges(p, act_c, 2 * start + k, value * slope_one[2 * start + k])

    levers = narrow_fold(p, act_c, w_lever, narrow, back)

    def natural(field, step):
        return pltpu.roll(field, (p.zp - p.zh - step) % p.zp, 2)[:, :, : p.zq]

    inner = cube[REACH : REACH + p.xo]
    here = natural(inner, 0)
    density = natural(current[REACH : REACH + p.xo], 0)
    source_here = natural(source[REACH : REACH + p.xo], 0)
    squared = here * here
    potential = (
        5.0 / 3.0 * squared * (C_TF + enhance)
        + levers[:, 0] / (3.0 * squared)
        + external
        - 4.0 / 3.0 * C_X * here
    )
    slopes = [
        natural(cube[REACH + 1 : REACH + 1 + p.xo], 0) - natural(cube[REACH - 1 : REACH - 1 + p.xo], 0),
        pltpu.roll(here, p.yw - 1, 1) - pltpu.roll(here, 1, 1),
        natural(inner, 1) - natural(inner, -1),
    ]
    weighted = density * jnp.exp(-TAU * potential)
    energy = source_here * (C_TF + enhance) + external * density - C_X * density * here
    terms = [weighted, density, energy - density * potential]
    for slope in slopes:
        for axis in range(3):
            terms.append(0.5 * slope * levers[:, 1 + axis])
    lane = iota((p.yw, p.zq), 1)
    y = iota((p.yw, p.zq), 0)
    own = (lane < p.zo) & (y >= p.own_y) & (y < p.own_y + p.ny)
    rows = []
    for term in terms:
        rows.append(jnp.sum(jnp.where(own, jnp.sum(term, axis=0), 0.0), axis=0, keepdims=True))
    rows.append(jnp.zeros((SUMS - len(rows), p.zq), F32))
    sums = jnp.sum(jnp.concatenate(rows, axis=0), axis=1, keepdims=True)
    onto = iota((SUMS, 128), 0) == iota((SUMS, 128), 1)
    row = jnp.sum(jnp.where(onto, sums, 0.0), axis=0, keepdims=True)
    return potential, weighted, jnp.broadcast_to(row, (8, 128))


def pick(row, number):
    return jnp.sum(jnp.where(iota(row.shape, 1) == number, row, 0.0), axis=1, keepdims=True)


def update_scratch(p):
    def pairs(planes):
        return pltpu.VMEM((2, planes // 2, p.lo + 2, STRIPS, p.lanes), BF)

    return [
        pltpu.VMEM((2, p.xe, p.yw, 3 * p.zp), F32),
        pairs(p.xo + 10),
        pairs(p.xo + 8),
        pltpu.VMEM((p.xo + 2, p.lo + 2, STRIPS, p.lanes), BF),
        pltpu.VMEM((p.xo + 2, p.ze, p.lanes), F32),
        pltpu.VMEM((p.xo + 4, p.ze, p.lanes), F32),
        pltpu.VMEM((p.xo + 2, p.ze, p.narrow), F32),
    ]


def update_cost(p):
    flops = 2 * 6 * p.lanes * p.lanes * p.ze * (4 * p.xo + 20)
    return pl.CostEstimate(flops=flops, bytes_accessed=6 << 20, transcendentals=0)


def kernel_call(p, name, body, out_shape, n_smem, n_vmem, scratch=(), cost=None, n_hbm=0):
    return pl.pallas_call(
        body,
        name=name,
        out_shape=out_shape,
        in_specs=[SM] * n_smem + [HB] * n_hbm + [VM] * n_vmem,
        out_specs=tuple(SM if len(shape.shape) == 1 else VM for shape in out_shape),
        scratch_shapes=list(scratch),
        compiler_params=pltpu.CompilerParams(vmem_limit_bytes=p.limit),
        cost_estimate=cost,
    )


def f32(*shape):
    return jax.ShapeDtypeStruct(shape, F32)


def widen(cells, axis, dim, before, after):
    size = cells.shape[dim]
    count = lax.axis_size(axis)

    def fetch(step, start, stop):
        piece = lax.slice_in_dim(cells, start, stop, axis=dim)
        if step % count == 0:
            return piece
        return lax.ppermute(piece, axis, [(i, (i + step) % count) for i in range(count)])

    pieces = [cells]
    left = before
    step = 1
    while left > 0:
        take = min(left, size)
        pieces.insert(0, fetch(step, size - take, size))
        left -= take
        step += 1
    left = after
    step = 1
    while left > 0:
        take = min(left, size)
        pieces.append(fetch(-step, 0, take))
        left -= take
        step += 1
    return jnp.concatenate(pieces, axis=dim)


def any_mesh(density, external, w_first, w_second, w_third, w_last):
    nx, ny, nz = density.shape
    ch = w_first.shape[1]
    yw = up(ny + 2 * REACH, 8)
    own_y = (yw - ny) // 2
    xo = up(nx, GROUP)
    p = Plan(xo, yw, own_y, ny, nz, ch, 60)
    weights = spread_weights(p, w_first, w_second, w_third, w_last)
    axes = ("gx", "gy", "gz")
    count = nx * ny * nz * lax.axis_size("gx") * lax.axis_size("gy") * lax.axis_size("gz")
    total_mass = lax.psum(jnp.sum(density), axes)

    def body(cur, ext, *refs):
        weight_refs, (o_pot, o_weighted, o_sums), scratch = refs[:6], refs[6:9], refs[9:]
        pot, weighted, sums = update_kernel(p, cur[...], ext[...], weight_refs, scratch)
        o_pot[...] = pot
        o_weighted[...] = weighted
        o_sums[...] = sums

    call = kernel_call(
        p,
        "update",
        body,
        (f32(xo, yw, p.zq), f32(xo, yw, p.zq), f32(8, 128)),
        0,
        8,
        update_scratch(p),
        update_cost(p),
    )
    ext = jnp.pad(
        external, ((0, xo - nx), (own_y, yw - ny - own_y), (0, p.zq - nz))
    )
    current = density
    chem, stress = [], []
    for _ in range(STEPS):
        tile = widen(current, "gz", 2, p.zh, p.ze - nz - p.zh)
        tile = widen(tile, "gy", 1, own_y, yw - ny - own_y)
        tile = widen(tile, "gx", 0, REACH, REACH)
        tile = jnp.pad(tile, ((0, 0), (0, 0), (0, p.zp - p.ze)), constant_values=1.0)
        pot, weighted, sums = call(tile, ext, *weights)
        totals = lax.psum(sums[0, :SUMS], axes)
        chem.append(jnp.log(total_mass / totals[0]) / TAU)
        moments = totals[3:12].reshape(3, 3)
        stress.append((moments + jnp.eye(3, dtype=F32) * totals[2]) / count)
        current = weighted[:nx, own_y : own_y + ny, :nz] * (total_mass / totals[0])
        potential = pot[:nx, own_y : own_y + ny, :nz]
    return current, potential, jnp.stack(chem), jnp.stack(stress)


def split_pairs(density, external, w_first, w_second, w_third, w_last):
    nx, ny, nz = density.shape
    ch = w_first.shape[1]
    half = nz // 2
    p = Plan(nx, 2 * ny, 0, 2 * ny, half, ch, 20)
    lanes = p.zp
    cells = nx * ny * nz * 16
    axes = ("gx", "gy", "gz")

    def along_x(cells_out, step):
        return lax.ppermute(cells_out, "gx", [(i, (i + step) % 4) for i in range(4)])

    def quarter(number):
        return (number % 2) * 2 + number // 2

    def along_z(cells_out, step):
        pairs = [(quarter(q), quarter((q + step) % 4)) for q in range(4)]
        return lax.ppermute(cells_out, ("gy", "gz"), pairs)

    weights = spread_weights(p, w_first, w_second, w_third, w_last)

    def widen_body(own_hbm, ext_hbm, left_ref, right_ref, o_wide, o_cells, sems):
        copies = [
            pltpu.make_async_copy(own_hbm, o_wide.at[REACH : REACH + nx], sems.at[0]),
            pltpu.make_async_copy(ext_hbm, o_wide.at[p.xe :], sems.at[1]),
        ]
        for copy in copies:
            copy.start()
        o_wide[:REACH] = left_ref[nx - REACH :]
        o_wide[REACH + nx : p.xe] = right_ref[:REACH]
        for copy in copies:
            copy.wait()
        o_cells[...] = o_wide[: p.xe]

    wide, cells_wide = kernel_call(
        p,
        "widen",
        widen_body,
        (f32(p.xe + nx, ny, nz), f32(p.xe, ny, nz)),
        0,
        2,
        [pltpu.SemaphoreType.DMA((2,))],
        n_hbm=2,
    )(
        *[pltpu.with_memory_space_constraint(a, pltpu.HBM) for a in (density, external)],
        along_x(density, 1),
        along_x(density, -1),
    )
    from_y = lax.ppermute(wide, "gy", [(0, 1), (1, 0)])
    from_z = lax.ppermute(cells_wide, "gz", [(0, 1), (1, 0)])
    from_yz = lax.ppermute(cells_wide, ("gy", "gz"), [(i, 3 - i) for i in range(4)])
    planes = p.xe + nx

    def first_body(own, y, z, yz, *refs):
        weight_refs, outs, tile, scratch = refs[:6], refs[6:11], refs[11], refs[12:]
        second = lax.axis_index("gy") == 1
        shift = jnp.where(second, nz - half + p.zh, p.zh)
        lane = iota((p.xe, p.yw, lanes), 2)
        for ref, other in ((own, y), (z, yz)):
            mine, theirs = ref[...], other[...]
            lower = jnp.where(second, theirs, mine)
            upper = jnp.where(second, mine, theirs)
            cells_here = jnp.concatenate([lower, upper], axis=1)
            moved = pltpu.roll(cells_here, shift, 2)
            if ref is own:
                tile[...] = moved
            else:
                begin = jnp.where(second, half + p.zh, 0)
                end = jnp.where(second, lanes, p.zh)
                tile[: p.xe] = jnp.where((lane >= begin) & (lane < end), moved, tile[: p.xe])
        cur = tile[: p.xe]
        ext = pltpu.roll(tile[p.xe :], lanes - p.zh, 2)
        _, weighted, sums = update_kernel(p, cur, ext, weight_refs, scratch)
        o_own, o_low, o_high, o_ext, o_sums = outs
        o_own[...] = weighted
        o_low[:REACH] = weighted[:REACH]
        o_low[REACH] = sums
        o_high[:REACH] = weighted[nx - REACH :]
        o_high[REACH] = sums
        o_ext[...] = ext
        o_sums[...] = sums

    message = f32(REACH + 1, p.yw, lanes)
    own, low, high, ext, sums = kernel_call(
        p,
        "update_one",
        first_body,
        (f32(nx, p.yw, lanes), message, message, f32(nx, p.yw, lanes), f32(8, 128)),
        0,
        10,
        [pltpu.VMEM((planes, p.yw, lanes), F32)] + update_scratch(p),
        update_cost(p),
    )(wide, from_y, from_z, from_yz, *weights)

    left = along_x(high, 1)
    right = along_x(low, -1)
    far = along_x(sums, 2)

    packs = up(p.xe, 8) // 8

    def join_body(own_ref, sums_ref, left_ref, right_ref, far_ref, o_tile, o_down, o_up, o_sums):
        tile = jnp.concatenate([left_ref[:REACH], own_ref[...], right_ref[:REACH]], axis=0)
        sums = sums_ref[...] + left_ref[REACH] + right_ref[REACH] + far_ref[...]
        o_tile[...] = tile
        o_sums[...] = sums
        lane = lax.div(iota((p.yw, lanes), 1), p.zh)
        for ref, start in ((o_down, 0), (o_up, half - p.zh)):
            for pack in range(packs):
                joined = jnp.zeros((p.yw, lanes), F32)
                for k in range(min(8, p.xe - 8 * pack)):
                    moved = pltpu.roll(tile[8 * pack + k], (k * p.zh - start) % lanes, 1)
                    joined = jnp.where(lane == k, moved, joined)
                ref[pack] = joined
            ref[packs] = sums

    edge = f32(packs + 1, p.yw, lanes)
    tile, down, upper, sums = kernel_call(
        p,
        "join",
        join_body,
        (f32(p.xe, p.yw, lanes), edge, edge, f32(8, 128)),
        0,
        5,
    )(own, sums, left, right, far)
    below = along_z(upper, 1)
    above = along_z(down, -1)
    across = lax.ppermute(sums, "gz", [(0, 1), (1, 0)])

    def second_body(tile_ref, below_ref, above_ref, sums_ref, across_ref, ext_ref, *refs):
        weight_refs, outs, cur, scratch = refs[:6], refs[6:10], refs[10], refs[11:]
        o_keep, o_send, o_sums, o_totals = outs
        totals = sums_ref[...] + across_ref[...] + below_ref[packs] + above_ref[packs]
        o_totals[...] = totals
        scale = pick(totals, 1) / pick(totals, 0)
        lane = iota((p.yw, lanes), 1)
        for x in range(p.xe):
            pack, k = divmod(x, 8)
            lower = pltpu.roll(below_ref[pack], -k * p.zh % lanes, 1)
            top = pltpu.roll(above_ref[pack], (p.zh + half - k * p.zh) % lanes, 1)
            middle = pltpu.roll(tile_ref[x], p.zh, 1)
            joined = jnp.where(lane < p.zh, lower, jnp.where(lane < p.zh + half, middle, top))
            cur[x] = joined * scale
        pot, weighted, sums_here = update_kernel(p, cur[...], ext_ref[...], weight_refs, scratch)
        o_sums[...] = jnp.broadcast_to(sums_here[:4], (16, 4, 128))
        both = jnp.where(
            iota(pot.shape, 2) < half, pot, pltpu.roll(weighted, half, 2)
        )
        second = lax.axis_index("gy") == 1
        lower, top = both[:, :ny], both[:, ny:]
        o_keep[...] = jnp.where(second, top, lower)
        o_send[...] = jnp.where(second, lower, top)

    share = f32(nx, ny, lanes)
    keep, send, sums, totals = kernel_call(
        p,
        "update_two",
        second_body,
        (share, share, f32(16, 4, 128), f32(8, 128)),
        0,
        12,
        [pltpu.VMEM((p.xe, p.yw, lanes), F32)] + update_scratch(p),
        update_cost(p),
    )(tile, below, above, sums, across, ext, *weights)

    other = lax.ppermute(send, "gy", [(0, 1), (1, 0)])
    gathered = lax.all_to_all(sums, axes, 0, 0, tiled=True)

    def last_body(keep_ref, other_ref, all_ref, totals_ref, o_new, o_pot, o_chem, o_stress):
        first = totals_ref[...]
        last = jnp.sum(all_ref[...], axis=0)
        last = jnp.concatenate([last, last], axis=0)
        mass = pick(first, 1)
        scale = mass / pick(last, 0)
        second = lax.axis_index("gy") == 1
        mine, theirs = keep_ref[...], other_ref[...]
        lower = jnp.where(second, theirs, mine)
        top = jnp.where(second, mine, theirs)
        lane = iota((nx, ny, nz), 2)
        o_pot[...] = jnp.where(lane < half, lower, pltpu.roll(top, half, 2))
        o_new[...] = jnp.where(lane < half, pltpu.roll(lower, half, 2), top) * scale[:ny]
        lane = iota((8, 128), 1)
        for step, total in enumerate((first, last)):
            chem = jnp.log(mass / pick(total, 0)) * (1.0 / TAU)
            o_chem[step] = chem[0, 0]
            for a in range(3):
                moments = pltpu.roll(total, 128 - 3 - 3 * a, 1)
                row = moments + jnp.where(lane == a, pick(total, 2), 0.0)
                o_stress[a, step : step + 1] = row[:1, :3] * (1.0 / cells)

    new, potential, chem, stress = kernel_call(
        p,
        "finish",
        last_body,
        (f32(nx, ny, nz), f32(nx, ny, nz), f32(STEPS), f32(3, STEPS, 3)),
        0,
        4,
    )(keep, other, gathered, totals)
    return new, potential, chem, jnp.transpose(stress, (1, 0, 2))


def on_device(density, external, w_first, w_second, w_third, w_last):
    mesh = tuple(lax.axis_size(axis) for axis in ("gx", "gy", "gz"))
    if mesh == (4, 2, 2) and density.shape == (8, 4, 128):
        return split_pairs(density, external, w_first, w_second, w_third, w_last)
    return any_mesh(density, external, w_first, w_second, w_third, w_last)


def solution(mesh):
    cells = P(("boxes", "gx"), "gy", "gz")
    return jax.shard_map(
        on_device,
        mesh=mesh,
        in_specs=(cells, cells, P(), P(), P(), P()),
        out_specs=(cells, cells, P("boxes"), P("boxes", None, None)),
        check_vma=False,
    )
```

```python
import functools

import jax
import jax.numpy as jnp
from jax import lax
from jax.experimental import pallas as pl
from jax.experimental.pallas import tpu as pltpu
from jax.sharding import PartitionSpec as P

STEPS = 2
C_TF = 2.871234
C_X = 0.7385588
TAU = 0.1
REACH = 6
STRIPS = 16
GROUP = 4
PAIRS = 8
SUMS = 16
BF = jnp.bfloat16
F32 = jnp.float32
VM = pl.BlockSpec(memory_space=pltpu.VMEM)
SM = pl.BlockSpec(memory_space=pltpu.SMEM)
HB = pl.BlockSpec(memory_space=pltpu.HBM)


def up(number, unit):
    return -(-number // unit) * unit


def iota(shape, dim):
    return lax.broadcasted_iota(jnp.int32, shape, dim)


def dot(a, b):
    return jnp.dot(a, b, preferred_element_type=F32)


def dot_tn(a, b):
    return lax.dot_general(a, b, (((0,), (0,)), ((), ())), preferred_element_type=F32)


def dot_nt(a, b):
    return lax.dot_general(a, b, (((1,), (1,)), ((), ())), preferred_element_type=F32)


class Plan:
    def __init__(self, xo, yw, own_y, ny, zo, ch, limit):
        self.xo, self.yw, self.own_y, self.ny, self.zo, self.ch = xo, yw, own_y, ny, zo, ch
        self.limit = limit << 20
        self.xe = xo + 2 * REACH
        self.ze = up(zo + 2 * REACH, STRIPS)
        self.zh = (self.ze - zo) // 2
        self.lo = self.ze // STRIPS
        self.zp = up(self.ze, 128)
        self.zq = up(zo, 128)
        self.lanes = yw * ch
        self.fields = 4 * yw
        self.narrow = up(GROUP * self.fields, 128)


PAIR_BLOCKS = (
    (0, 0, 0, 0),
    (0, 0, 1, 1),
    (1, 0, 1, 0),
    (1, 1, 0, 1),
    (2, 1, 0, 0),
    (2, 1, 1, 1),
)


def weights_kernel(p, dense_in, single_in, dense_out, first_out, last_out, arrivals):
    ch, yw, lanes = p.ch, p.yw, p.lanes
    half, wide = yw // 2, lanes // 2

    tile = (
        jnp.bitwise_and(iota((ch, lanes), 1), ch - 1) == iota((ch, lanes), 0)
    ).astype(F32).astype(BF)
    tiled = [dot(ref[...], tile).astype(BF) for ref in single_in]

    rows = 18 * yw
    row = iota((rows, 1), 0)
    yi = lax.rem(row, yw)
    tx = lax.rem(lax.div(row, yw), 3)
    tz = lax.rem(lax.div(row, 3 * yw), 3)
    yo = lax.div(iota((rows, lanes), 1), ch)
    for single, ref_out, direction in zip(tiled, first_out, (1, -1)):
        total = jnp.zeros((rows, lanes), F32)
        for ty in range(3):
            number = 9 * tx + 3 * ty + tz
            number = number if direction > 0 else 26 - number
            pick = (iota((rows, 27), 1) == number).astype(F32).astype(BF)
            here = lax.rem(yo + (ty - 1 + yw), yw) == yi
            total = total + jnp.where(here, dot(pick, single), 0.0)
        ref_out[...] = (0.5 * total).astype(BF)

    rows = p.narrow
    row = iota((rows, 1), 0)
    yo = lax.rem(row, yw)
    field = lax.rem(lax.div(row, yw), 4)
    tx = lax.div(row, 4 * yw)
    yi = lax.div(iota((rows, lanes), 1), ch)
    for single, ref_out, direction in zip(tiled[::-1], last_out, (1, -1)):
        for tz in range(3):
            total = jnp.zeros((rows, lanes), F32)
            for ty in range(3):
                number = 9 * tx + 3 * ty + tz
                number = number if direction > 0 else 26 - number
                if direction > 0:
                    factor = jnp.where(field == 0, 1, 0)
                else:
                    factor = jnp.where(
                        field == 0,
                        1,
                        jnp.where(field == 1, 1 - tx, jnp.where(field == 2, 1 - ty, 1 - tz)),
                    )
                factor = jnp.where(tx < 3, factor, 0).astype(F32)
                pick = jnp.where(iota((rows, 27), 1) == number, factor, 0.0).astype(BF)
                here = lax.rem(yo + (ty - 1 + yw), yw) == yi
                total = total + jnp.where(here, dot(pick, single), 0.0)
            ref_out[tz] = total.astype(BF)

    for ref_in, ref_out, arrive in zip(dense_in, dense_out, arrivals):
        arrive()
        taps = []
        for ty in range(3):
            taps.append(
                jnp.concatenate(
                    [ref_in[26 - (9 * (t // 3) + 3 * ty + t % 3)] for t in range(9)], axis=0
                )
            )
        taps = jnp.concatenate(taps, axis=1)
        row, column = iota((3 * ch, lanes), 0), iota((3 * ch, lanes), 1)
        ty = lax.div(row, ch)
        minus = column >= wide
        for yi in range(half):
            raw = yi + 1 - ty
            wraps = (raw < 0) | (raw >= half)
            yo = lax.rem(raw + half, half)
            target = row + (yo - ty) * ch
            match = jnp.where(minus, column - wide, column) == target
            value = jnp.where(wraps & minus, -0.25, 0.25)
            place = jnp.where(match, value, 0.0).astype(BF)
            spread = dot(taps, place).astype(BF).reshape(3, 3, ch, lanes)
            for sign in range(2):
                for tx, step, x_in, x_out in PAIR_BLOCKS:
                    begin = x_in * wide + yi * ch
                    ref_out[
                        sign, step, :, begin : begin + ch, x_out * wide : (x_out + 1) * wide
                    ] = spread[tx, :, :, sign * wide : (sign + 1) * wide]
        none = jnp.zeros((2, 3, wide, wide), BF)
        ref_out[:, 0, :, :wide, wide:] = none
        ref_out[:, 1, :, wide:, :wide] = none


def spread_weights(p, w_first, w_second, w_third, w_last):
    inputs = (w_second, w_third, w_first, w_last)

    def body(*refs):
        hbm, outs, held, sems = refs[:4], refs[4:10], refs[10:14], refs[14]
        copies = [pltpu.make_async_copy(hbm[i], held[i], sems.at[i]) for i in range(4)]
        for copy in copies[::-1]:
            copy.start()
        for copy in copies[2:]:
            copy.wait()
        arrivals = [copy.wait for copy in copies[:2]]
        weights_kernel(p, held[:2], held[2:], outs[:2], outs[2:4], outs[4:], arrivals)

    dense = jax.ShapeDtypeStruct((2, 2, 3, p.lanes, p.lanes), BF)
    single = jax.ShapeDtypeStruct((18 * p.yw, p.lanes), BF)
    narrow = jax.ShapeDtypeStruct((3, p.narrow, p.lanes), BF)
    flops = 2 * 2 * 9 * 3 * p.ch * p.lanes * p.lanes
    return pl.pallas_call(
        body,
        name="spread_weights",
        out_shape=(dense,) * 2 + (single,) * 2 + (narrow,) * 2,
        in_specs=[HB] * 4,
        out_specs=(VM,) * 6,
        scratch_shapes=[pltpu.VMEM(a.shape, a.dtype) for a in inputs]
        + [pltpu.SemaphoreType.DMA((4,))],
        compiler_params=pltpu.CompilerParams(vmem_limit_bytes=p.limit),
        cost_estimate=pl.CostEstimate(flops=flops, bytes_accessed=3 << 20, transcendentals=0),
    )(*[pltpu.with_memory_space_constraint(a, pltpu.HBM) for a in inputs])


def cube_root(value):
    guess = jnp.exp(jnp.log(value) * (1.0 / 3.0))
    return guess - (guess - value / (guess * guess)) * (1.0 / 3.0)


def store_edges(p, ref, place, value):
    tiles = value.reshape(p.lo, STRIPS, p.lanes)
    ref[place, 1 : p.lo + 1] = tiles.astype(BF)
    ref[place, 0] = pltpu.roll(tiles[p.lo - 1], 1, 0).astype(BF)
    ref[place, p.lo + 1] = pltpu.roll(tiles[0], STRIPS - 1, 0).astype(BF)


def blocks(total, size):
    return [(start, min(size, total - start)) for start in range(0, total, size)]


def store_pairs(p, ref, place, value):
    wide = p.lanes // 2
    first, second = value[:, :wide], value[:, wide:]
    pair, side = divmod(place, 2)
    lanes = slice(side * wide, (side + 1) * wide)
    for sign, part in enumerate((first + second, first - second)):
        tiles = part.reshape(p.lo, STRIPS, wide)
        ref[sign, pair, 1 : p.lo + 1, :, lanes] = tiles.astype(BF)
        ref[sign, pair, 0, :, lanes] = pltpu.roll(tiles[p.lo - 1], 1, 0).astype(BF)
        ref[sign, pair, p.lo + 1, :, lanes] = pltpu.roll(tiles[0], STRIPS - 1, 0).astype(BF)


def dense_planes(p, ref, w_ref, start, count, forward):
    halves = []
    for sign in range(2):
        total = None
        for step in range(2):
            for tz in range(3):
                rows = ref[sign, start + step : start + step + count, tz : tz + p.lo]
                rows = rows.reshape(count * p.ze, p.lanes)
                if forward:
                    part = dot_nt(rows, w_ref[sign, 1 - step, 2 - tz])
                else:
                    part = dot(rows, w_ref[sign, step, tz])
                total = part if total is None else total + part
        halves.append(total)
    wide = p.lanes // 2
    planes = []
    for k in range(2 * count):
        rows = slice(k // 2 * p.ze, (k // 2 + 1) * p.ze)
        lanes = slice(k % 2 * wide, (k % 2 + 1) * wide)
        plus, minus = halves[0][rows, lanes], halves[1][rows, lanes]
        planes.append(jnp.concatenate([plus + minus, plus - minus], axis=1))
    return planes


def gate(value, slope=True):
    wave = jnp.tanh(value)
    product = value * wave
    act = value + product
    if not slope:
        return act, None
    rise = 1.0 + wave
    return act, rise + rise * (value - product)


def to_planes(p, field, spread, planes_ref):
    high = field.astype(BF)
    low = (field - high.astype(F32)).astype(BF)
    flat = jnp.concatenate(
        [high.reshape(p.xe * p.yw, p.zp), low.reshape(p.xe * p.yw, p.zp)], axis=0
    )
    planes_ref[...] = dot(flat, spread).reshape(2, p.xe, p.yw, 3 * p.zp)


def single_plane(p, planes_ref, place, w_ref):
    pieces = []
    for half in range(2):
        for tz in range(3):
            piece = planes_ref[half, place : place + 3, :, tz * p.zp : tz * p.zp + p.ze]
            pieces.append(piece.reshape(3 * p.yw, p.ze))
    window = jnp.concatenate(pieces, axis=0).astype(BF)
    return dot_tn(window, w_ref[...])


def narrow_fold(p, ref, w_ref, planes_ref, back):
    for start, count in blocks(p.xo + 2, 5):
        total = None
        for tz in range(3):
            rows = ref[start : start + count, tz : tz + p.lo].reshape(count * p.ze, p.lanes)
            part = dot_nt(rows, w_ref[tz])
            total = part if total is None else total + part
        planes_ref[start : start + count] = total.reshape(count, p.ze, p.narrow)
    lane = lax.div(iota((p.ze, p.narrow), 1), p.fields)
    fields = []
    for first in range(0, p.xo, GROUP):
        joined = jnp.zeros((p.ze, p.narrow), F32)
        for k in range(GROUP):
            total = None
            for tx in range(3):
                part = planes_ref[first + k + tx]
                shift = (k - tx) * p.fields % p.narrow
                part = pltpu.roll(part, shift, 1) if shift else part
                total = part if total is None else total + part
            joined = jnp.where(lane == k, total, joined)
        high = joined.astype(BF)
        rest = joined - high.astype(F32)
        mid = rest.astype(BF)
        low = (rest - mid.astype(F32)).astype(BF)
        parts = jnp.concatenate([high, mid, low], axis=0)
        natural = dot_tn(parts, back)[: GROUP * p.fields]
        fields.append(natural.reshape(GROUP, 4, p.yw, p.zq))
    return jnp.concatenate(fields, axis=0)


def update_kernel(p, current, external, weights, scratch):
    w_two, w_three, w_one, w_source, w_enhance, w_lever = weights
    planes, act_a, act_b, act_c, slope_one, slope_two, narrow = scratch

    current = jnp.where(iota(current.shape, 2) < p.ze, current, 1.0)
    cube = cube_root(current)
    source = current * cube * cube

    shape = (p.zp, 3 * p.zp)
    lane = iota(shape, 1)
    tz = lax.div(lane, p.zp)
    row = lane - tz * p.zp
    cell = p.lo * jnp.bitwise_and(row, STRIPS - 1) + lax.div(row, STRIPS) + tz - 1
    spread = jnp.where((cell == iota(shape, 0)) & (row < p.ze), 1.0, 0.0).astype(BF)
    shape = (3 * p.ze, p.zq)
    row = lax.rem(iota(shape, 0), p.ze)
    cell = p.lo * jnp.bitwise_and(row, STRIPS - 1) + lax.div(row, STRIPS) - p.zh
    back = jnp.where((cell == iota(shape, 1)) & (cell < p.zo), 1.0, 0.0).astype(BF)

    to_planes(p, cube, spread, planes)
    for x in range(p.xo + 10):
        value = single_plane(p, planes, x, w_one)
        inside = 4 <= x < p.xo + 6
        act, slope = gate(value, inside)
        store_pairs(p, act_a, x, act)
        if inside:
            slope_one[x - 4] = slope

    for start, count in blocks((p.xo + 8) // 2, PAIRS):
        for k, value in enumerate(dense_planes(p, act_a, w_two, start, count, True)):
            x = 2 * start + k
            inside = 2 <= x < p.xo + 6
            act, slope = gate(value, inside)
            store_pairs(p, act_b, x, act)
            if inside:
                slope_two[x - 2] = slope

    to_planes(p, source, spread, planes)
    for start, count in blocks((p.xo + 6) // 2, PAIRS):
        for k, value in enumerate(dense_planes(p, act_b, w_three, start, count, True)):
            x = 2 * start + k
            act, slope = gate(value)
            if 2 <= x < p.xo + 4:
                store_edges(p, act_c, x - 2, act)
            store_pairs(p, act_a, x, single_plane(p, planes, x + 2, w_source) * slope)

    enhance = narrow_fold(p, act_c, w_enhance, narrow, back)[:, 0]

    for start, count in blocks((p.xo + 4) // 2, PAIRS):
        for k, value in enumerate(dense_planes(p, act_a, w_three, start, count, False)):
            store_pairs(p, act_b, 2 * start + k, value * slope_two[2 * start + k])

    for start, count in blocks((p.xo + 2) // 2, PAIRS):
        for k, value in enumerate(dense_planes(p, act_b, w_two, start, count, False)):
            store_edges(p, act_c, 2 * start + k, value * slope_one[2 * start + k])

    levers = narrow_fold(p, act_c, w_lever, narrow, back)

    def natural(field, step):
        return pltpu.roll(field, (p.zp - p.zh - step) % p.zp, 2)[:, :, : p.zq]

    inner = cube[REACH : REACH + p.xo]
    here = natural(inner, 0)
    density = natural(current[REACH : REACH + p.xo], 0)
    source_here = natural(source[REACH : REACH + p.xo], 0)
    squared = here * here
    potential = (
        5.0 / 3.0 * squared * (C_TF + enhance)
        + levers[:, 0] / (3.0 * squared)
        + external
        - 4.0 / 3.0 * C_X * here
    )
    slopes = [
        natural(cube[REACH + 1 : REACH + 1 + p.xo], 0) - natural(cube[REACH - 1 : REACH - 1 + p.xo], 0),
        pltpu.roll(here, p.yw - 1, 1) - pltpu.roll(here, 1, 1),
        natural(inner, 1) - natural(inner, -1),
    ]
    weighted = density * jnp.exp(-TAU * potential)
    energy = source_here * (C_TF + enhance) + external * density - C_X * density * here
    terms = [weighted, density, energy - density * potential]
    for slope in slopes:
        for axis in range(3):
            terms.append(0.5 * slope * levers[:, 1 + axis])
    lane = iota((p.yw, p.zq), 1)
    y = iota((p.yw, p.zq), 0)
    own = (lane < p.zo) & (y >= p.own_y) & (y < p.own_y + p.ny)
    rows = []
    for term in terms:
        rows.append(jnp.sum(jnp.where(own, jnp.sum(term, axis=0), 0.0), axis=0, keepdims=True))
    rows.append(jnp.zeros((SUMS - len(rows), p.zq), F32))
    sums = jnp.sum(jnp.concatenate(rows, axis=0), axis=1, keepdims=True)
    onto = iota((SUMS, 128), 0) == iota((SUMS, 128), 1)
    row = jnp.sum(jnp.where(onto, sums, 0.0), axis=0, keepdims=True)
    return potential, weighted, jnp.broadcast_to(row, (8, 128))


def pick(row, number):
    return jnp.sum(jnp.where(iota(row.shape, 1) == number, row, 0.0), axis=1, keepdims=True)


def update_scratch(p):
    def pairs(planes):
        return pltpu.VMEM((2, planes // 2, p.lo + 2, STRIPS, p.lanes), BF)

    return [
        pltpu.VMEM((2, p.xe, p.yw, 3 * p.zp), F32),
        pairs(p.xo + 10),
        pairs(p.xo + 8),
        pltpu.VMEM((p.xo + 2, p.lo + 2, STRIPS, p.lanes), BF),
        pltpu.VMEM((p.xo + 2, p.ze, p.lanes), F32),
        pltpu.VMEM((p.xo + 4, p.ze, p.lanes), F32),
        pltpu.VMEM((p.xo + 2, p.ze, p.narrow), F32),
    ]


def update_cost(p):
    flops = 2 * 6 * p.lanes * p.lanes * p.ze * (4 * p.xo + 20)
    return pl.CostEstimate(flops=flops, bytes_accessed=6 << 20, transcendentals=0)


def kernel_call(p, name, body, out_shape, n_smem, n_vmem, scratch=(), cost=None, n_hbm=0):
    return pl.pallas_call(
        body,
        name=name,
        out_shape=out_shape,
        in_specs=[SM] * n_smem + [HB] * n_hbm + [VM] * n_vmem,
        out_specs=tuple(SM if len(shape.shape) == 1 else VM for shape in out_shape),
        scratch_shapes=list(scratch),
        compiler_params=pltpu.CompilerParams(vmem_limit_bytes=p.limit),
        cost_estimate=cost,
    )


def f32(*shape):
    return jax.ShapeDtypeStruct(shape, F32)


def widen(cells, axis, dim, before, after):
    size = cells.shape[dim]
    count = lax.axis_size(axis)

    def fetch(step, start, stop):
        piece = lax.slice_in_dim(cells, start, stop, axis=dim)
        if step % count == 0:
            return piece
        return lax.ppermute(piece, axis, [(i, (i + step) % count) for i in range(count)])

    pieces = [cells]
    left = before
    step = 1
    while left > 0:
        take = min(left, size)
        pieces.insert(0, fetch(step, size - take, size))
        left -= take
        step += 1
    left = after
    step = 1
    while left > 0:
        take = min(left, size)
        pieces.append(fetch(-step, 0, take))
        left -= take
        step += 1
    return jnp.concatenate(pieces, axis=dim)


def any_mesh(density, external, w_first, w_second, w_third, w_last):
    nx, ny, nz = density.shape
    ch = w_first.shape[1]
    yw = up(ny + 2 * REACH, 8)
    own_y = (yw - ny) // 2
    xo = up(nx, GROUP)
    p = Plan(xo, yw, own_y, ny, nz, ch, 60)
    weights = spread_weights(p, w_first, w_second, w_third, w_last)
    axes = ("gx", "gy", "gz")
    count = nx * ny * nz * lax.axis_size("gx") * lax.axis_size("gy") * lax.axis_size("gz")
    total_mass = lax.psum(jnp.sum(density), axes)

    def body(cur, ext, *refs):
        weight_refs, (o_pot, o_weighted, o_sums), scratch = refs[:6], refs[6:9], refs[9:]
        pot, weighted, sums = update_kernel(p, cur[...], ext[...], weight_refs, scratch)
        o_pot[...] = pot
        o_weighted[...] = weighted
        o_sums[...] = sums

    call = kernel_call(
        p,
        "update",
        body,
        (f32(xo, yw, p.zq), f32(xo, yw, p.zq), f32(8, 128)),
        0,
        8,
        update_scratch(p),
        update_cost(p),
    )
    ext = jnp.pad(
        external, ((0, xo - nx), (own_y, yw - ny - own_y), (0, p.zq - nz))
    )
    current = density
    chem, stress = [], []
    for _ in range(STEPS):
        tile = widen(current, "gz", 2, p.zh, p.ze - nz - p.zh)
        tile = widen(tile, "gy", 1, own_y, yw - ny - own_y)
        tile = widen(tile, "gx", 0, REACH, REACH)
        tile = jnp.pad(tile, ((0, 0), (0, 0), (0, p.zp - p.ze)), constant_values=1.0)
        pot, weighted, sums = call(tile, ext, *weights)
        totals = lax.psum(sums[0, :SUMS], axes)
        chem.append(jnp.log(total_mass / totals[0]) / TAU)
        moments = totals[3:12].reshape(3, 3)
        stress.append((moments + jnp.eye(3, dtype=F32) * totals[2]) / count)
        current = weighted[:nx, own_y : own_y + ny, :nz] * (total_mass / totals[0])
        potential = pot[:nx, own_y : own_y + ny, :nz]
    return current, potential, jnp.stack(chem), jnp.stack(stress)


def split_pairs(density, external, w_first, w_second, w_third, w_last):
    nx, ny, nz = density.shape
    ch = w_first.shape[1]
    half = nz // 2
    p = Plan(nx, 2 * ny, 0, 2 * ny, half, ch, 20)
    lanes = p.zp
    cells = nx * ny * nz * 16
    axes = ("gx", "gy", "gz")

    def along_x(cells_out, step):
        return lax.ppermute(cells_out, "gx", [(i, (i + step) % 4) for i in range(4)])

    def quarter(number):
        return (number % 2) * 2 + number // 2

    def along_z(cells_out, step):
        pairs = [(quarter(q), quarter((q + step) % 4)) for q in range(4)]
        return lax.ppermute(cells_out, ("gy", "gz"), pairs)

    weights = spread_weights(p, w_first, w_second, w_third, w_last)

    def widen_body(own_hbm, ext_hbm, left_ref, right_ref, o_wide, o_cells, sems):
        copies = [
            pltpu.make_async_copy(own_hbm, o_wide.at[REACH : REACH + nx], sems.at[0]),
            pltpu.make_async_copy(ext_hbm, o_wide.at[p.xe :], sems.at[1]),
        ]
        for copy in copies:
            copy.start()
        o_wide[:REACH] = left_ref[nx - REACH :]
        o_wide[REACH + nx : p.xe] = right_ref[:REACH]
        for copy in copies:
            copy.wait()
        o_cells[...] = o_wide[: p.xe]

    wide, cells_wide = kernel_call(
        p,
        "widen",
        widen_body,
        (f32(p.xe + nx, ny, nz), f32(p.xe, ny, nz)),
        0,
        2,
        [pltpu.SemaphoreType.DMA((2,))],
        n_hbm=2,
    )(
        *[pltpu.with_memory_space_constraint(a, pltpu.HBM) for a in (density, external)],
        along_x(density, 1),
        along_x(density, -1),
    )
    from_y = lax.ppermute(wide, "gy", [(0, 1), (1, 0)])
    from_z = lax.ppermute(cells_wide, "gz", [(0, 1), (1, 0)])
    from_yz = lax.ppermute(cells_wide, ("gy", "gz"), [(i, 3 - i) for i in range(4)])
    planes = p.xe + nx

    def first_body(own, y, z, yz, *refs):
        weight_refs, outs, tile, scratch = refs[:6], refs[6:11], refs[11], refs[12:]
        second = lax.axis_index("gy") == 1
        shift = jnp.where(second, nz - half + p.zh, p.zh)
        lane = iota((p.xe, p.yw, lanes), 2)
        for ref, other in ((own, y), (z, yz)):
            mine, theirs = ref[...], other[...]
            lower = jnp.where(second, theirs, mine)
            upper = jnp.where(second, mine, theirs)
            cells_here = jnp.concatenate([lower, upper], axis=1)
            moved = pltpu.roll(cells_here, shift, 2)
            if ref is own:
                tile[...] = moved
            else:
                begin = jnp.where(second, half + p.zh, 0)
                end = jnp.where(second, lanes, p.zh)
                tile[: p.xe] = jnp.where((lane >= begin) & (lane < end), moved, tile[: p.xe])
        cur = tile[: p.xe]
        ext = pltpu.roll(tile[p.xe :], lanes - p.zh, 2)
        _, weighted, sums = update_kernel(p, cur, ext, weight_refs, scratch)
        o_own, o_low, o_high, o_ext, o_sums = outs
        o_own[...] = weighted
        o_low[:REACH] = weighted[:REACH]
        o_low[REACH] = sums
        o_high[:REACH] = weighted[nx - REACH :]
        o_high[REACH] = sums
        o_ext[...] = ext
        o_sums[...] = sums

    message = f32(REACH + 1, p.yw, lanes)
    own, low, high, ext, sums = kernel_call(
        p,
        "update_one",
        first_body,
        (f32(nx, p.yw, lanes), message, message, f32(nx, p.yw, lanes), f32(8, 128)),
        0,
        10,
        [pltpu.VMEM((planes, p.yw, lanes), F32)] + update_scratch(p),
        update_cost(p),
    )(wide, from_y, from_z, from_yz, *weights)

    left = along_x(high, 1)
    right = along_x(low, -1)
    far = along_x(sums, 2)

    packs = up(p.xe, 8) // 8

    def join_body(own_ref, sums_ref, left_ref, right_ref, far_ref, o_tile, o_down, o_up, o_sums):
        tile = jnp.concatenate([left_ref[:REACH], own_ref[...], right_ref[:REACH]], axis=0)
        sums = sums_ref[...] + left_ref[REACH] + right_ref[REACH] + far_ref[...]
        o_tile[...] = tile
        o_sums[...] = sums
        lane = lax.div(iota((p.yw, lanes), 1), p.zh)
        for ref, start in ((o_down, 0), (o_up, half - p.zh)):
            for pack in range(packs):
                joined = jnp.zeros((p.yw, lanes), F32)
                for k in range(min(8, p.xe - 8 * pack)):
                    moved = pltpu.roll(tile[8 * pack + k], (k * p.zh - start) % lanes, 1)
                    joined = jnp.where(lane == k, moved, joined)
                ref[pack] = joined
            ref[packs] = sums

    edge = f32(packs + 1, p.yw, lanes)
    tile, down, upper, sums = kernel_call(
        p,
        "join",
        join_body,
        (f32(p.xe, p.yw, lanes), edge, edge, f32(8, 128)),
        0,
        5,
    )(own, sums, left, right, far)
    below = along_z(upper, 1)
    above = along_z(down, -1)
    across = lax.ppermute(sums, "gz", [(0, 1), (1, 0)])

    def second_body(tile_ref, below_ref, above_ref, sums_ref, across_ref, ext_ref, *refs):
        weight_refs, outs, cur, scratch = refs[:6], refs[6:10], refs[10], refs[11:]
        o_keep, o_send, o_sums, o_totals = outs
        totals = sums_ref[...] + across_ref[...] + below_ref[packs] + above_ref[packs]
        o_totals[...] = totals
        scale = pick(totals, 1) / pick(totals, 0)
        lane = iota((p.yw, lanes), 1)
        for x in range(p.xe):
            pack, k = divmod(x, 8)
            lower = pltpu.roll(below_ref[pack], -k * p.zh % lanes, 1)
            top = pltpu.roll(above_ref[pack], (p.zh + half - k * p.zh) % lanes, 1)
            middle = pltpu.roll(tile_ref[x], p.zh, 1)
            joined = jnp.where(lane < p.zh, lower, jnp.where(lane < p.zh + half, middle, top))
            cur[x] = joined * scale
        pot, weighted, sums_here = update_kernel(p, cur[...], ext_ref[...], weight_refs, scratch)
        o_sums[...] = jnp.broadcast_to(sums_here[:2], (16, 2, 128))
        both = jnp.where(
            iota(pot.shape, 2) < half, pot, pltpu.roll(weighted, half, 2)
        )
        second = lax.axis_index("gy") == 1
        lower, top = both[:, :ny], both[:, ny:]
        o_keep[...] = jnp.where(second, top, lower)
        o_send[...] = jnp.where(second, lower, top)

    share = f32(nx, ny, lanes)
    keep, send, sums, totals = kernel_call(
        p,
        "update_two",
        second_body,
        (share, share, f32(16, 2, 128), f32(8, 128)),
        0,
        12,
        [pltpu.VMEM((p.xe, p.yw, lanes), F32)] + update_scratch(p),
        update_cost(p),
    )(tile, below, above, sums, across, ext, *weights)

    other = lax.ppermute(send, "gy", [(0, 1), (1, 0)])
    gathered = lax.all_to_all(sums, axes, 0, 0, tiled=True)

    def last_body(keep_ref, other_ref, all_ref, totals_ref, o_new, o_pot, o_chem, o_stress):
        first = totals_ref[...]
        last = jnp.sum(all_ref[...], axis=0)
        last = jnp.concatenate([last] * 4, axis=0)
        mass = pick(first, 1)
        scale = mass / pick(last, 0)
        second = lax.axis_index("gy") == 1
        mine, theirs = keep_ref[...], other_ref[...]
        lower = jnp.where(second, theirs, mine)
        top = jnp.where(second, mine, theirs)
        lane = iota((nx, ny, nz), 2)
        o_pot[...] = jnp.where(lane < half, lower, pltpu.roll(top, half, 2))
        o_new[...] = jnp.where(lane < half, pltpu.roll(lower, half, 2), top) * scale[:ny]
        lane = iota((8, 128), 1)
        for step, total in enumerate((first, last)):
            chem = jnp.log(mass / pick(total, 0)) * (1.0 / TAU)
            o_chem[step] = chem[0, 0]
            for a in range(3):
                moments = pltpu.roll(total, 128 - 3 - 3 * a, 1)
                row = moments + jnp.where(lane == a, pick(total, 2), 0.0)
                o_stress[a, step : step + 1] = row[:1, :3] * (1.0 / cells)

    new, potential, chem, stress = kernel_call(
        p,
        "finish",
        last_body,
        (f32(nx, ny, nz), f32(nx, ny, nz), f32(STEPS), f32(3, STEPS, 3)),
        0,
        4,
    )(keep, other, gathered, totals)
    return new, potential, chem, jnp.transpose(stress, (1, 0, 2))


def on_device(density, external, w_first, w_second, w_third, w_last):
    mesh = tuple(lax.axis_size(axis) for axis in ("gx", "gy", "gz"))
    if mesh == (4, 2, 2) and density.shape == (8, 4, 128):
        return split_pairs(density, external, w_first, w_second, w_third, w_last)
    return any_mesh(density, external, w_first, w_second, w_third, w_last)


def solution(mesh):
    cells = P(("boxes", "gx"), "gy", "gz")
    return jax.shard_map(
        on_device,
        mesh=mesh,
        in_specs=(cells, cells, P(), P(), P(), P()),
        out_specs=(cells, cells, P("boxes"), P("boxes", None, None)),
        check_vma=False,
    )
```
